32 devices in a mesh: fsdp: 4 (over z), seq: 8 (over y, x, core).
Axes of the slice: x: 2, y: 2, z: 4, core: 2. Of those that a mesh axis runs over, the one named last changes fastest.
Arguments:
- queries: bfloat16 [4, 2048, 2048], P('fsdp', 'seq'), may hold values from -32 to 32
- keys: bfloat16 [4, 2048, 2048], P('fsdp', 'seq'), may hold values from -6 to 6
- values: bfloat16 [4, 2048, 2048], P('fsdp', 'seq'), may hold values from -6 to 6
- out_grad: bfloat16 [4, 2048, 2048], P('fsdp', 'seq'), may hold values from -6 to 6
- out_weight: bfloat16 [2048, 2048], P('fsdp'), may hold values from -0.125 to 0.125
- key_blocks: int32 [4, 16, 10], P('fsdp'), may hold values from 0 to 15, as said below
- block_counts: int32 [4, 16], P('fsdp'), may hold values from 2 to 10, as said below
Outputs:
- query_grad: bfloat16 [4, 2048, 2048], P('fsdp', 'seq')
- key_grad: bfloat16 [4, 2048, 2048], P('fsdp', 'seq')
- value_grad: bfloat16 [4, 2048, 2048], P('fsdp', 'seq')
- wo_grad: float32 [2048, 2048], P('fsdp')
The draws below stay inside these ranges and needn't reach their ends.
Inputs may be any that keep to these rules, and one draw needn't show every extreme that they name: `key_blocks`: within a row the numbers are distinct; slots 0, 1 and 2 hold blocks i, i + 1 and i - 1 modulo 16; slots at or past the row's count are ignored. `block_counts`: every sample has a query block whose count is 10.
All inputs are finite; a program needn't handle non-finite values.
Results may differ from the reference program's by a relative error of at most 0.025.
Values may be sent and summed in bfloat16 or wider, within the bound.
No kernel may reach another device: no remote copies, remote signals or barrier semaphores. Data moves between devices by JAX's collectives and lax.ppermute only.
A program may use at most 128 MiB of HBM per device.

```python
import jax
import jax.numpy as jnp
from jax import lax

HEADS = 32
HD = 64
D = 2048
BLK = 128
MAXK = 10
SEQLEN = 2048
NBLK = 16
BATCH = 4


def base_field(key):
    return jax.random.truncated_normal(jax.random.fold_in(key, 11), -6.0, 6.0, (BATCH, SEQLEN, D), jnp.float32)


def draw_queries(key, part):
    field = base_field(jax.random.fold_in(key, 1))
    return field.astype(jnp.bfloat16)


def draw_keys(key, part):
    field = base_field(jax.random.fold_in(key, 2))
    return field.astype(jnp.bfloat16)


def draw_key_blocks(key, part):
    row_keys = jax.random.split(jax.random.fold_in(key, 5), BATCH * NBLK)

    def one_row(row_key):
        others = jax.random.permutation(row_key, jnp.arange(2, NBLK - 1, dtype=jnp.int32))
        return jnp.concatenate([jnp.array([0, 1, NBLK - 1], jnp.int32), others[:MAXK - 3].astype(jnp.int32)])
    offsets = jax.vmap(one_row)(row_keys).reshape(BATCH, NBLK, MAXK)
    own = jnp.arange(NBLK, dtype=jnp.int32)[None, :, None]
    return ((own + offsets) % NBLK).astype(jnp.int32)


def draw_block_counts(key, part):
    counts = jax.random.randint(jax.random.fold_in(key, 3), (BATCH, NBLK), 2, MAXK + 1)
    fullest = jax.random.randint(jax.random.fold_in(key, 4), (BATCH, 1), 0, NBLK)
    return jnp.where(jnp.arange(NBLK)[None, :] == fullest, MAXK, counts).astype(jnp.int32)


def steps_of(rng, extent, cuts, least, top_value):
    gain, own = 1.0, jax.random.fold_in(rng, 6)
    for position, blocks in cuts:
        steps = jnp.exp(jax.random.uniform(jax.random.fold_in(own, position), (blocks,), jnp.float32, least / len(cuts), top_value / len(cuts)))
        gain = gain * jnp.repeat(steps, extent[position] // blocks).reshape([-1 if axis == position else 1 for axis in range(len(extent))])
    return gain


def gaussian(rng, extent, deviation, limit, cuts=(), held_as=jnp.bfloat16):
    values = jax.random.normal(rng, extent, jnp.float32) * deviation
    if len(cuts) > 0:
        values = steps_of(rng, extent, cuts, -0.22, 0.18) * values
    return jnp.clip(values, min=-limit, max=limit).astype(held_as)


def setup_inputs(seed: int = 0) -> dict:
    seeds = jax.random.split(jax.random.key(seed), 8)
    queries = draw_queries(jax.random.fold_in(seeds[7], 71), 0)
    keys = draw_keys(jax.random.fold_in(seeds[7], 71), 0)
    values = gaussian(seeds[2], (BATCH, SEQLEN, D), 1.0, 6.0, ((0, 4), (1, 8)))
    out_grad = gaussian(seeds[3], (BATCH, SEQLEN, D), 1.0, 6.0, ((0, 4), (1, 8)))
    out_weight = gaussian(seeds[4], (D, D), D ** -0.5, 0.125, ((0, 4),))
    key_blocks = draw_key_blocks(jax.random.fold_in(seeds[7], 71), 0)
    block_counts = draw_block_counts(jax.random.fold_in(seeds[7], 71), 0)
    return dict(queries=queries, keys=keys, values=values, out_grad=out_grad, out_weight=out_weight, key_blocks=key_blocks, block_counts=block_counts)


NEG_FILL = -1e30


def attend_head(query_h, key_h, value_h, grad_h, adjacency, counts):
    scale_factor = HD ** -0.5
    keys_taken = key_h[adjacency].astype(jnp.float32)
    values_taken = value_h[adjacency].astype(jnp.float32)
    slot_live = jnp.arange(MAXK)[None, :] < counts[:, None]
    usable = slot_live[:, None, :, None]
    query_full = query_h.astype(jnp.float32)
    grad_full = grad_h.astype(jnp.float32)
    score = jnp.einsum('iqd,ijkd->iqjk', query_full, keys_taken) * scale_factor
    score = jnp.where(usable, score, NEG_FILL)
    row_max = jnp.max(score, axis=(2, 3))
    expo = jnp.where(usable, jnp.exp(score - row_max[:, :, None, None]), 0.0)
    row_sum = jnp.sum(expo, axis=(2, 3))
    prob_full = expo / row_sum[:, :, None, None]
    prob_half = prob_full.astype(jnp.bfloat16)
    attn_out = jnp.einsum('iqjk,ijkd->iqd', prob_half.astype(jnp.float32), values_taken).astype(jnp.bfloat16)
    row_dot = jnp.sum(grad_full * attn_out.astype(jnp.float32), axis=-1)
    prob_grad = jnp.einsum('iqd,ijkd->iqjk', grad_full, values_taken)
    score_grad = (prob_full * (prob_grad - row_dot[:, :, None, None])).astype(jnp.bfloat16)
    score_wide = score_grad.astype(jnp.float32)
    query_grad = (jnp.einsum('iqjk,ijkd->iqd', score_wide, keys_taken) * scale_factor).astype(jnp.bfloat16)
    key_terms = jnp.einsum('iqjk,iqd->ijkd', score_wide, query_full) * scale_factor
    key_grad = jnp.zeros((NBLK, BLK, HD), jnp.float32).at[adjacency].add(key_terms).astype(jnp.bfloat16)
    value_terms = jnp.einsum('iqjk,iqd->ijkd', prob_half.astype(jnp.float32), grad_full)
    value_grad = jnp.zeros((NBLK, BLK, HD), jnp.float32).at[adjacency].add(value_terms).astype(jnp.bfloat16)
    return query_grad, key_grad, value_grad, attn_out


def split_heads(array):
    return array.reshape(NBLK, BLK, HEADS, HD).transpose(2, 0, 1, 3)


def merge_heads(array):
    return array.transpose(1, 2, 0, 3).reshape(SEQLEN, D)


def reference(queries, keys, values, out_grad, out_weight, key_blocks, block_counts):
    attn_grad = jnp.dot(out_grad.reshape(-1, D), out_weight.T, preferred_element_type=jnp.float32)
    attn_grad = attn_grad.astype(jnp.bfloat16).reshape(BATCH, SEQLEN, D)

    def one_sample(packed):
        query_s, key_s, value_s, grad_s, adjacency, counts = packed

        def one_head(heads_in):
            return attend_head(heads_in[0], heads_in[1], heads_in[2], heads_in[3], adjacency, counts)

        results = lax.map(one_head, (split_heads(query_s), split_heads(key_s), split_heads(value_s), split_heads(grad_s)))
        return tuple(merge_heads(result) for result in results)

    query_grad, key_grad, value_grad, attn_out = lax.map(one_sample, (queries, keys, values, attn_grad, key_blocks, block_counts))
    wo_grad = jnp.dot(attn_out.reshape(-1, D).T, out_grad.reshape(-1, D), preferred_element_type=jnp.float32)
    return query_grad, key_grad, value_grad, wo_grad
```

```python
import math

import jax
import jax.numpy as jnp
from jax import lax
from jax.experimental import pallas as pl
from jax.experimental.pallas import tpu as pltpu
from jax.sharding import PartitionSpec as P

HEADS = 32
HD = 64
BLK = 128
MAXK = 10


NEG_FILL = -1e30


def pair_scores(query_blocks, chosen):
    return jnp.einsum(
        "iqhd,ikhd->ihqk", query_blocks, chosen, preferred_element_type=jnp.float32
    ) * HD ** (-0.5)


def blocked(array):
    return array.reshape(-1, BLK, array.shape[1], HD)


def head_forward(query_h, key_h, value_h, adjacency, slot_live):
    query_blocks = blocked(query_h)
    key_heads = blocked(key_h)
    value_heads = blocked(value_h)
    blocks_total = query_blocks.shape[0]
    head_count = query_blocks.shape[2]

    def stat_step(carried, slot):
        row_max, row_sum = carried
        score = pair_scores(query_blocks, key_heads[adjacency[:, slot]])
        usable = slot_live[:, slot][:, None, None, None]
        score = jnp.where(usable, score, NEG_FILL)
        new_max = jnp.maximum(row_max, jnp.max(score, axis=-1))
        expo = jnp.where(usable, jnp.exp(score - new_max[..., None]), 0.0)
        row_sum = row_sum * jnp.exp(row_max - new_max) + jnp.sum(expo, axis=-1)
        return ((new_max, row_sum), None)

    start_max = jnp.full((blocks_total, head_count, BLK), NEG_FILL, jnp.float32)
    start_sum = jnp.zeros((blocks_total, head_count, BLK), jnp.float32)
    (row_max, row_sum), _ = lax.scan(stat_step, (start_max, start_sum), jnp.arange(MAXK))

    def output_step(accum, slot):
        picked = adjacency[:, slot]
        score = pair_scores(query_blocks, key_heads[picked])
        usable = slot_live[:, slot][:, None, None, None]
        prob_half = jnp.where(
            usable, jnp.exp(score - row_max[..., None]) / row_sum[..., None], 0.0
        ).astype(jnp.bfloat16)
        accum = accum + jnp.einsum(
            "ihqk,ikhd->iqhd", prob_half, value_heads[picked], preferred_element_type=jnp.float32
        )
        return (accum, None)

    start_out = jnp.zeros(query_blocks.shape, jnp.float32)
    accum, _ = lax.scan(output_step, start_out, jnp.arange(MAXK))
    return (row_max, row_sum, accum.astype(jnp.bfloat16))


def head_backward(
    query_h, key_h, value_h, grad_h, row_max, row_sum, attn_blocks, adjacency, slot_live
):
    query_blocks = blocked(query_h)
    key_heads = blocked(key_h)
    value_heads = blocked(value_h)
    grad_blocks = blocked(grad_h)
    scale_factor = HD ** (-0.5)
    row_dot = jnp.sum(
        grad_blocks.astype(jnp.float32) * attn_blocks.astype(jnp.float32), axis=-1
    ).transpose(0, 2, 1)

    def grad_step(carried, slot):
        query_accum, key_accum, value_accum = carried
        picked = adjacency[:, slot]
        chosen_keys = key_heads[picked]
        chosen_values = value_heads[picked]
        score = pair_scores(query_blocks, chosen_keys)
        usable = slot_live[:, slot][:, None, None, None]
        prob_full = jnp.where(usable, jnp.exp(score - row_max[..., None]) / row_sum[..., None], 0.0)
        prob_half = prob_full.astype(jnp.bfloat16)
        prob_grad = jnp.einsum(
            "iqhd,ikhd->ihqk", grad_blocks, chosen_values, preferred_element_type=jnp.float32
        )
        score_grad = (prob_full * (prob_grad - row_dot[..., None])).astype(jnp.bfloat16)
        query_accum = (
            query_accum
            + jnp.einsum(
                "ihqk,ikhd->iqhd", score_grad, chosen_keys, preferred_element_type=jnp.float32
            )
            * scale_factor
        )
        key_terms = (
            jnp.einsum(
                "ihqk,iqhd->ikhd", score_grad, query_blocks, preferred_element_type=jnp.float32
            )
            * scale_factor
        )
        value_terms = jnp.einsum(
            "ihqk,iqhd->ikhd", prob_half, grad_blocks, preferred_element_type=jnp.float32
        )
        key_accum = key_accum.at[picked].add(key_terms)
        value_accum = value_accum.at[picked].add(value_terms)
        return ((query_accum, key_accum, value_accum), None)

    zeros_start = jnp.zeros(query_blocks.shape, jnp.float32)
    (query_accum, key_accum, value_accum), _ = lax.scan(
        grad_step, (zeros_start, zeros_start, zeros_start), jnp.arange(MAXK)
    )
    head_count = query_h.shape[1]
    return tuple(
        (
            accum.astype(jnp.bfloat16).reshape(-1, head_count, HD)
            for accum in (query_accum, key_accum, value_accum)
        )
    )


PAIR = 2 * HD
SCALE = HD ** (-0.5)


def fold_rows(tile, combine):
    return combine(tile.reshape(-1, 8, tile.shape[1]), axis=0)


def by_head(block):
    first = lax.broadcasted_iota(jnp.int32, block.shape, 1) < HD
    zero = jnp.zeros_like(block)
    return jnp.concatenate([jnp.where(first, block, zero), jnp.where(first, zero, block)], axis=0)


def own_parts(wide):
    return jnp.concatenate([wide[:HD, :BLK], wide[HD:, BLK:]], axis=0)


def dot(left, right, dims=(((1,), (0,)), ((), ()))):
    return lax.dot_general(left, right, dims, preferred_element_type=jnp.float32)


TRANSPOSED = (((1,), (1,)), ((), ()))


def attend_kernel(
    adjacency, counts, query, key, value, grad, query_g, key_g, value_g, attn_out,
    key_t, value_t, key_sum, value_sum, prob, half, score_g,
):
    blocks = query.shape[0] // BLK

    def rows(index):
        return pl.ds(pl.multiple_of(index * BLK, BLK), BLK)

    @pl.loop(0, blocks)
    def _(index):
        key_t[index] = key[rows(index), :].T
        value_t[index] = value[rows(index), :].T
        key_sum[rows(index), :] = jnp.zeros((BLK, PAIR), jnp.float32)
        value_sum[rows(index), :] = jnp.zeros((BLK, PAIR), jnp.float32)

    def query_block(index, slots):
        live = counts[index]
        picked = [adjacency[index, slot] for slot in range(slots)]
        queries = by_head(query[rows(index), :])
        grad_block = grad[rows(index), :]
        grads = by_head(grad_block)

        row_max = jnp.full((8, 2 * BLK), NEG_FILL, jnp.float32)
        for slot in range(slots):
            score = dot(key[rows(picked[slot]), :], queries, TRANSPOSED)
            if slot == slots - 1:
                score = jnp.where(slot < live, score, NEG_FILL)
            prob[slot] = score
            row_max = jnp.maximum(row_max, fold_rows(score, jnp.max))
        row_max = jnp.max(row_max, axis=0, keepdims=True)

        row_sum = jnp.zeros((8, 2 * BLK), jnp.float32)
        for slot in range(slots):
            expo = jnp.exp2((prob[slot] - row_max) * (SCALE * math.log2(math.e)))
            prob[slot] = expo
            row_sum = row_sum + fold_rows(expo, jnp.sum)
        inverse = 1.0 / jnp.sum(row_sum, axis=0, keepdims=True)

        for slot in range(slots):
            full = prob[slot] * inverse
            prob[slot] = full
            half[rows(slot), :] = full.astype(jnp.bfloat16)

        out_t = jnp.zeros((PAIR, 2 * BLK), jnp.float32)
        for slot in range(0, slots, 2):
            out_t = out_t + dot(
                jnp.concatenate([value_t[picked[slot]], value_t[picked[slot + 1]]], axis=1),
                half[pl.ds(slot * BLK, 2 * BLK), :],
            )
        out_t = own_parts(out_t).astype(jnp.bfloat16).astype(jnp.float32)
        attn_out[rows(index), :] = out_t.T.astype(jnp.bfloat16)
        products = grad_block.astype(jnp.float32).T * out_t
        row_dot = jnp.concatenate(
            [
                jnp.sum(products[:HD], axis=0, keepdims=True),
                jnp.sum(products[HD:], axis=0, keepdims=True),
            ],
            axis=1,
        )

        for slot in range(slots):
            prob_grad = dot(value[rows(picked[slot]), :], grads, TRANSPOSED)
            term = (prob[slot] * (prob_grad - row_dot)).astype(jnp.bfloat16)
            score_g[rows(slot), :] = term
            key_sum[rows(picked[slot]), :] += dot(term, queries)
            value_sum[rows(picked[slot]), :] += dot(half[rows(slot), :], grads)

        query_t = jnp.zeros((PAIR, 2 * BLK), jnp.float32)
        for slot in range(0, slots, 2):
            query_t = query_t + dot(
                jnp.concatenate([key_t[picked[slot]], key_t[picked[slot + 1]]], axis=1),
                score_g[pl.ds(slot * BLK, 2 * BLK), :],
            )
        query_g[rows(index), :] = (own_parts(query_t).T * SCALE).astype(jnp.bfloat16)

    @pl.loop(0, blocks)
    def _(index):
        for slots in range(2, MAXK + 1, 2):
            @pl.when((counts[index] + 1) // 2 == slots // 2)
            def _():
                query_block(index, slots)

    key_g[...] = (key_sum[...] * SCALE).astype(jnp.bfloat16)
    value_g[...] = value_sum[...].astype(jnp.bfloat16)


def attend(query, key, value, grad, adjacency, counts):
    tokens, width = query.shape
    blocks = tokens // BLK
    pair = pl.BlockSpec((tokens, PAIR), lambda step: (0, step))
    scalars = pl.BlockSpec(memory_space=pltpu.SMEM)
    tiles = width // PAIR * blocks * MAXK
    return pl.pallas_call(
        attend_kernel,
        grid=(width // PAIR,),
        in_specs=[scalars, scalars] + [pair] * 4,
        out_specs=[pair] * 4,
        out_shape=[jax.ShapeDtypeStruct((tokens, width), jnp.bfloat16)] * 4,
        scratch_shapes=[
            pltpu.VMEM((blocks, PAIR, BLK), jnp.bfloat16),
            pltpu.VMEM((blocks, PAIR, BLK), jnp.bfloat16),
            pltpu.VMEM((tokens, PAIR), jnp.float32),
            pltpu.VMEM((tokens, PAIR), jnp.float32),
            pltpu.VMEM((MAXK, BLK, 2 * BLK), jnp.float32),
            pltpu.VMEM((MAXK * BLK, 2 * BLK), jnp.bfloat16),
            pltpu.VMEM((MAXK * BLK, 2 * BLK), jnp.bfloat16),
        ],
        compiler_params=pltpu.CompilerParams(vmem_limit_bytes=48 * 2**20),
        cost_estimate=pl.CostEstimate(
            flops=tiles * 2 * 6 * 2 * BLK * BLK * HD,
            bytes_accessed=8 * 2 * tokens * width,
            transcendentals=tiles * 2 * BLK * BLK,
        ),
        name="attend",
    )(adjacency, counts, query, key, value, grad)


def on_device(queries, keys, values, out_grad, out_weight, key_blocks, block_counts):
    local_tokens = queries.shape[1]
    model_width = queries.shape[2]
    seq_devices = lax.axis_size("seq")
    loss_grad = out_grad[0]
    adjacency = key_blocks[0]
    slot_live = jnp.arange(MAXK)[None, :] < block_counts[0][:, None]

    def head_groups(array):
        return array[0].reshape(local_tokens, seq_devices, HEADS // seq_devices, HD)

    attn_grad = lax.dot_general(
        loss_grad,
        lax.all_gather(out_weight, "fsdp", axis=0, tiled=True),
        (((1,), (1,)), ((), ())),
        preferred_element_type=jnp.float32,
    ).astype(jnp.bfloat16)

    def attend_heads(heads_in):
        if HEADS // seq_devices % 2 == 0:
            flat = (member.reshape(-1, HEADS // seq_devices * HD) for member in heads_in)
            results = attend(*flat, adjacency, block_counts[0])
            return tuple(result.reshape(-1, HEADS // seq_devices, HD) for result in results)
        query_h, key_h, value_h, grad_h = (member[:, 0] for member in heads_in)
        row_max, row_sum, attn_blocks = head_forward(query_h, key_h, value_h, adjacency, slot_live)
        query_g, key_g, value_g = head_backward(
            query_h, key_h, value_h, grad_h, row_max, row_sum, attn_blocks, adjacency, slot_live
        )
        return (query_g, key_g, value_g, attn_blocks.reshape(-1, query_h.shape[1], HD))

    query_g, key_g, value_g, attn_heads = attend_heads(
        (
            lax.all_to_all(head_groups(queries), "seq", split_axis=1, concat_axis=0, tiled=True),
            lax.all_to_all(head_groups(keys), "seq", split_axis=1, concat_axis=0, tiled=True),
            lax.all_to_all(head_groups(values), "seq", split_axis=1, concat_axis=0, tiled=True),
            lax.all_to_all(
                head_groups(attn_grad[None]), "seq", split_axis=1, concat_axis=0, tiled=True
            ),
        )
    )
    query_t, key_t, value_t, attn_t = (
        lax.all_to_all(query_g, "seq", split_axis=0, concat_axis=1, tiled=True),
        lax.all_to_all(key_g, "seq", split_axis=0, concat_axis=1, tiled=True),
        lax.all_to_all(value_g, "seq", split_axis=0, concat_axis=1, tiled=True),
        lax.all_to_all(attn_heads, "seq", split_axis=0, concat_axis=1, tiled=True),
    )
    attn_out = attn_t.reshape(local_tokens, model_width)
    share = lax.psum_scatter(
        lax.dot_general(
            attn_out, loss_grad, (((0,), (0,)), ((), ())), preferred_element_type=jnp.float32
        ),
        ("fsdp", "seq"),
        scatter_dimension=0,
        tiled=True,
    )
    wo_grad = lax.all_gather(share.astype(jnp.bfloat16), "seq", axis=0, tiled=True).astype(
        share.dtype
    )

    def to_tokens(array):
        return array.reshape(1, local_tokens, model_width)

    return (to_tokens(query_t), to_tokens(key_t), to_tokens(value_t), wo_grad)


def solution(mesh):
    return jax.shard_map(
        on_device,
        mesh=mesh,
        in_specs=(
            P("fsdp", "seq", None),
            P("fsdp", "seq", None),
            P("fsdp", "seq", None),
            P("fsdp", "seq", None),
            P("fsdp", None),
            P("fsdp", None, None),
            P("fsdp", None),
        ),
        out_specs=(
            P("fsdp", "seq", None),
            P("fsdp", "seq", None),
            P("fsdp", "seq", None),
            P("fsdp", None),
        ),
        check_vma=False,
    )
```

```python
import functools
import math

import jax
import jax.numpy as jnp
from jax import lax
from jax.experimental import pallas as pl
from jax.experimental.pallas import tpu as pltpu
from jax.sharding import PartitionSpec as P

HEADS = 32
HD = 64
BLK = 128
MAXK = 10


NEG_FILL = -1e30


def pair_scores(query_blocks, chosen):
    return jnp.einsum(
        "iqhd,ikhd->ihqk", query_blocks, chosen, preferred_element_type=jnp.float32
    ) * HD ** (-0.5)


def blocked(array):
    return array.reshape(-1, BLK, array.shape[1], HD)


def head_forward(query_h, key_h, value_h, adjacency, slot_live):
    query_blocks = blocked(query_h)
    key_heads = blocked(key_h)
    value_heads = blocked(value_h)
    blocks_total = query_blocks.shape[0]
    head_count = query_blocks.shape[2]

    def stat_step(carried, slot):
        row_max, row_sum = carried
        score = pair_scores(query_blocks, key_heads[adjacency[:, slot]])
        usable = slot_live[:, slot][:, None, None, None]
        score = jnp.where(usable, score, NEG_FILL)
        new_max = jnp.maximum(row_max, jnp.max(score, axis=-1))
        expo = jnp.where(usable, jnp.exp(score - new_max[..., None]), 0.0)
        row_sum = row_sum * jnp.exp(row_max - new_max) + jnp.sum(expo, axis=-1)
        return ((new_max, row_sum), None)

    start_max = jnp.full((blocks_total, head_count, BLK), NEG_FILL, jnp.float32)
    start_sum = jnp.zeros((blocks_total, head_count, BLK), jnp.float32)
    (row_max, row_sum), _ = lax.scan(stat_step, (start_max, start_sum), jnp.arange(MAXK))

    def output_step(accum, slot):
        picked = adjacency[:, slot]
        score = pair_scores(query_blocks, key_heads[picked])
        usable = slot_live[:, slot][:, None, None, None]
        prob_half = jnp.where(
            usable, jnp.exp(score - row_max[..., None]) / row_sum[..., None], 0.0
        ).astype(jnp.bfloat16)
        accum = accum + jnp.einsum(
            "ihqk,ikhd->iqhd", prob_half, value_heads[picked], preferred_element_type=jnp.float32
        )
        return (accum, None)

    start_out = jnp.zeros(query_blocks.shape, jnp.float32)
    accum, _ = lax.scan(output_step, start_out, jnp.arange(MAXK))
    return (row_max, row_sum, accum.astype(jnp.bfloat16))


def head_backward(
    query_h, key_h, value_h, grad_h, row_max, row_sum, attn_blocks, adjacency, slot_live
):
    query_blocks = blocked(query_h)
    key_heads = blocked(key_h)
    value_heads = blocked(value_h)
    grad_blocks = blocked(grad_h)
    scale_factor = HD ** (-0.5)
    row_dot = jnp.sum(
        grad_blocks.astype(jnp.float32) * attn_blocks.astype(jnp.float32), axis=-1
    ).transpose(0, 2, 1)

    def grad_step(carried, slot):
        query_accum, key_accum, value_accum = carried
        picked = adjacency[:, slot]
        chosen_keys = key_heads[picked]
        chosen_values = value_heads[picked]
        score = pair_scores(query_blocks, chosen_keys)
        usable = slot_live[:, slot][:, None, None, None]
        prob_full = jnp.where(usable, jnp.exp(score - row_max[..., None]) / row_sum[..., None], 0.0)
        prob_half = prob_full.astype(jnp.bfloat16)
        prob_grad = jnp.einsum(
            "iqhd,ikhd->ihqk", grad_blocks, chosen_values, preferred_element_type=jnp.float32
        )
        score_grad = (prob_full * (prob_grad - row_dot[..., None])).astype(jnp.bfloat16)
        query_accum = (
            query_accum
            + jnp.einsum(
                "ihqk,ikhd->iqhd", score_grad, chosen_keys, preferred_element_type=jnp.float32
            )
            * scale_factor
        )
        key_terms = (
            jnp.einsum(
                "ihqk,iqhd->ikhd", score_grad, query_blocks, preferred_element_type=jnp.float32
            )
            * scale_factor
        )
        value_terms = jnp.einsum(
            "ihqk,iqhd->ikhd", prob_half, grad_blocks, preferred_element_type=jnp.float32
        )
        key_accum = key_accum.at[picked].add(key_terms)
        value_accum = value_accum.at[picked].add(value_terms)
        return ((query_accum, key_accum, value_accum), None)

    zeros_start = jnp.zeros(query_blocks.shape, jnp.float32)
    (query_accum, key_accum, value_accum), _ = lax.scan(
        grad_step, (zeros_start, zeros_start, zeros_start), jnp.arange(MAXK)
    )
    head_count = query_h.shape[1]
    return tuple(
        (
            accum.astype(jnp.bfloat16).reshape(-1, head_count, HD)
            for accum in (query_accum, key_accum, value_accum)
        )
    )


PAIR = 2 * HD
PAIR = 2 * HD
SCALE = HD ** (-0.5)
BASE2 = SCALE * math.log2(math.e)


def fold_rows(tile, combine):
    return combine(tile.reshape(-1, 8, tile.shape[1]), axis=0)


def block_rows(index, height=BLK):
    return pl.ds(pl.multiple_of(index * height, height), height)


def by_head(block):
    first = lax.broadcasted_iota(jnp.int32, block.shape, 1) < HD
    zero = jnp.zeros_like(block)
    return jnp.concatenate([jnp.where(first, block, zero), jnp.where(first, zero, block)], axis=0)


def by_head_t(block):
    turned = block.T
    first = lax.broadcasted_iota(jnp.int32, turned.shape, 0) < HD
    zero = jnp.zeros_like(turned)
    return jnp.concatenate([jnp.where(first, turned, zero), jnp.where(first, zero, turned)], axis=1)


def own_parts(wide):
    return jnp.concatenate([wide[:HD, :BLK], wide[HD:, BLK:]], axis=0)


def dot(left, right):
    return lax.dot_general(left, right, (((1,), (0,)), ((), ())), preferred_element_type=jnp.float32)


def each_block(counts, blocks, body):
    @pl.loop(0, blocks)
    def _(index):
        for slots in range(2, MAXK + 1, 2):
            @pl.when((counts[index] + 1) // 2 == slots // 2)
            def _():
                body(index, slots)


def forward_kernel(adjacency, counts, packed, attn_out, stats, value_t, raw, *, blocks):
    query, key, value = (packed.at[:, pl.ds(PAIR * part, PAIR)] for part in range(3))

    @pl.loop(0, blocks)
    def _(index):
        value_t[index] = value[block_rows(index), :].T

    def query_block(index, slots):
        live = counts[index]
        picked = [adjacency[index, slot] for slot in range(slots)]
        queries = by_head_t(query[block_rows(index), :])
        row_max = jnp.full((8, 2 * BLK), NEG_FILL, jnp.float32)
        for slot in range(slots):
            score = dot(key[block_rows(picked[slot]), :], queries)
            if slot == slots - 1:
                score = jnp.where(slot < live, score, NEG_FILL)
            raw[slot] = score
            row_max = jnp.maximum(row_max, fold_rows(score, jnp.max))
        row_max = jnp.max(row_max, axis=0, keepdims=True)
        row_sum = jnp.zeros((8, 2 * BLK), jnp.float32)
        out_t = jnp.zeros((PAIR, 2 * BLK), jnp.float32)
        for slot in range(0, slots, 2):
            halves = []
            for each in (slot, slot + 1):
                expo = jnp.exp2((raw[each] - row_max) * BASE2)
                row_sum = row_sum + fold_rows(expo, jnp.sum)
                halves.append(expo.astype(jnp.bfloat16))
            out_t = out_t + dot(
                jnp.concatenate([value_t[picked[slot]], value_t[picked[slot + 1]]], axis=1),
                jnp.concatenate(halves, axis=0),
            )
        row_sum = jnp.sum(row_sum, axis=0, keepdims=True)
        out_t = own_parts(out_t / row_sum)
        attn_out[block_rows(index), :] = out_t.T.astype(jnp.bfloat16)
        stats[block_rows(index, 8), :] = jnp.broadcast_to(
            row_max * BASE2 + jnp.log2(row_sum), (8, 2 * BLK)
        )

    each_block(counts, blocks, query_block)


def backward_kernel(
    adjacency, counts, packed, grad, attn_out, stats, packed_g, key_t, key_sum, value_sum, *, blocks
):
    query, key, value = (packed.at[:, pl.ds(PAIR * part, PAIR)] for part in range(3))

    @pl.loop(0, blocks)
    def _(index):
        key_t[index] = key[block_rows(index), :].T
        key_sum[block_rows(index), :] = jnp.zeros((BLK, PAIR), jnp.float32)
        value_sum[block_rows(index), :] = jnp.zeros((BLK, PAIR), jnp.float32)

    def query_block(index, slots):
        live = counts[index]
        picked = [adjacency[index, slot] for slot in range(slots)]
        query_rows = query[block_rows(index), :]
        grad_rows = grad[block_rows(index), :]
        queries, queries_t = by_head(query_rows), by_head_t(query_rows)
        grads, grads_t = by_head(grad_rows), by_head_t(grad_rows)
        stat = stats[pl.ds(pl.multiple_of(index * 8, 8), 1), :]
        products = (
            grad_rows.astype(jnp.float32) * attn_out[block_rows(index), :].astype(jnp.float32)
        ).T
        row_dot = jnp.concatenate(
            [
                jnp.sum(products[:HD], axis=0, keepdims=True),
                jnp.sum(products[HD:], axis=0, keepdims=True),
            ],
            axis=1,
        )
        query_t = jnp.zeros((PAIR, 2 * BLK), jnp.float32)
        for slot in range(0, slots, 2):
            terms = []
            for each in (slot, slot + 1):
                at = block_rows(picked[each])
                prob = jnp.exp2(dot(key[at, :], queries_t) * BASE2 - stat)
                if each == slots - 1:
                    prob = jnp.where(each < live, prob, 0.0)
                prob_grad = dot(value[at, :], grads_t)
                term = (prob * (prob_grad - row_dot)).astype(jnp.bfloat16)
                key_sum[at, :] += dot(term, queries)
                value_sum[at, :] += dot(prob.astype(jnp.bfloat16), grads)
                terms.append(term)
            query_t = query_t + dot(
                jnp.concatenate([key_t[picked[slot]], key_t[picked[slot + 1]]], axis=1),
                jnp.concatenate(terms, axis=0),
            )
        packed_g[block_rows(index), :PAIR] = (own_parts(query_t).T * SCALE).astype(jnp.bfloat16)

    each_block(counts, blocks, query_block)
    packed_g[:, PAIR : 2 * PAIR] = (key_sum[...] * SCALE).astype(jnp.bfloat16)
    packed_g[:, 2 * PAIR :] = value_sum[...].astype(jnp.bfloat16)


VMEM = pl.BlockSpec(memory_space=pltpu.VMEM)
SMEM = pl.BlockSpec(memory_space=pltpu.SMEM)
PARAMS = pltpu.CompilerParams(vmem_limit_bytes=48 * 2**20)


def cost(tokens, products):
    tiles = tokens // BLK * MAXK * 2
    return pl.CostEstimate(
        flops=tiles * products * 2 * BLK * BLK * HD * 16,
        bytes_accessed=12 * tokens * PAIR,
        transcendentals=tiles * BLK * BLK,
    )


def forward(packed, adjacency, counts):
    tokens = packed.shape[0]
    blocks = tokens // BLK
    return pl.pallas_call(
        functools.partial(forward_kernel, blocks=blocks),
        in_specs=[SMEM, SMEM, VMEM],
        out_specs=[VMEM, VMEM],
        out_shape=[
            jax.ShapeDtypeStruct((tokens, PAIR), jnp.bfloat16),
            jax.ShapeDtypeStruct((blocks * 8, 2 * BLK), jnp.float32),
        ],
        scratch_shapes=[
            pltpu.VMEM((blocks, PAIR, BLK), jnp.bfloat16),
            pltpu.VMEM((MAXK, BLK, 2 * BLK), jnp.float32),
        ],
        compiler_params=PARAMS,
        cost_estimate=cost(tokens, 2),
        name="attend_forward",
    )(adjacency, counts, packed)


def backward(packed, grad, pair, attn_out, stats, adjacency, counts):
    tokens = packed.shape[0]
    blocks = tokens // BLK
    whole = lambda array: pl.BlockSpec(array.shape, lambda step: (0, 0))
    return pl.pallas_call(
        functools.partial(backward_kernel, blocks=blocks),
        grid=(1,),
        in_specs=[
            SMEM, SMEM, whole(packed), pl.BlockSpec((tokens, PAIR), lambda step: (0, pair)),
            whole(attn_out), whole(stats),
        ],
        out_specs=whole(packed),
        out_shape=jax.ShapeDtypeStruct(packed.shape, jnp.bfloat16),
        scratch_shapes=[
            pltpu.VMEM((blocks, PAIR, BLK), jnp.bfloat16),
            pltpu.VMEM((tokens, PAIR), jnp.float32),
            pltpu.VMEM((tokens, PAIR), jnp.float32),
        ],
        compiler_params=PARAMS,
        cost_estimate=cost(tokens, 5),
        name="attend_backward",
    )(adjacency, counts, packed, grad, attn_out, stats)


def pack_kernel(queries, keys, values, first, second):
    for group in range(first.shape[0]):
        for pair, out in enumerate((first, second)):
            start = PAIR * (2 * group + pair)
            for part, source in enumerate((queries, keys, values)):
                out[group, :, PAIR * part : PAIR * (part + 1)] = source[:, start : start + PAIR]


def pack(queries, keys, values, groups):
    tokens, width = queries.shape
    height = tokens // 4
    taken = pl.BlockSpec((height, width), lambda step: (step, 0))
    given = pl.BlockSpec((groups, height, 3 * PAIR), lambda step: (0, step, 0))
    return pl.pallas_call(
        pack_kernel,
        grid=(4,),
        in_specs=[taken] * 3,
        out_specs=[given] * 2,
        out_shape=[jax.ShapeDtypeStruct((groups, tokens, 3 * PAIR), queries.dtype)] * 2,
        compiler_params=PARAMS,
        name="pack",
    )(queries, keys, values)


def unpack_kernel(first, second, query_g, key_g, value_g):
    for group in range(first.shape[0]):
        for pair, source in enumerate((first, second)):
            start = PAIR * (2 * group + pair)
            for part, out in enumerate((query_g, key_g, value_g)):
                out[:, start : start + PAIR] = source[group, :, PAIR * part : PAIR * (part + 1)]


def unpack(first, second):
    groups, tokens, _ = first.shape
    height = tokens // 4
    taken = pl.BlockSpec((groups, height, 3 * PAIR), lambda step: (0, step, 0))
    given = pl.BlockSpec((height, groups * 2 * PAIR), lambda step: (step, 0))
    return pl.pallas_call(
        unpack_kernel,
        grid=(4,),
        in_specs=[taken] * 2,
        out_specs=[given] * 3,
        out_shape=[jax.ShapeDtypeStruct((tokens, groups * 2 * PAIR), first.dtype)] * 3,
        compiler_params=PARAMS,
        name="unpack",
    )(first, second)


def spread_kernel(gathered, out):
    groups, _, width = gathered.shape
    for group in range(groups):
        out[:, width * group : width * (group + 1)] = gathered[group].astype(out.dtype)


def spread(gathered):
    groups, rows, columns = gathered.shape
    height = rows // 8
    return pl.pallas_call(
        spread_kernel,
        grid=(8,),
        in_specs=[pl.BlockSpec((groups, height, columns), lambda step: (0, step, 0))],
        out_specs=pl.BlockSpec((height, groups * columns), lambda step: (step, 0)),
        out_shape=jax.ShapeDtypeStruct((rows, groups * columns), jnp.float32),
        compiler_params=PARAMS,
        name="spread",
    )(gathered)


def exchange(chunks):
    return lax.all_to_all(chunks, "seq", split_axis=0, concat_axis=0, tiled=True)


def weight_rows_sent(out_weight, member, planes, members):
    per_plane = members // planes
    height = out_weight.shape[0] // per_plane
    own = lax.dynamic_slice_in_dim(out_weight, (member % per_plane) * height, height)
    received = [own]
    for offset in range(1, planes):
        routes = [
            (s // per_plane * members + s, (s // per_plane ^ offset) * members + s)
            for s in range(members)
        ]
        received.append(lax.ppermute(own, ("fsdp", "seq"), routes))
    return received


def gather_pieces(shard, members):
    def swap(array, mask):
        return lax.ppermute(array, "seq", [(s, s ^ mask) for s in range(members)])

    height = shard.shape[0] // 2
    along, across = swap(shard, 2), swap(shard, 4)
    pieces = [
        (0, 0, shard),
        (2, 0, along),
        (4, 0, across),
        (6, 0, swap(along[:height], 4)),
        (6, height, swap(across[height:], 2)),
    ]
    return pieces + [(mask ^ 1, row, swap(piece, 1)) for mask, row, piece in pieces]


def project_kernel(places, where, *refs, offsets, groups):
    count = len(places)
    pieces, rest = refs[:count], refs[count:]
    weights, (first, second, attn_grad, terms, whole, weight, landed, fetched) = rest[:offsets], rest[offsets:]
    local = whole.shape[0] // groups
    copies = []
    for number, (mask, row) in enumerate(places):
        start = pl.multiple_of((where[0] ^ mask) * local + row, BLK)
        target = whole.at[pl.ds(start, pieces[number].shape[0]), :]
        copies.append((start, pltpu.make_async_copy(pieces[number], target, landed.at[number])))
    for offset in range(offsets):
        @pl.when(where[1] == offset)
        def _():
            pltpu.make_async_copy(weights[offset], weight, fetched).start()
    for _, copy in copies:
        copy.start()
    pltpu.make_async_copy(weights[0], weight, fetched).wait()
    for number, (start, copy) in enumerate(copies):
        copy.wait()
        rows = pl.ds(start, pieces[number].shape[0])
        attn_grad[rows, :] = lax.dot_general(
            whole[rows, :], weight[...], (((1,), (1,)), ((), ())), preferred_element_type=jnp.float32
        ).astype(jnp.bfloat16)
    width = whole.shape[1] // groups
    attn_t = jnp.concatenate([first[...].T, second[...].T], axis=0)
    for group in range(groups):
        terms[group] = dot(attn_t, whole[:, width * group : width * (group + 1)]).astype(jnp.bfloat16)


def project(pieces, weights, first, second, where, groups):
    places = [(mask, row) for mask, row, _ in pieces]
    arrays = [piece for _, _, piece in pieces]
    height, width = weights[0].shape
    tokens = first.shape[0]
    far = pl.BlockSpec(memory_space=pl.ANY)
    return pl.pallas_call(
        lambda *refs: project_kernel(places, *refs, offsets=len(weights), groups=groups),
        in_specs=[SMEM] + [far] * (len(arrays) + len(weights)) + [VMEM] * 2,
        out_specs=[VMEM] * 2,
        out_shape=[
            jax.ShapeDtypeStruct((tokens, height), jnp.bfloat16),
            jax.ShapeDtypeStruct((groups, height, width // groups), jnp.bfloat16),
        ],
        scratch_shapes=[
            pltpu.VMEM((tokens, width), jnp.bfloat16),
            pltpu.VMEM((height, width), jnp.bfloat16),
            pltpu.SemaphoreType.DMA((len(arrays),)),
            pltpu.SemaphoreType.DMA,
        ],
        compiler_params=PARAMS,
        cost_estimate=pl.CostEstimate(
            flops=4 * tokens * width * height,
            bytes_accessed=2 * tokens * width + 8 * height * width,
            transcendentals=0,
        ),
        name="project",
    )(where, *arrays, *weights, first, second)


def plane_sum(rows, plane, planes):
    height = rows.shape[0] // planes

    def part(offset):
        return lax.dynamic_slice_in_dim(rows, (plane ^ offset) * height, height)

    total = part(0).astype(jnp.float32)
    for offset in range(1, planes):
        routes = [(z, z ^ offset) for z in range(planes)]
        total = total + lax.ppermute(part(offset), "fsdp", routes).astype(jnp.float32)
    return total


def fits_pairs(sizes):
    planes, members = sizes["fsdp"], sizes["seq"]
    return members == 8 and planes == 4 and members * 2 * PAIR == HEADS * HD


def pair_device(queries, keys, values, out_grad, out_weight, key_blocks, block_counts):
    planes, members = lax.axis_size("fsdp"), lax.axis_size("seq")
    plane, member = lax.axis_index("fsdp"), lax.axis_index("seq")
    local_tokens, model_width = queries.shape[1:]
    tokens = local_tokens * members
    adjacency, counts = key_blocks[0], block_counts[0]

    chunks = pack(queries[0], keys[0], values[0], members)
    packed = [exchange(chunk).reshape(tokens, 3 * PAIR) for chunk in chunks]
    weights = weight_rows_sent(out_weight, member, planes, members)
    pieces = gather_pieces(out_grad[0], members)
    forwards = [forward(one, adjacency, counts) for one in packed]
    where = jnp.stack([member, plane ^ (member // (members // planes))]).astype(jnp.int32)
    attn_grad, by_columns = project(
        pieces, weights, forwards[0][0], forwards[1][0], where, members
    )
    returned = []
    for pair in range(2):
        attn_out, stats = forwards[pair]
        packed_g = backward(packed[pair], attn_grad, pair, attn_out, stats, adjacency, counts)
        returned.append(exchange(packed_g.reshape(members, local_tokens, 3 * PAIR)))
    query_g, key_g, value_g = unpack(*returned)

    columns = exchange(by_columns).reshape(model_width, -1)
    summed = plane_sum(columns, plane, planes).astype(jnp.bfloat16)
    wo_grad = spread(lax.all_gather(summed, "seq", axis=0))
    return (query_g[None], key_g[None], value_g[None], wo_grad)


def general_device(queries, keys, values, out_grad, out_weight, key_blocks, block_counts):
    local_tokens = queries.shape[1]
    model_width = queries.shape[2]
    seq_devices = lax.axis_size("seq")
    loss_grad = out_grad[0]
    adjacency = key_blocks[0]
    slot_live = jnp.arange(MAXK)[None, :] < block_counts[0][:, None]

    def head_groups(array):
        return array[0].reshape(local_tokens, seq_devices, HEADS // seq_devices, HD)

    attn_grad = lax.dot_general(
        loss_grad,
        lax.all_gather(out_weight, "fsdp", axis=0, tiled=True),
        (((1,), (1,)), ((), ())),
        preferred_element_type=jnp.float32,
    ).astype(jnp.bfloat16)

    def attend(heads_in):
        query_h, key_h, value_h, grad_h = (member[:, 0] for member in heads_in)
        row_max, row_sum, attn_blocks = head_forward(query_h, key_h, value_h, adjacency, slot_live)
        query_g, key_g, value_g = head_backward(
            query_h, key_h, value_h, grad_h, row_max, row_sum, attn_blocks, adjacency, slot_live
        )
        return (query_g, key_g, value_g, attn_blocks.reshape(-1, query_h.shape[1], HD))

    query_g, key_g, value_g, attn_heads = attend(
        (
            lax.all_to_all(head_groups(queries), "seq", split_axis=1, concat_axis=0, tiled=True),
            lax.all_to_all(head_groups(keys), "seq", split_axis=1, concat_axis=0, tiled=True),
            lax.all_to_all(head_groups(values), "seq", split_axis=1, concat_axis=0, tiled=True),
            lax.all_to_all(
                head_groups(attn_grad[None]), "seq", split_axis=1, concat_axis=0, tiled=True
            ),
        )
    )
    query_t, key_t, value_t, attn_t = (
        lax.all_to_all(query_g, "seq", split_axis=0, concat_axis=1, tiled=True),
        lax.all_to_all(key_g, "seq", split_axis=0, concat_axis=1, tiled=True),
        lax.all_to_all(value_g, "seq", split_axis=0, concat_axis=1, tiled=True),
        lax.all_to_all(attn_heads, "seq", split_axis=0, concat_axis=1, tiled=True),
    )
    attn_out = attn_t.reshape(local_tokens, model_width)
    share = lax.psum_scatter(
        lax.dot_general(
            attn_out, loss_grad, (((0,), (0,)), ((), ())), preferred_element_type=jnp.float32
        ),
        ("fsdp", "seq"),
        scatter_dimension=0,
        tiled=True,
    )
    wo_grad = lax.all_gather(share.astype(jnp.bfloat16), "seq", axis=0, tiled=True).astype(
        share.dtype
    )

    def to_tokens(array):
        return array.reshape(1, local_tokens, model_width)

    return (to_tokens(query_t), to_tokens(key_t), to_tokens(value_t), wo_grad)


def on_device(mesh):
    return pair_device if fits_pairs(mesh.shape) else general_device


def solution(mesh):
    return jax.shard_map(
        on_device(mesh),
        mesh=mesh,
        in_specs=(
            P("fsdp", "seq", None),
            P("fsdp", "seq", None),
            P("fsdp", "seq", None),
            P("fsdp", "seq", None),
            P("fsdp", None),
            P("fsdp", None, None),
            P("fsdp", None),
        ),
        out_specs=(
            P("fsdp", "seq", None),
            P("fsdp", "seq", None),
            P("fsdp", "seq", None),
            P("fsdp", None),
        ),
        check_vma=False,
    )
```

```python
import functools
import math

import jax
import jax.numpy as jnp
from jax import lax
from jax.experimental import pallas as pl
from jax.experimental.pallas import tpu as pltpu
from jax.sharding import PartitionSpec as P

HEADS = 32
HD = 64
BLK = 128
MAXK = 10


NEG_FILL = -1e30


def pair_scores(query_blocks, chosen):
    return jnp.einsum(
        "iqhd,ikhd->ihqk", query_blocks, chosen, preferred_element_type=jnp.float32
    ) * HD ** (-0.5)


def blocked(array):
    return array.reshape(-1, BLK, array.shape[1], HD)


def head_forward(query_h, key_h, value_h, adjacency, slot_live):
    query_blocks = blocked(query_h)
    key_heads = blocked(key_h)
    value_heads = blocked(value_h)
    blocks_total = query_blocks.shape[0]
    head_count = query_blocks.shape[2]

    def stat_step(carried, slot):
        row_max, row_sum = carried
        score = pair_scores(query_blocks, key_heads[adjacency[:, slot]])
        usable = slot_live[:, slot][:, None, None, None]
        score = jnp.where(usable, score, NEG_FILL)
        new_max = jnp.maximum(row_max, jnp.max(score, axis=-1))
        expo = jnp.where(usable, jnp.exp(score - new_max[..., None]), 0.0)
        row_sum = row_sum * jnp.exp(row_max - new_max) + jnp.sum(expo, axis=-1)
        return ((new_max, row_sum), None)

    start_max = jnp.full((blocks_total, head_count, BLK), NEG_FILL, jnp.float32)
    start_sum = jnp.zeros((blocks_total, head_count, BLK), jnp.float32)
    (row_max, row_sum), _ = lax.scan(stat_step, (start_max, start_sum), jnp.arange(MAXK))

    def output_step(accum, slot):
        picked = adjacency[:, slot]
        score = pair_scores(query_blocks, key_heads[picked])
        usable = slot_live[:, slot][:, None, None, None]
        prob_half = jnp.where(
            usable, jnp.exp(score - row_max[..., None]) / row_sum[..., None], 0.0
        ).astype(jnp.bfloat16)
        accum = accum + jnp.einsum(
            "ihqk,ikhd->iqhd", prob_half, value_heads[picked], preferred_element_type=jnp.float32
        )
        return (accum, None)

    start_out = jnp.zeros(query_blocks.shape, jnp.float32)
    accum, _ = lax.scan(output_step, start_out, jnp.arange(MAXK))
    return (row_max, row_sum, accum.astype(jnp.bfloat16))


def head_backward(
    query_h, key_h, value_h, grad_h, row_max, row_sum, attn_blocks, adjacency, slot_live
):
    query_blocks = blocked(query_h)
    key_heads = blocked(key_h)
    value_heads = blocked(value_h)
    grad_blocks = blocked(grad_h)
    scale_factor = HD ** (-0.5)
    row_dot = jnp.sum(
        grad_blocks.astype(jnp.float32) * attn_blocks.astype(jnp.float32), axis=-1
    ).transpose(0, 2, 1)

    def grad_step(carried, slot):
        query_accum, key_accum, value_accum = carried
        picked = adjacency[:, slot]
        chosen_keys = key_heads[picked]
        chosen_values = value_heads[picked]
        score = pair_scores(query_blocks, chosen_keys)
        usable = slot_live[:, slot][:, None, None, None]
        prob_full = jnp.where(usable, jnp.exp(score - row_max[..., None]) / row_sum[..., None], 0.0)
        prob_half = prob_full.astype(jnp.bfloat16)
        prob_grad = jnp.einsum(
            "iqhd,ikhd->ihqk", grad_blocks, chosen_values, preferred_element_type=jnp.float32
        )
        score_grad = (prob_full * (prob_grad - row_dot[..., None])).astype(jnp.bfloat16)
        query_accum = (
            query_accum
            + jnp.einsum(
                "ihqk,ikhd->iqhd", score_grad, chosen_keys, preferred_element_type=jnp.float32
            )
            * scale_factor
        )
        key_terms = (
            jnp.einsum(
                "ihqk,iqhd->ikhd", score_grad, query_blocks, preferred_element_type=jnp.float32
            )
            * scale_factor
        )
        value_terms = jnp.einsum(
            "ihqk,iqhd->ikhd", prob_half, grad_blocks, preferred_element_type=jnp.float32
        )
        key_accum = key_accum.at[picked].add(key_terms)
        value_accum = value_accum.at[picked].add(value_terms)
        return ((query_accum, key_accum, value_accum), None)

    zeros_start = jnp.zeros(query_blocks.shape, jnp.float32)
    (query_accum, key_accum, value_accum), _ = lax.scan(
        grad_step, (zeros_start, zeros_start, zeros_start), jnp.arange(MAXK)
    )
    head_count = query_h.shape[1]
    return tuple(
        (
            accum.astype(jnp.bfloat16).reshape(-1, head_count, HD)
            for accum in (query_accum, key_accum, value_accum)
        )
    )


PAIR = 2 * HD
SCALE = HD ** (-0.5)
BASE2 = SCALE * math.log2(math.e)


def fold_rows(tile, combine):
    return combine(tile.reshape(-1, 8, tile.shape[1]), axis=0)


def block_rows(index, height=BLK):
    return pl.ds(pl.multiple_of(index * height, height), height)


def by_head(block):
    first = lax.broadcasted_iota(jnp.int32, block.shape, 1) < HD
    zero = jnp.zeros_like(block)
    return jnp.concatenate([jnp.where(first, block, zero), jnp.where(first, zero, block)], axis=0)


def by_head_t(block):
    turned = block.T
    first = lax.broadcasted_iota(jnp.int32, turned.shape, 0) < HD
    zero = jnp.zeros_like(turned)
    return jnp.concatenate([jnp.where(first, turned, zero), jnp.where(first, zero, turned)], axis=1)


def own_parts(wide):
    return jnp.concatenate([wide[:HD, :BLK], wide[HD:, BLK:]], axis=0)


def columns(pair, part):
    return pl.ds(PAIR * (3 * pair + part), PAIR)


def dot(left, right):
    return lax.dot_general(left, right, (((1,), (0,)), ((), ())), preferred_element_type=jnp.float32)


def stack(source, places, right):
    return dot(jnp.concatenate([source[at, :] for at in places], axis=0), right)


def each_block(counts, begin, end, body):
    @pl.loop(begin, end)
    def _(index):
        for slots in range(2, MAXK + 1):
            @pl.when(counts[index] == slots)
            def _():
                body(index, slots)


def forward_kernel(adjacency, counts, packed, first, second, stats, value_t, *, blocks):
    outs = (first, second)

    @pl.loop(0, blocks)
    def _(index):
        for pair in range(2):
            value_t[pair, index] = packed[block_rows(index), columns(pair, 2)].T

    def query_block(index, slots):
        picked = [adjacency[index, slot] for slot in range(slots)]
        places = [block_rows(block) for block in picked]
        raws = [
            stack(
                packed.at[:, columns(pair, 1)],
                places,
                by_head_t(packed[block_rows(index), columns(pair, 0)]),
            )
            for pair in range(2)
        ]
        for pair, raw in enumerate(raws):
            row_max = jnp.max(fold_rows(raw, jnp.max), axis=0, keepdims=True)
            expo = jnp.exp2((raw - row_max) * BASE2)
            row_sum = jnp.sum(fold_rows(expo, jnp.sum), axis=0, keepdims=True)
            out_t = dot(
                jnp.concatenate([value_t[pair, block] for block in picked], axis=1),
                expo.astype(jnp.bfloat16),
            )
            outs[pair][block_rows(index), :] = own_parts(out_t / row_sum).T.astype(jnp.bfloat16)
            stats[pair, block_rows(index, 8), :] = jnp.broadcast_to(
                row_max * BASE2 + jnp.log2(row_sum), (8, 2 * BLK)
            )

    each_block(counts, 0, blocks, query_block)


def backward_kernel(
    adjacency, counts, packed, grad, attn_out, stats, *refs, blocks, begin, end
):
    query, key, value = (packed.at[:, pl.ds(PAIR * part, PAIR)] for part in range(3))
    carried, rest = refs[: 3 if begin else 0], refs[3 if begin else 0 :]
    outs, (key_t, key_sum, value_sum) = rest[:-3], rest[-3:]
    query_g = outs[0]

    @pl.loop(0, blocks)
    def _(index):
        key_t[index] = key[block_rows(index), :].T
        if begin:
            key_sum[block_rows(index), :] = carried[1][block_rows(index), :]
            value_sum[block_rows(index), :] = carried[2][block_rows(index), :]
        else:
            key_sum[block_rows(index), :] = jnp.zeros((BLK, PAIR), jnp.float32)
            value_sum[block_rows(index), :] = jnp.zeros((BLK, PAIR), jnp.float32)

    def query_block(index, slots):
        picked = [adjacency[index, slot] for slot in range(slots)]
        query_rows = query[block_rows(index), :]
        grad_rows = grad[block_rows(index), :]
        queries, queries_t = by_head(query_rows), by_head_t(query_rows)
        grads, grads_t = by_head(grad_rows), by_head_t(grad_rows)
        stat = stats[0, pl.ds(pl.multiple_of(index * 8, 8), 1), :]
        products = (
            grad_rows.astype(jnp.float32) * attn_out[block_rows(index), :].astype(jnp.float32)
        ).T
        row_dot = jnp.concatenate(
            [
                jnp.sum(products[:HD], axis=0, keepdims=True),
                jnp.sum(products[HD:], axis=0, keepdims=True),
            ],
            axis=1,
        )
        places = [block_rows(block) for block in picked]
        prob = jnp.exp2(stack(key, places, queries_t) * BASE2 - stat)
        term = (prob * (stack(value, places, grads_t) - row_dot)).astype(jnp.bfloat16)
        key_terms = dot(term, queries)
        value_terms = dot(prob.astype(jnp.bfloat16), grads)
        for number, at in enumerate(places):
            key_sum[at, :] += key_terms[BLK * number : BLK * (number + 1)]
            value_sum[at, :] += value_terms[BLK * number : BLK * (number + 1)]
        query_t = dot(jnp.concatenate([key_t[block] for block in picked], axis=1), term)
        query_g[block_rows(index), :PAIR] = (own_parts(query_t).T * SCALE).astype(jnp.bfloat16)

    each_block(counts, begin, end, query_block)
    if end < blocks:
        outs[1][...], outs[2][...] = key_sum[...], value_sum[...]
    else:
        if begin:
            query_g[: BLK * begin, :PAIR] = carried[0][: BLK * begin, :]
        query_g[:, PAIR : 2 * PAIR] = (key_sum[...] * SCALE).astype(jnp.bfloat16)
        query_g[:, 2 * PAIR :] = value_sum[...].astype(jnp.bfloat16)


VMEM = pl.BlockSpec(memory_space=pltpu.VMEM)
SMEM = pl.BlockSpec(memory_space=pltpu.SMEM)
PARAMS = pltpu.CompilerParams(vmem_limit_bytes=48 * 2**20)


def cost(tokens, products):
    tiles = tokens // BLK * MAXK * 2
    return pl.CostEstimate(
        flops=tiles * products * 2 * BLK * BLK * HD * 4,
        bytes_accessed=12 * tokens * PAIR,
        transcendentals=tiles * BLK * BLK,
    )


def forward(packed, adjacency, counts):
    tokens = packed.shape[0]
    blocks = tokens // BLK
    return pl.pallas_call(
        functools.partial(forward_kernel, blocks=blocks),
        in_specs=[SMEM, SMEM, VMEM],
        out_specs=[VMEM] * 3,
        out_shape=[
            jax.ShapeDtypeStruct((tokens, PAIR), jnp.bfloat16),
            jax.ShapeDtypeStruct((tokens, PAIR), jnp.bfloat16),
            jax.ShapeDtypeStruct((2, blocks * 8, 2 * BLK), jnp.float32),
        ],
        scratch_shapes=[pltpu.VMEM((2, blocks, PAIR, BLK), jnp.bfloat16)],
        compiler_params=PARAMS,
        cost_estimate=cost(tokens, 4),
        name="attend_forward",
    )(adjacency, counts, packed)


def backward(packed, grad, pair, attn_out, stats, adjacency, counts, begin=0, end=None, carried=()):
    tokens = packed.shape[0]
    blocks = tokens // BLK
    end = end or blocks
    one = pl.BlockSpec((tokens, PAIR), lambda step: (0, 0))
    three = pl.BlockSpec((tokens, 3 * PAIR), lambda step: (0, pair))
    whole = pl.BlockSpec((tokens, 3 * PAIR), lambda step: (0, 0))
    if end < blocks:
        out_specs = [one] * 3
        out_shape = [jax.ShapeDtypeStruct((tokens, PAIR), jnp.bfloat16)]
        out_shape += [jax.ShapeDtypeStruct((tokens, PAIR), jnp.float32)] * 2
    else:
        out_specs = whole
        out_shape = jax.ShapeDtypeStruct((tokens, 3 * PAIR), jnp.bfloat16)
    return pl.pallas_call(
        functools.partial(backward_kernel, blocks=blocks, begin=begin, end=end),
        grid=(1,),
        in_specs=[
            SMEM, SMEM, three, pl.BlockSpec((tokens, PAIR), lambda step: (0, pair)), one,
            pl.BlockSpec((1, blocks * 8, 2 * BLK), lambda step: (pair, 0, 0)),
        ] + [one] * len(carried),
        out_specs=out_specs,
        out_shape=out_shape,
        scratch_shapes=[
            pltpu.VMEM((blocks, PAIR, BLK), jnp.bfloat16),
            pltpu.VMEM((tokens, PAIR), jnp.float32),
            pltpu.VMEM((tokens, PAIR), jnp.float32),
        ],
        compiler_params=PARAMS,
        cost_estimate=cost(tokens * (end - begin) // blocks, 5),
        name="attend_backward",
    )(adjacency, counts, packed, grad, attn_out, stats, *carried)


WIDE = pltpu.CompilerParams(vmem_limit_bytes=60 * 2**20)


STEPS = 4


def pack_kernel(queries, keys, values, weight, packed, own):
    for group in range(packed.shape[0]):
        for pair in range(2):
            start = PAIR * (2 * group + pair)
            for part, source in enumerate((queries, keys, values)):
                packed[group, :, columns(pair, part)] = source[:, start : start + PAIR]
    own[...] = weight[...]


def pack(queries, keys, values, out_weight, groups):
    tokens, width = queries.shape
    height, share = tokens // STEPS, width // groups // STEPS

    def weight_place(step):
        skipped = lax.axis_index("seq") * (width // groups) % out_weight.shape[0]
        return (skipped // share + step, 0)

    taken = pl.BlockSpec((height, width), lambda step: (step, 0))
    return pl.pallas_call(
        pack_kernel,
        grid=(STEPS,),
        in_specs=[taken] * 3 + [pl.BlockSpec((share, width), weight_place)],
        out_specs=[
            pl.BlockSpec((groups, height, 6 * PAIR), lambda step: (0, step, 0)),
            pl.BlockSpec((share, width), lambda step: (step, 0)),
        ],
        out_shape=[
            jax.ShapeDtypeStruct((groups, tokens, 6 * PAIR), queries.dtype),
            jax.ShapeDtypeStruct((width // groups, width), queries.dtype),
        ],
        compiler_params=WIDE,
        name="pack",
    )(queries, keys, values, out_weight)


def unpack_kernel(first, second, query_g, key_g, value_g):
    for group in range(first.shape[0]):
        for pair, source in enumerate((first, second)):
            start = PAIR * (2 * group + pair)
            for part, out in enumerate((query_g, key_g, value_g)):
                out[:, start : start + PAIR] = source[group, :, PAIR * part : PAIR * (part + 1)]


def unpack(first, second):
    groups, tokens, _ = first.shape
    height = tokens // 4
    taken = pl.BlockSpec((groups, height, 3 * PAIR), lambda step: (0, step, 0))
    given = pl.BlockSpec((height, groups * 2 * PAIR), lambda step: (step, 0))
    return pl.pallas_call(
        unpack_kernel,
        grid=(4,),
        in_specs=[taken] * 2,
        out_specs=[given] * 3,
        out_shape=[jax.ShapeDtypeStruct((tokens, groups * 2 * PAIR), first.dtype)] * 3,
        compiler_params=WIDE,
        name="unpack",
    )(first, second)


def spread_kernel(*refs):
    pieces, out = refs[:-1], refs[-1]
    member = lax.axis_index("seq")
    for mask, piece in enumerate(pieces):
        width = piece.shape[1]
        start = pl.multiple_of((member ^ mask) * width, width)
        out[:, pl.ds(start, width)] = piece[...].astype(out.dtype)


def spread(pieces):
    rows, width = pieces[0].shape
    height = rows // STEPS
    return pl.pallas_call(
        spread_kernel,
        grid=(STEPS,),
        in_specs=[pl.BlockSpec((height, width), lambda step: (step, 0))] * len(pieces),
        out_specs=pl.BlockSpec((height, len(pieces) * width), lambda step: (step, 0)),
        out_shape=jax.ShapeDtypeStruct((rows, len(pieces) * width), jnp.float32),
        compiler_params=WIDE,
        name="spread",
    )(*pieces)


def exchange(chunks):
    return lax.all_to_all(chunks, "seq", split_axis=0, concat_axis=0, tiled=True)


WEIGHT_ROUTES = (
    ((0, 1), (1, 2), (2, 1), (3, 2)),
    ((0, 2), (1, 3), (2, 0), (3, 1)),
    ((2, 3), (1, 0), (2, 3), (1, 0)),
)


def send_weight(rows, step):
    planes, members = lax.axis_size("fsdp"), lax.axis_size("seq")
    routes = []
    for member in range(members):
        source, target = WEIGHT_ROUTES[step][member * planes // members]
        routes.append((source * members + member, target * members + member))
    return lax.ppermute(rows, ("fsdp", "seq"), routes)


def swap(array, mask):
    routes = [(s, s ^ mask) for s in range(lax.axis_size("seq"))]
    return lax.ppermute(array, "seq", routes)


def project_kernel(places, *refs):
    pieces, rest = refs[: len(places)], refs[len(places) :]
    weights, (first, second, attn_grad, terms) = rest[:4], rest[4:8]
    whole, weight, landed, fetched = rest[8:]
    plane, member = lax.axis_index("fsdp"), lax.axis_index("seq")
    local = whole.shape[0] // terms.shape[0]
    copies = []
    for number, (mask, row) in enumerate(places):
        start = pl.multiple_of((member ^ mask) * local + row, BLK)
        target = whole.at[pl.ds(start, pieces[number].shape[0]), :]
        copies.append(pltpu.make_async_copy(pieces[number], target, landed.at[number]))
    for source, rows in enumerate(weights):
        held = (plane == member // 2) if source == 0 else False
        for home, (_, target) in enumerate(WEIGHT_ROUTES[source - 1] if source else ()):
            held = held | ((member // 2 == home) & (plane == target))

        @pl.when(held)
        def _():
            pltpu.make_async_copy(rows, weight, fetched).start()
    for copy in copies:
        copy.start()
    pltpu.make_async_copy(weights[0], weight, fetched).wait()
    for copy in copies:
        copy.wait()
    attn_t = jnp.concatenate([first[...].T, second[...].T], axis=0)
    groups, _, width = terms.shape
    for group in range(0, groups, 2):
        wide = dot(attn_t, whole[:, width * group : width * (group + 2)]).astype(terms.dtype)
        terms[group], terms[group + 1] = wide[:, :width], wide[:, width:]

    @pl.loop(0, 4)
    def _(part):
        rows = block_rows(part, whole.shape[0] // 4)
        attn_grad[rows, :] = lax.dot_general(
            whole[rows, :], weight[...], (((1,), (1,)), ((), ())), preferred_element_type=jnp.float32
        ).astype(attn_grad.dtype)


def project(pieces, weights, first, second, groups):
    places = [(mask, row) for mask, row, _ in pieces]
    arrays = [piece for _, _, piece in pieces]
    height, width = weights[0].shape
    tokens = first.shape[0]
    far = pl.BlockSpec(memory_space=pl.ANY)
    return pl.pallas_call(
        functools.partial(project_kernel, places),
        in_specs=[far] * (len(arrays) + len(weights)) + [VMEM] * 2,
        out_specs=[VMEM] * 2,
        out_shape=[
            jax.ShapeDtypeStruct((tokens, height), jnp.bfloat16),
            jax.ShapeDtypeStruct((groups, height, width // groups), jnp.bfloat16),
        ],
        scratch_shapes=[
            pltpu.VMEM((tokens, width), jnp.bfloat16),
            pltpu.VMEM((height, width), jnp.bfloat16),
            pltpu.SemaphoreType.DMA((len(arrays),)),
            pltpu.SemaphoreType.DMA,
        ],
        compiler_params=PARAMS,
        cost_estimate=pl.CostEstimate(
            flops=4 * tokens * width * height,
            bytes_accessed=2 * tokens * width + 8 * height * width,
            transcendentals=0,
        ),
        name="project",
    )(*arrays, *weights, first, second)


def split_kernel(whole, *parts):
    height = parts[0].shape[0]
    for offset, part in enumerate(parts):
        start = pl.multiple_of((lax.axis_index("fsdp") ^ offset) * height, height)
        part[...] = whole[pl.ds(start, height), :]


def split(whole, planes):
    rows, width = whole.shape
    return pl.pallas_call(
        split_kernel,
        in_specs=[VMEM],
        out_specs=[VMEM] * planes,
        out_shape=[jax.ShapeDtypeStruct((rows // planes, width), whole.dtype)] * planes,
        compiler_params=PARAMS,
        name="split",
    )(whole)


def fits_pairs(sizes):
    planes, members = sizes["fsdp"], sizes["seq"]
    return members == 8 and planes == 4 and members * 2 * PAIR == HEADS * HD


def pair_device(queries, keys, values, out_grad, out_weight, key_blocks, block_counts):
    planes, members = lax.axis_size("fsdp"), lax.axis_size("seq")
    home = lax.axis_index("seq") // 2
    local_tokens, model_width = queries.shape[1:]
    tokens = local_tokens * members
    adjacency, counts = key_blocks[0], block_counts[0]
    shard = out_grad[0]

    along, across = swap(shard, 2), swap(shard, 4)
    chunks, own = pack(queries[0], keys[0], values[0], out_weight, members)
    packed = exchange(chunks).reshape(tokens, 6 * PAIR)
    near, far = send_weight(own, 0), send_weight(own, 1)
    beside = swap(shard, 1)
    packed, shard, near, far, along, across, beside = lax.optimization_barrier(
        (packed, shard, near, far, along, across, beside)
    )

    last = send_weight(jnp.where((home == 1) | (home == 2), own, far), 2)
    middle = local_tokens // 2
    corner_top, corner_bottom = swap(along[:middle], 4), swap(across[middle:], 2)
    beside = [beside, swap(along, 1), swap(across, 1)]
    first, second, stats = forward(packed, adjacency, counts)
    first, second, stats, corner_top, corner_bottom, *beside = lax.optimization_barrier(
        (first, second, stats, corner_top, corner_bottom, *beside)
    )
    pieces = [(0, 0, shard), (2, 0, along), (4, 0, across)]
    pieces += [(mask, 0, piece) for mask, piece in zip((1, 3, 5), beside)]
    pieces += [(6, 0, corner_top), (6, middle, corner_bottom)]
    pieces += [(7, 0, swap(corner_top, 1)), (7, middle, swap(corner_bottom, 1))]
    attn_grad, by_columns = project(pieces, (own, near, far, last), first, second, members)

    terms = exchange(by_columns).reshape(model_width, -1)
    first_g = backward(packed, attn_grad, 0, first, stats, adjacency, counts)
    first_g, terms = lax.optimization_barrier((first_g, terms))
    parts = split(terms, planes)
    received = [
        lax.ppermute(parts[offset], "fsdp", [(z, z ^ offset) for z in range(planes)])
        for offset in range(1, planes)
    ]
    first_r = exchange(first_g.reshape(members, local_tokens, 3 * PAIR))
    split_at = tokens // BLK // 2
    started = backward(
        packed, attn_grad, 1, second, stats, adjacency, counts, end=split_at
    )
    *started, received = lax.optimization_barrier((*started, received))
    summed = sum(part.astype(jnp.float32) for part in [parts[0], *received]).astype(terms.dtype)
    sides = [summed, swap(summed, 2), swap(summed, 4), swap(summed, 6)]
    second_g = backward(
        packed, attn_grad, 1, second, stats, adjacency, counts, begin=split_at, carried=started
    )
    second_g, *sides = lax.optimization_barrier((second_g, *sides))
    wo_grad = spread([part for one in sides for part in (one, swap(one, 1))])
    second_r = exchange(second_g.reshape(members, local_tokens, 3 * PAIR))
    query_g, key_g, value_g = unpack(first_r, second_r)
    return (query_g[None], key_g[None], value_g[None], wo_grad)


def general_device(queries, keys, values, out_grad, out_weight, key_blocks, block_counts):
    local_tokens = queries.shape[1]
    model_width = queries.shape[2]
    seq_devices = lax.axis_size("seq")
    loss_grad = out_grad[0]
    adjacency = key_blocks[0]
    slot_live = jnp.arange(MAXK)[None, :] < block_counts[0][:, None]

    def head_groups(array):
        return array[0].reshape(local_tokens, seq_devices, HEADS // seq_devices, HD)

    attn_grad = lax.dot_general(
        loss_grad,
        lax.all_gather(out_weight, "fsdp", axis=0, tiled=True),
        (((1,), (1,)), ((), ())),
        preferred_element_type=jnp.float32,
    ).astype(jnp.bfloat16)

    def attend(heads_in):
        query_h, key_h, value_h, grad_h = (member[:, 0] for member in heads_in)
        row_max, row_sum, attn_blocks = head_forward(query_h, key_h, value_h, adjacency, slot_live)
        query_g, key_g, value_g = head_backward(
            query_h, key_h, value_h, grad_h, row_max, row_sum, attn_blocks, adjacency, slot_live
        )
        return (query_g, key_g, value_g, attn_blocks.reshape(-1, query_h.shape[1], HD))

    query_g, key_g, value_g, attn_heads = attend(
        (
            lax.all_to_all(head_groups(queries), "seq", split_axis=1, concat_axis=0, tiled=True),
            lax.all_to_all(head_groups(keys), "seq", split_axis=1, concat_axis=0, tiled=True),
            lax.all_to_all(head_groups(values), "seq", split_axis=1, concat_axis=0, tiled=True),
            lax.all_to_all(
                head_groups(attn_grad[None]), "seq", split_axis=1, concat_axis=0, tiled=True
            ),
        )
    )
    query_t, key_t, value_t, attn_t = (
        lax.all_to_all(query_g, "seq", split_axis=0, concat_axis=1, tiled=True),
        lax.all_to_all(key_g, "seq", split_axis=0, concat_axis=1, tiled=True),
        lax.all_to_all(value_g, "seq", split_axis=0, concat_axis=1, tiled=True),
        lax.all_to_all(attn_heads, "seq", split_axis=0, concat_axis=1, tiled=True),
    )
    attn_out = attn_t.reshape(local_tokens, model_width)
    share = lax.psum_scatter(
        lax.dot_general(
            attn_out, loss_grad, (((0,), (0,)), ((), ())), preferred_element_type=jnp.float32
        ),
        ("fsdp", "seq"),
        scatter_dimension=0,
        tiled=True,
    )
    wo_grad = lax.all_gather(share.astype(jnp.bfloat16), "seq", axis=0, tiled=True).astype(
        share.dtype
    )

    def to_tokens(array):
        return array.reshape(1, local_tokens, model_width)

    return (to_tokens(query_t), to_tokens(key_t), to_tokens(value_t), wo_grad)


def on_device(mesh):
    return pair_device if fits_pairs(mesh.shape) else general_device


def solution(mesh):
    return jax.shard_map(
        on_device(mesh),
        mesh=mesh,
        in_specs=(
            P("fsdp", "seq", None),
            P("fsdp", "seq", None),
            P("fsdp", "seq", None),
            P("fsdp", "seq", None),
            P("fsdp", None),
            P("fsdp", None, None),
            P("fsdp", None),
        ),
        out_specs=(
            P("fsdp", "seq", None),
            P("fsdp", "seq", None),
            P("fsdp", "seq", None),
            P("fsdp", None),
        ),
        check_vma=False,
    )
```

```python
import functools
import math

import jax
import jax.numpy as jnp
from jax import lax
from jax.experimental import pallas as pl
from jax.experimental.pallas import tpu as pltpu
from jax.sharding import PartitionSpec as P

HEADS = 32
HD = 64
BLK = 128
MAXK = 10


NEG_FILL = -1e30


def pair_scores(query_blocks, chosen):
    return jnp.einsum(
        "iqhd,ikhd->ihqk", query_blocks, chosen, preferred_element_type=jnp.float32
    ) * HD ** (-0.5)


def blocked(array):
    return array.reshape(-1, BLK, array.shape[1], HD)


def head_forward(query_h, key_h, value_h, adjacency, slot_live):
    query_blocks = blocked(query_h)
    key_heads = blocked(key_h)
    value_heads = blocked(value_h)
    blocks_total = query_blocks.shape[0]
    head_count = query_blocks.shape[2]

    def stat_step(carried, slot):
        row_max, row_sum = carried
        score = pair_scores(query_blocks, key_heads[adjacency[:, slot]])
        usable = slot_live[:, slot][:, None, None, None]
        score = jnp.where(usable, score, NEG_FILL)
        new_max = jnp.maximum(row_max, jnp.max(score, axis=-1))
        expo = jnp.where(usable, jnp.exp(score - new_max[..., None]), 0.0)
        row_sum = row_sum * jnp.exp(row_max - new_max) + jnp.sum(expo, axis=-1)
        return ((new_max, row_sum), None)

    start_max = jnp.full((blocks_total, head_count, BLK), NEG_FILL, jnp.float32)
    start_sum = jnp.zeros((blocks_total, head_count, BLK), jnp.float32)
    (row_max, row_sum), _ = lax.scan(stat_step, (start_max, start_sum), jnp.arange(MAXK))

    def output_step(accum, slot):
        picked = adjacency[:, slot]
        score = pair_scores(query_blocks, key_heads[picked])
        usable = slot_live[:, slot][:, None, None, None]
        prob_half = jnp.where(
            usable, jnp.exp(score - row_max[..., None]) / row_sum[..., None], 0.0
        ).astype(jnp.bfloat16)
        accum = accum + jnp.einsum(
            "ihqk,ikhd->iqhd", prob_half, value_heads[picked], preferred_element_type=jnp.float32
        )
        return (accum, None)

    start_out = jnp.zeros(query_blocks.shape, jnp.float32)
    accum, _ = lax.scan(output_step, start_out, jnp.arange(MAXK))
    return (row_max, row_sum, accum.astype(jnp.bfloat16))


def head_backward(
    query_h, key_h, value_h, grad_h, row_max, row_sum, attn_blocks, adjacency, slot_live
):
    query_blocks = blocked(query_h)
    key_heads = blocked(key_h)
    value_heads = blocked(value_h)
    grad_blocks = blocked(grad_h)
    scale_factor = HD ** (-0.5)
    row_dot = jnp.sum(
        grad_blocks.astype(jnp.float32) * attn_blocks.astype(jnp.float32), axis=-1
    ).transpose(0, 2, 1)

    def grad_step(carried, slot):
        query_accum, key_accum, value_accum = carried
        picked = adjacency[:, slot]
        chosen_keys = key_heads[picked]
        chosen_values = value_heads[picked]
        score = pair_scores(query_blocks, chosen_keys)
        usable = slot_live[:, slot][:, None, None, None]
        prob_full = jnp.where(usable, jnp.exp(score - row_max[..., None]) / row_sum[..., None], 0.0)
        prob_half = prob_full.astype(jnp.bfloat16)
        prob_grad = jnp.einsum(
            "iqhd,ikhd->ihqk", grad_blocks, chosen_values, preferred_element_type=jnp.float32
        )
        score_grad = (prob_full * (prob_grad - row_dot[..., None])).astype(jnp.bfloat16)
        query_accum = (
            query_accum
            + jnp.einsum(
                "ihqk,ikhd->iqhd", score_grad, chosen_keys, preferred_element_type=jnp.float32
            )
            * scale_factor
        )
        key_terms = (
            jnp.einsum(
                "ihqk,iqhd->ikhd", score_grad, query_blocks, preferred_element_type=jnp.float32
            )
            * scale_factor
        )
        value_terms = jnp.einsum(
            "ihqk,iqhd->ikhd", prob_half, grad_blocks, preferred_element_type=jnp.float32
        )
        key_accum = key_accum.at[picked].add(key_terms)
        value_accum = value_accum.at[picked].add(value_terms)
        return ((query_accum, key_accum, value_accum), None)

    zeros_start = jnp.zeros(query_blocks.shape, jnp.float32)
    (query_accum, key_accum, value_accum), _ = lax.scan(
        grad_step, (zeros_start, zeros_start, zeros_start), jnp.arange(MAXK)
    )
    head_count = query_h.shape[1]
    return tuple(
        (
            accum.astype(jnp.bfloat16).reshape(-1, head_count, HD)
            for accum in (query_accum, key_accum, value_accum)
        )
    )


PAIR = 2 * HD
SCALE = HD ** (-0.5)
BASE2 = SCALE * math.log2(math.e)


def fold_rows(tile, combine):
    return combine(tile.reshape(-1, 8, tile.shape[1]), axis=0)


def block_rows(index, height=BLK):
    return pl.ds(pl.multiple_of(index * height, height), height)


def by_head(block):
    first = lax.broadcasted_iota(jnp.int32, block.shape, 1) < HD
    zero = jnp.zeros_like(block)
    return jnp.concatenate([jnp.where(first, block, zero), jnp.where(first, zero, block)], axis=0)


def by_head_t(block):
    turned = block.T
    first = lax.broadcasted_iota(jnp.int32, turned.shape, 0) < HD
    zero = jnp.zeros_like(turned)
    return jnp.concatenate([jnp.where(first, turned, zero), jnp.where(first, zero, turned)], axis=1)


def own_parts(wide):
    return jnp.concatenate([wide[:HD, :BLK], wide[HD:, BLK:]], axis=0)


def columns(pair, part):
    return pl.ds(PAIR * (3 * pair + part), PAIR)


def dot(left, right):
    return lax.dot_general(left, right, (((1,), (0,)), ((), ())), preferred_element_type=jnp.float32)


def stack(source, places, right):
    return dot(jnp.concatenate([source[at, :] for at in places], axis=0), right)


def each_block(counts, begin, end, body):
    @pl.loop(begin, end)
    def _(index):
        for slots in range(2, MAXK + 1):
            @pl.when(counts[index] == slots)
            def _():
                body(index, slots)


def forward_kernel(adjacency, counts, packed, *refs, begin, end):
    carried, (first, second, stats, value_t) = refs[:-4], refs[-4:]
    outs = (first, second)
    blocks = packed.shape[0] // BLK
    if begin:
        done = pl.ds(0, BLK * begin)
        first[done, :], second[done, :] = carried[0][done, :], carried[1][done, :]
        stats[:, : 8 * begin, :] = carried[2][:, : 8 * begin, :]

    @pl.loop(0, blocks)
    def _(index):
        for pair in range(2):
            value_t[pair, index] = packed[block_rows(index), columns(pair, 2)].T

    def query_block(index, slots):
        picked = [adjacency[index, slot] for slot in range(slots)]
        places = [block_rows(block) for block in picked]
        raws = [
            stack(
                packed.at[:, columns(pair, 1)],
                places,
                by_head_t(packed[block_rows(index), columns(pair, 0)]),
            )
            for pair in range(2)
        ]
        for pair, raw in enumerate(raws):
            row_max = jnp.max(fold_rows(raw, jnp.max), axis=0, keepdims=True)
            expo = jnp.exp2((raw - row_max) * BASE2)
            row_sum = jnp.sum(fold_rows(expo, jnp.sum), axis=0, keepdims=True)
            out_t = dot(
                jnp.concatenate([value_t[pair, block] for block in picked], axis=1),
                expo.astype(jnp.bfloat16),
            )
            outs[pair][block_rows(index), :] = own_parts(out_t / row_sum).T.astype(jnp.bfloat16)
            stats[pair, block_rows(index, 8), :] = jnp.broadcast_to(
                row_max * BASE2 + jnp.log2(row_sum), (8, 2 * BLK)
            )

    each_block(counts, begin, end, query_block)


def backward_kernel(
    adjacency, counts, packed, grad, attn_out, stats, *refs, blocks, begin, end
):
    query, key, value = (packed.at[:, pl.ds(PAIR * part, PAIR)] for part in range(3))
    carried, rest = refs[: 3 if begin else 0], refs[3 if begin else 0 :]
    outs, (key_t, key_sum, value_sum) = rest[:-3], rest[-3:]
    query_g = outs[0]

    @pl.loop(0, blocks)
    def _(index):
        key_t[index] = key[block_rows(index), :].T
        if begin:
            key_sum[block_rows(index), :] = carried[1][block_rows(index), :]
            value_sum[block_rows(index), :] = carried[2][block_rows(index), :]
        else:
            key_sum[block_rows(index), :] = jnp.zeros((BLK, PAIR), jnp.float32)
            value_sum[block_rows(index), :] = jnp.zeros((BLK, PAIR), jnp.float32)

    def query_block(index, slots):
        picked = [adjacency[index, slot] for slot in range(slots)]
        query_rows = query[block_rows(index), :]
        grad_rows = grad[block_rows(index), :]
        queries, queries_t = by_head(query_rows), by_head_t(query_rows)
        grads, grads_t = by_head(grad_rows), by_head_t(grad_rows)
        stat = stats[0, pl.ds(pl.multiple_of(index * 8, 8), 1), :]
        products = (
            grad_rows.astype(jnp.float32) * attn_out[block_rows(index), :].astype(jnp.float32)
        ).T
        row_dot = jnp.concatenate(
            [
                jnp.sum(products[:HD], axis=0, keepdims=True),
                jnp.sum(products[HD:], axis=0, keepdims=True),
            ],
            axis=1,
        )
        places = [block_rows(block) for block in picked]
        prob = jnp.exp2(stack(key, places, queries_t) * BASE2 - stat)
        term = (prob * (stack(value, places, grads_t) - row_dot)).astype(jnp.bfloat16)
        key_terms = dot(term, queries)
        value_terms = dot(prob.astype(jnp.bfloat16), grads)
        for number, at in enumerate(places):
            key_sum[at, :] += key_terms[BLK * number : BLK * (number + 1)]
            value_sum[at, :] += value_terms[BLK * number : BLK * (number + 1)]
        query_t = dot(jnp.concatenate([key_t[block] for block in picked], axis=1), term)
        query_g[block_rows(index), :PAIR] = (own_parts(query_t).T * SCALE).astype(jnp.bfloat16)

    each_block(counts, begin, end, query_block)
    if end < blocks:
        outs[1][...], outs[2][...] = key_sum[...], value_sum[...]
    else:
        if begin:
            query_g[: BLK * begin, :PAIR] = carried[0][: BLK * begin, :]
        query_g[:, PAIR : 2 * PAIR] = (key_sum[...] * SCALE).astype(jnp.bfloat16)
        query_g[:, 2 * PAIR :] = value_sum[...].astype(jnp.bfloat16)


VMEM = pl.BlockSpec(memory_space=pltpu.VMEM)
SMEM = pl.BlockSpec(memory_space=pltpu.SMEM)
PARAMS = pltpu.CompilerParams(vmem_limit_bytes=32 * 2**20)


def cost(tokens, products):
    tiles = tokens // BLK * MAXK * 2
    return pl.CostEstimate(
        flops=tiles * products * 2 * BLK * BLK * HD * 4,
        bytes_accessed=12 * tokens * PAIR,
        transcendentals=tiles * BLK * BLK,
    )


def forward(packed, adjacency, counts, begin, end, carried=()):
    tokens = packed.shape[0]
    blocks = tokens // BLK
    return pl.pallas_call(
        functools.partial(forward_kernel, begin=begin, end=end),
        in_specs=[SMEM, SMEM, VMEM] + [VMEM] * len(carried),
        out_specs=[VMEM] * 3,
        out_shape=[
            jax.ShapeDtypeStruct((tokens, PAIR), jnp.bfloat16),
            jax.ShapeDtypeStruct((tokens, PAIR), jnp.bfloat16),
            jax.ShapeDtypeStruct((2, blocks * 8, 2 * BLK), jnp.float32),
        ],
        scratch_shapes=[pltpu.VMEM((2, blocks, PAIR, BLK), jnp.bfloat16)],
        compiler_params=PARAMS,
        cost_estimate=cost(tokens * (end - begin) // blocks, 4),
        name="attend_forward",
    )(adjacency, counts, packed, *carried)


def backward(packed, grad, pair, attn_out, stats, adjacency, counts, begin=0, end=None, carried=()):
    tokens = packed.shape[0]
    blocks = tokens // BLK
    end = end or blocks
    one = pl.BlockSpec((tokens, PAIR), lambda step: (0, 0))
    three = pl.BlockSpec((tokens, 3 * PAIR), lambda step: (0, pair))
    whole = pl.BlockSpec((tokens, 3 * PAIR), lambda step: (0, 0))
    if end < blocks:
        out_specs = [one] * 3
        out_shape = [jax.ShapeDtypeStruct((tokens, PAIR), jnp.bfloat16)]
        out_shape += [jax.ShapeDtypeStruct((tokens, PAIR), jnp.float32)] * 2
    else:
        out_specs = whole
        out_shape = jax.ShapeDtypeStruct((tokens, 3 * PAIR), jnp.bfloat16)
    return pl.pallas_call(
        functools.partial(backward_kernel, blocks=blocks, begin=begin, end=end),
        grid=(1,),
        in_specs=[
            SMEM, SMEM, three, pl.BlockSpec((tokens, PAIR), lambda step: (0, pair)), one,
            pl.BlockSpec((1, blocks * 8, 2 * BLK), lambda step: (pair, 0, 0)),
        ] + [one] * len(carried),
        out_specs=out_specs,
        out_shape=out_shape,
        scratch_shapes=[
            pltpu.VMEM((blocks, PAIR, BLK), jnp.bfloat16),
            pltpu.VMEM((tokens, PAIR), jnp.float32),
            pltpu.VMEM((tokens, PAIR), jnp.float32),
        ],
        compiler_params=PARAMS,
        cost_estimate=cost(tokens * (end - begin) // blocks, 5),
        name="attend_backward",
    )(adjacency, counts, packed, grad, attn_out, stats, *carried)


SMALL = pltpu.CompilerParams(vmem_limit_bytes=16 * 2**20)
WIDE = pltpu.CompilerParams(vmem_limit_bytes=60 * 2**20)


STEPS = 4


def pack_kernel(queries, keys, values, out_grad, weight, packed, top, bottom, own):
    step = pl.program_id(0)
    for group in range(packed.shape[0]):
        for pair in range(2):
            start = PAIR * (2 * group + pair)
            for part, source in enumerate((queries, keys, values)):
                packed[group, :, columns(pair, part)] = source[:, start : start + PAIR]
    own[...] = weight[...]

    @pl.when(step < STEPS // 2)
    def _():
        top[...] = out_grad[...]

    @pl.when(step >= STEPS // 2)
    def _():
        bottom[...] = out_grad[...]


def pack(queries, keys, values, out_grad, out_weight, groups):
    tokens, width = queries.shape
    height, middle = tokens // STEPS, STEPS // 2
    share = width // groups // STEPS

    def weight_place(step):
        skipped = lax.axis_index("seq") * (width // groups) % out_weight.shape[0]
        return (skipped // share + step, 0)

    taken = pl.BlockSpec((height, width), lambda step: (step, 0))
    return pl.pallas_call(
        pack_kernel,
        grid=(STEPS,),
        in_specs=[taken] * 4 + [pl.BlockSpec((share, width), weight_place)],
        out_specs=[
            pl.BlockSpec((groups, height, 6 * PAIR), lambda step: (0, step, 0)),
            pl.BlockSpec((height, width), lambda step: (jnp.minimum(step, middle - 1), 0)),
            pl.BlockSpec((height, width), lambda step: (jnp.maximum(step - middle, 0), 0)),
            pl.BlockSpec((share, width), lambda step: (step, 0)),
        ],
        out_shape=[
            jax.ShapeDtypeStruct((groups, tokens, 6 * PAIR), queries.dtype),
            jax.ShapeDtypeStruct((tokens // 2, width), queries.dtype),
            jax.ShapeDtypeStruct((tokens // 2, width), queries.dtype),
            jax.ShapeDtypeStruct((width // groups, width), queries.dtype),
        ],
        compiler_params=WIDE,
        name="pack",
    )(queries, keys, values, out_grad, out_weight)


def unpack_kernel(first, second, query_g, key_g, value_g):
    for group in range(first.shape[0]):
        for pair, source in enumerate((first, second)):
            start = PAIR * (2 * group + pair)
            for part, out in enumerate((query_g, key_g, value_g)):
                out[:, start : start + PAIR] = source[group, :, PAIR * part : PAIR * (part + 1)]


def unpack(first, second):
    groups, tokens, _ = first.shape
    height = tokens // 4
    taken = pl.BlockSpec((groups, height, 3 * PAIR), lambda step: (0, step, 0))
    given = pl.BlockSpec((height, groups * 2 * PAIR), lambda step: (step, 0))
    return pl.pallas_call(
        unpack_kernel,
        grid=(4,),
        in_specs=[taken] * 2,
        out_specs=[given] * 3,
        out_shape=[jax.ShapeDtypeStruct((tokens, groups * 2 * PAIR), first.dtype)] * 3,
        compiler_params=SMALL,
        name="unpack",
    )(first, second)


def spread_kernel(*refs):
    pieces, out = refs[:-1], refs[-1]
    member = lax.axis_index("seq")
    for mask, piece in enumerate(pieces):
        width = piece.shape[1]
        start = pl.multiple_of((member ^ mask) * width, width)
        out[:, pl.ds(start, width)] = piece[...].astype(out.dtype)


def spread(pieces):
    rows, width = pieces[0].shape
    height = rows // STEPS
    return pl.pallas_call(
        spread_kernel,
        grid=(STEPS,),
        in_specs=[pl.BlockSpec((height, width), lambda step: (step, 0))] * len(pieces),
        out_specs=pl.BlockSpec((height, len(pieces) * width), lambda step: (step, 0)),
        out_shape=jax.ShapeDtypeStruct((rows, len(pieces) * width), jnp.float32),
        compiler_params=SMALL,
        name="spread",
    )(*pieces)


def exchange(chunks):
    return lax.all_to_all(chunks, "seq", split_axis=0, concat_axis=0, tiled=True)


WEIGHT_ROUTES = (
    ((0, 1), (1, 2), (2, 1), (3, 2)),
    ((0, 2), (1, 3), (2, 0), (3, 1)),
    ((2, 3), (1, 0), (2, 3), (1, 0)),
)


def send_weight(rows, step):
    planes, members = lax.axis_size("fsdp"), lax.axis_size("seq")
    routes = []
    for member in range(members):
        source, target = WEIGHT_ROUTES[step][member * planes // members]
        routes.append((source * members + member, target * members + member))
    return lax.ppermute(rows, ("fsdp", "seq"), routes)


def swap(array, mask):
    routes = [(s, s ^ mask) for s in range(lax.axis_size("seq"))]
    return lax.ppermute(array, "seq", routes)


def project_kernel(places, *refs):
    pieces, rest = refs[: len(places)], refs[len(places) :]
    weights, (first, second, attn_grad, terms) = rest[:4], rest[4:8]
    whole, weight, weight_t, landed, fetched = rest[8:]
    plane, member = lax.axis_index("fsdp"), lax.axis_index("seq")
    local = whole.shape[0] // terms.shape[0]
    copies = []
    for number, (mask, row) in enumerate(places):
        start = pl.multiple_of((member ^ mask) * local + row, BLK)
        target = whole.at[pl.ds(start, pieces[number].shape[0]), :]
        copies.append(pltpu.make_async_copy(pieces[number], target, landed.at[number]))
    for source, rows in enumerate(weights):
        held = (plane == member // 2) if source == 0 else False
        for home, (_, target) in enumerate(WEIGHT_ROUTES[source - 1] if source else ()):
            held = held | ((member // 2 == home) & (plane == target))

        @pl.when(held)
        def _():
            pltpu.make_async_copy(rows, weight, fetched).start()
    for copy in copies:
        copy.start()
    pltpu.make_async_copy(weights[0], weight, fetched).wait()
    weight_t[...] = weight[...].T
    attn_t = jnp.concatenate([first[...].T, second[...].T], axis=0)
    for copy in copies:
        copy.wait()
    groups, _, width = terms.shape
    for group in range(0, groups, 2):
        wide = dot(attn_t, whole[:, width * group : width * (group + 2)]).astype(terms.dtype)
        terms[group], terms[group + 1] = wide[:, :width], wide[:, width:]

    @pl.loop(0, 4)
    def _(part):
        rows = block_rows(part, whole.shape[0] // 4)
        attn_grad[rows, :] = dot(whole[rows, :], weight_t[...]).astype(attn_grad.dtype)


def project(pieces, weights, first, second, groups):
    places = [(mask, row) for mask, row, _ in pieces]
    arrays = [piece for _, _, piece in pieces]
    height, width = weights[0].shape
    tokens = first.shape[0]
    far = pl.BlockSpec(memory_space=pl.ANY)
    return pl.pallas_call(
        functools.partial(project_kernel, places),
        in_specs=[far] * (len(arrays) + len(weights)) + [VMEM] * 2,
        out_specs=[VMEM] * 2,
        out_shape=[
            jax.ShapeDtypeStruct((tokens, height), jnp.bfloat16),
            jax.ShapeDtypeStruct((groups, height, width // groups), jnp.bfloat16),
        ],
        scratch_shapes=[
            pltpu.VMEM((tokens, width), jnp.bfloat16),
            pltpu.VMEM((height, width), jnp.bfloat16),
            pltpu.VMEM((width, height), jnp.bfloat16),
            pltpu.SemaphoreType.DMA((len(arrays),)),
            pltpu.SemaphoreType.DMA,
        ],
        compiler_params=PARAMS,
        cost_estimate=pl.CostEstimate(
            flops=4 * tokens * width * height,
            bytes_accessed=2 * tokens * width + 8 * height * width,
            transcendentals=0,
        ),
        name="project",
    )(*arrays, *weights, first, second)


def split_kernel(whole, *parts):
    height = parts[0].shape[0]
    for offset, part in enumerate(parts):
        start = pl.multiple_of((lax.axis_index("fsdp") ^ offset) * height, height)
        part[...] = whole[pl.ds(start, height), :]


def split(whole, planes):
    rows, width = whole.shape
    return pl.pallas_call(
        split_kernel,
        in_specs=[VMEM],
        out_specs=[VMEM] * planes,
        out_shape=[jax.ShapeDtypeStruct((rows // planes, width), whole.dtype)] * planes,
        compiler_params=PARAMS,
        name="split",
    )(whole)


def fits_pairs(sizes):
    planes, members = sizes["fsdp"], sizes["seq"]
    return members == 8 and planes == 4 and members * 2 * PAIR == HEADS * HD


def pair_device(queries, keys, values, out_grad, out_weight, key_blocks, block_counts):
    planes, members = lax.axis_size("fsdp"), lax.axis_size("seq")
    home = lax.axis_index("seq") // 2
    local_tokens, model_width = queries.shape[1:]
    tokens = local_tokens * members
    adjacency, counts = key_blocks[0], block_counts[0]
    shard = out_grad[0]

    chunks, top, bottom, own = pack(queries[0], keys[0], values[0], shard, out_weight, members)
    packed = exchange(chunks).reshape(tokens, 6 * PAIR)
    near, far = send_weight(own, 0), send_weight(own, 1)
    beside = swap(shard, 1)
    packed, shard, top, bottom, near, beside = lax.optimization_barrier(
        (packed, shard, top, bottom, near, beside)
    )

    along = swap(top, 2), swap(bottom, 2)
    across = swap(top, 4), swap(bottom, 4)
    blocks = tokens // BLK
    done = forward(packed, adjacency, counts, 0, blocks // 2)
    done, far = lax.optimization_barrier((done, far))
    last = send_weight(jnp.where((home == 1) | (home == 2), own, far), 2)
    done = forward(packed, adjacency, counts, blocks // 2, blocks, done)
    (first, second, stats), along, across = lax.optimization_barrier((done, along, across))

    halves = list(zip((2, 2, 4, 4, 6, 6), (0, 1) * 3, (*along, *across, swap(along[0], 4), swap(across[1], 2))))
    pieces = [(0, 0, shard), (1, 0, beside)]
    for mask, half, piece in halves:
        row = half * local_tokens // 2
        pieces += [(mask, row, piece), (mask ^ 1, row, swap(piece, 1))]
    attn_grad, by_columns = project(pieces, (own, near, far, last), first, second, members)

    terms = exchange(by_columns).reshape(model_width, -1)
    first_g = backward(packed, attn_grad, 0, first, stats, adjacency, counts)
    first_g, terms = lax.optimization_barrier((first_g, terms))
    parts = split(terms, planes)
    received = [
        lax.ppermute(parts[offset], "fsdp", [(z, z ^ offset) for z in range(planes)])
        for offset in range(1, planes)
    ]
    first_r = exchange(first_g.reshape(members, local_tokens, 3 * PAIR))
    split_at = tokens // BLK // 2
    started = backward(
        packed, attn_grad, 1, second, stats, adjacency, counts, end=split_at
    )
    *started, received = lax.optimization_barrier((*started, received))
    summed = sum(part.astype(jnp.float32) for part in [parts[0], *received]).astype(terms.dtype)
    sides = [summed, swap(summed, 2), swap(summed, 4), swap(summed, 6)]
    second_g = backward(
        packed, attn_grad, 1, second, stats, adjacency, counts, begin=split_at, carried=started
    )
    second_g, *sides = lax.optimization_barrier((second_g, *sides))
    wo_grad = spread([part for one in sides for part in (one, swap(one, 1))])
    second_r = exchange(second_g.reshape(members, local_tokens, 3 * PAIR))
    query_g, key_g, value_g = unpack(first_r, second_r)
    return (query_g[None], key_g[None], value_g[None], wo_grad)


def general_device(queries, keys, values, out_grad, out_weight, key_blocks, block_counts):
    local_tokens = queries.shape[1]
    model_width = queries.shape[2]
    seq_devices = lax.axis_size("seq")
    loss_grad = out_grad[0]
    adjacency = key_blocks[0]
    slot_live = jnp.arange(MAXK)[None, :] < block_counts[0][:, None]

    def head_groups(array):
        return array[0].reshape(local_tokens, seq_devices, HEADS // seq_devices, HD)

    attn_grad = lax.dot_general(
        loss_grad,
        lax.all_gather(out_weight, "fsdp", axis=0, tiled=True),
        (((1,), (1,)), ((), ())),
        preferred_element_type=jnp.float32,
    ).astype(jnp.bfloat16)

    def attend(heads_in):
        query_h, key_h, value_h, grad_h = (member[:, 0] for member in heads_in)
        row_max, row_sum, attn_blocks = head_forward(query_h, key_h, value_h, adjacency, slot_live)
        query_g, key_g, value_g = head_backward(
            query_h, key_h, value_h, grad_h, row_max, row_sum, attn_blocks, adjacency, slot_live
        )
        return (query_g, key_g, value_g, attn_blocks.reshape(-1, query_h.shape[1], HD))

    query_g, key_g, value_g, attn_heads = attend(
        (
            lax.all_to_all(head_groups(queries), "seq", split_axis=1, concat_axis=0, tiled=True),
            lax.all_to_all(head_groups(keys), "seq", split_axis=1, concat_axis=0, tiled=True),
            lax.all_to_all(head_groups(values), "seq", split_axis=1, concat_axis=0, tiled=True),
            lax.all_to_all(
                head_groups(attn_grad[None]), "seq", split_axis=1, concat_axis=0, tiled=True
            ),
        )
    )
    query_t, key_t, value_t, attn_t = (
        lax.all_to_all(query_g, "seq", split_axis=0, concat_axis=1, tiled=True),
        lax.all_to_all(key_g, "seq", split_axis=0, concat_axis=1, tiled=True),
        lax.all_to_all(value_g, "seq", split_axis=0, concat_axis=1, tiled=True),
        lax.all_to_all(attn_heads, "seq", split_axis=0, concat_axis=1, tiled=True),
    )
    attn_out = attn_t.reshape(local_tokens, model_width)
    share = lax.psum_scatter(
        lax.dot_general(
            attn_out, loss_grad, (((0,), (0,)), ((), ())), preferred_element_type=jnp.float32
        ),
        ("fsdp", "seq"),
        scatter_dimension=0,
        tiled=True,
    )
    wo_grad = lax.all_gather(share.astype(jnp.bfloat16), "seq", axis=0, tiled=True).astype(
        share.dtype
    )

    def to_tokens(array):
        return array.reshape(1, local_tokens, model_width)

    return (to_tokens(query_t), to_tokens(key_t), to_tokens(value_t), wo_grad)


def on_device(mesh):
    return pair_device if fits_pairs(mesh.shape) else general_device


def solution(mesh):
    return jax.shard_map(
        on_device(mesh),
        mesh=mesh,
        in_specs=(
            P("fsdp", "seq", None),
            P("fsdp", "seq", None),
            P("fsdp", "seq", None),
            P("fsdp", "seq", None),
            P("fsdp", None),
            P("fsdp", None, None),
            P("fsdp", None),
        ),
        out_specs=(
            P("fsdp", "seq", None),
            P("fsdp", "seq", None),
            P("fsdp", "seq", None),
            P("fsdp", None),
        ),
        check_vma=False,
    )
```

```python
import functools
import math

import jax
import jax.numpy as jnp
from jax import lax
from jax.experimental import pallas as pl
from jax.experimental.pallas import tpu as pltpu
from jax.sharding import PartitionSpec as P

HEADS = 32
HD = 64
BLK = 128
MAXK = 10


NEG_FILL = -1e30


def pair_scores(query_blocks, chosen):
    return jnp.einsum(
        "iqhd,ikhd->ihqk", query_blocks, chosen, preferred_element_type=jnp.float32
    ) * HD ** (-0.5)


def blocked(array):
    return array.reshape(-1, BLK, array.shape[1], HD)


def head_forward(query_h, key_h, value_h, adjacency, slot_live):
    query_blocks = blocked(query_h)
    key_heads = blocked(key_h)
    value_heads = blocked(value_h)
    blocks_total = query_blocks.shape[0]
    head_count = query_blocks.shape[2]

    def stat_step(carried, slot):
        row_max, row_sum = carried
        score = pair_scores(query_blocks, key_heads[adjacency[:, slot]])
        usable = slot_live[:, slot][:, None, None, None]
        score = jnp.where(usable, score, NEG_FILL)
        new_max = jnp.maximum(row_max, jnp.max(score, axis=-1))
        expo = jnp.where(usable, jnp.exp(score - new_max[..., None]), 0.0)
        row_sum = row_sum * jnp.exp(row_max - new_max) + jnp.sum(expo, axis=-1)
        return ((new_max, row_sum), None)

    start_max = jnp.full((blocks_total, head_count, BLK), NEG_FILL, jnp.float32)
    start_sum = jnp.zeros((blocks_total, head_count, BLK), jnp.float32)
    (row_max, row_sum), _ = lax.scan(stat_step, (start_max, start_sum), jnp.arange(MAXK))

    def output_step(accum, slot):
        picked = adjacency[:, slot]
        score = pair_scores(query_blocks, key_heads[picked])
        usable = slot_live[:, slot][:, None, None, None]
        prob_half = jnp.where(
            usable, jnp.exp(score - row_max[..., None]) / row_sum[..., None], 0.0
        ).astype(jnp.bfloat16)
        accum = accum + jnp.einsum(
            "ihqk,ikhd->iqhd", prob_half, value_heads[picked], preferred_element_type=jnp.float32
        )
        return (accum, None)

    start_out = jnp.zeros(query_blocks.shape, jnp.float32)
    accum, _ = lax.scan(output_step, start_out, jnp.arange(MAXK))
    return (row_max, row_sum, accum.astype(jnp.bfloat16))


def head_backward(
    query_h, key_h, value_h, grad_h, row_max, row_sum, attn_blocks, adjacency, slot_live
):
    query_blocks = blocked(query_h)
    key_heads = blocked(key_h)
    value_heads = blocked(value_h)
    grad_blocks = blocked(grad_h)
    scale_factor = HD ** (-0.5)
    row_dot = jnp.sum(
        grad_blocks.astype(jnp.float32) * attn_blocks.astype(jnp.float32), axis=-1
    ).transpose(0, 2, 1)

    def grad_step(carried, slot):
        query_accum, key_accum, value_accum = carried
        picked = adjacency[:, slot]
        chosen_keys = key_heads[picked]
        chosen_values = value_heads[picked]
        score = pair_scores(query_blocks, chosen_keys)
        usable = slot_live[:, slot][:, None, None, None]
        prob_full = jnp.where(usable, jnp.exp(score - row_max[..., None]) / row_sum[..., None], 0.0)
        prob_half = prob_full.astype(jnp.bfloat16)
        prob_grad = jnp.einsum(
            "iqhd,ikhd->ihqk", grad_blocks, chosen_values, preferred_element_type=jnp.float32
        )
        score_grad = (prob_full * (prob_grad - row_dot[..., None])).astype(jnp.bfloat16)
        query_accum = (
            query_accum
            + jnp.einsum(
                "ihqk,ikhd->iqhd", score_grad, chosen_keys, preferred_element_type=jnp.float32
            )
            * scale_factor
        )
        key_terms = (
            jnp.einsum(
                "ihqk,iqhd->ikhd", score_grad, query_blocks, preferred_element_type=jnp.float32
            )
            * scale_factor
        )
        value_terms = jnp.einsum(
            "ihqk,iqhd->ikhd", prob_half, grad_blocks, preferred_element_type=jnp.float32
        )
        key_accum = key_accum.at[picked].add(key_terms)
        value_accum = value_accum.at[picked].add(value_terms)
        return ((query_accum, key_accum, value_accum), None)

    zeros_start = jnp.zeros(query_blocks.shape, jnp.float32)
    (query_accum, key_accum, value_accum), _ = lax.scan(
        grad_step, (zeros_start, zeros_start, zeros_start), jnp.arange(MAXK)
    )
    head_count = query_h.shape[1]
    return tuple(
        (
            accum.astype(jnp.bfloat16).reshape(-1, head_count, HD)
            for accum in (query_accum, key_accum, value_accum)
        )
    )


PAIR = 2 * HD
SCALE = HD ** (-0.5)
BASE2 = SCALE * math.log2(math.e)


def fold_rows(tile, combine):
    return combine(tile.reshape(-1, 8, tile.shape[1]), axis=0)


def block_rows(index, height=BLK):
    return pl.ds(pl.multiple_of(index * height, height), height)


def by_head(block):
    first = lax.broadcasted_iota(jnp.int32, block.shape, 1) < HD
    zero = jnp.zeros_like(block)
    return jnp.concatenate([jnp.where(first, block, zero), jnp.where(first, zero, block)], axis=0)


def by_head_t(block):
    turned = block.T
    first = lax.broadcasted_iota(jnp.int32, turned.shape, 0) < HD
    zero = jnp.zeros_like(turned)
    return jnp.concatenate([jnp.where(first, turned, zero), jnp.where(first, zero, turned)], axis=1)


def own_parts(wide):
    return jnp.concatenate([wide[:HD, :BLK], wide[HD:, BLK:]], axis=0)


def columns(pair, part):
    return pl.ds(PAIR * (3 * pair + part), PAIR)


def dot(left, right):
    return lax.dot_general(left, right, (((1,), (0,)), ((), ())), preferred_element_type=jnp.float32)


def stack(source, places, right):
    return dot(jnp.concatenate([source[at, :] for at in places], axis=0), right)


def each_block(counts, begin, end, step, body):
    @pl.loop(begin, end)
    def _(index):
        for slots in range(2, MAXK + 1, step):
            @pl.when((counts[index] + step - 1) // step * step == slots)
            def _():
                body(index, slots)


def forward_kernel(adjacency, counts, packed, *refs, begin, end):
    carried, (first, second, stats, value_t) = refs[:-4], refs[-4:]
    outs = (first, second)
    blocks = packed.shape[0] // BLK
    if begin:
        done = pl.ds(0, BLK * begin)
        first[done, :], second[done, :] = carried[0][done, :], carried[1][done, :]
        stats[:, : 8 * begin, :] = carried[2][:, : 8 * begin, :]

    @pl.loop(0, blocks)
    def _(index):
        for pair in range(2):
            value_t[pair, index] = packed[block_rows(index), columns(pair, 2)].T

    def query_block(index, slots):
        picked = [adjacency[index, slot] for slot in range(slots)]
        places = [block_rows(block) for block in picked]
        raws = []
        for pair in range(2):
            queries = by_head_t(packed[block_rows(index), columns(pair, 0)])
            raw = stack(packed.at[:, columns(pair, 1)], places, queries)
            unsure = jnp.where(slots - 1 < counts[index], raw[-BLK:], NEG_FILL)
            raws.append(jnp.concatenate([raw[:-BLK], unsure], axis=0))
        for pair, raw in enumerate(raws):
            row_max = jnp.max(fold_rows(raw, jnp.max), axis=0, keepdims=True)
            expo = jnp.exp2((raw - row_max) * BASE2)
            row_sum = jnp.sum(fold_rows(expo, jnp.sum), axis=0, keepdims=True)
            out_t = dot(
                jnp.concatenate([value_t[pair, block] for block in picked], axis=1),
                expo.astype(jnp.bfloat16),
            )
            outs[pair][block_rows(index), :] = own_parts(out_t / row_sum).T.astype(jnp.bfloat16)
            stats[pair, block_rows(index, 8), :] = jnp.broadcast_to(
                row_max * BASE2 + jnp.log2(row_sum), (8, 2 * BLK)
            )

    each_block(counts, begin, end, 2, query_block)


def backward_kernel(
    adjacency, counts, packed, grad, attn_out, stats, *refs, blocks, begin, end
):
    query, key, value = (packed.at[:, pl.ds(PAIR * part, PAIR)] for part in range(3))
    carried, rest = refs[: 3 if begin else 0], refs[3 if begin else 0 :]
    outs, (key_t, key_sum, value_sum) = rest[:-3], rest[-3:]
    query_g = outs[0]

    @pl.loop(0, blocks)
    def _(index):
        key_t[index] = key[block_rows(index), :].T
        if begin:
            key_sum[block_rows(index), :] = carried[1][block_rows(index), :]
            value_sum[block_rows(index), :] = carried[2][block_rows(index), :]
        else:
            key_sum[block_rows(index), :] = jnp.zeros((BLK, PAIR), jnp.float32)
            value_sum[block_rows(index), :] = jnp.zeros((BLK, PAIR), jnp.float32)

    def query_block(index, slots):
        picked = [adjacency[index, slot] for slot in range(slots)]
        query_rows = query[block_rows(index), :]
        grad_rows = grad[block_rows(index), :]
        queries, queries_t = by_head(query_rows), by_head_t(query_rows)
        grads, grads_t = by_head(grad_rows), by_head_t(grad_rows)
        stat = stats[0, pl.ds(pl.multiple_of(index * 8, 8), 1), :]
        products = (
            grad_rows.astype(jnp.float32) * attn_out[block_rows(index), :].astype(jnp.float32)
        ).T
        row_dot = jnp.concatenate(
            [
                jnp.sum(products[:HD], axis=0, keepdims=True),
                jnp.sum(products[HD:], axis=0, keepdims=True),
            ],
            axis=1,
        )
        places = [block_rows(block) for block in picked]
        prob = jnp.exp2(stack(key, places, queries_t) * BASE2 - stat)
        term = (prob * (stack(value, places, grads_t) - row_dot)).astype(jnp.bfloat16)
        key_terms = dot(term, queries)
        value_terms = dot(prob.astype(jnp.bfloat16), grads)
        for number, at in enumerate(places):
            key_sum[at, :] += key_terms[BLK * number : BLK * (number + 1)]
            value_sum[at, :] += value_terms[BLK * number : BLK * (number + 1)]
        query_t = dot(jnp.concatenate([key_t[block] for block in picked], axis=1), term)
        query_g[block_rows(index), :PAIR] = (own_parts(query_t).T * SCALE).astype(jnp.bfloat16)

    each_block(counts, begin, end, 1, query_block)
    if end < blocks:
        outs[1][...], outs[2][...] = key_sum[...], value_sum[...]
    else:
        if begin:
            query_g[: BLK * begin, :PAIR] = carried[0][: BLK * begin, :]
        query_g[:, PAIR : 2 * PAIR] = (key_sum[...] * SCALE).astype(jnp.bfloat16)
        query_g[:, 2 * PAIR :] = value_sum[...].astype(jnp.bfloat16)


VMEM = pl.BlockSpec(memory_space=pltpu.VMEM)
SMEM = pl.BlockSpec(memory_space=pltpu.SMEM)
SMALL = pltpu.CompilerParams(vmem_limit_bytes=16 * 2**20)
PARAMS = pltpu.CompilerParams(vmem_limit_bytes=32 * 2**20)
WIDE = pltpu.CompilerParams(vmem_limit_bytes=60 * 2**20)


def cost(tokens, products):
    tiles = tokens // BLK * MAXK * 2
    return pl.CostEstimate(
        flops=tiles * products * 2 * BLK * BLK * HD * 4,
        bytes_accessed=12 * tokens * PAIR,
        transcendentals=tiles * BLK * BLK,
    )


def forward(packed, adjacency, counts, begin, end, carried=()):
    tokens = packed.shape[0]
    blocks = tokens // BLK
    return pl.pallas_call(
        functools.partial(forward_kernel, begin=begin, end=end),
        in_specs=[SMEM, SMEM, VMEM] + [VMEM] * len(carried),
        out_specs=[VMEM] * 3,
        out_shape=[
            jax.ShapeDtypeStruct((tokens, PAIR), jnp.bfloat16),
            jax.ShapeDtypeStruct((tokens, PAIR), jnp.bfloat16),
            jax.ShapeDtypeStruct((2, blocks * 8, 2 * BLK), jnp.float32),
        ],
        scratch_shapes=[pltpu.VMEM((2, blocks, PAIR, BLK), jnp.bfloat16)],
        compiler_params=PARAMS,
        cost_estimate=cost(tokens * (end - begin) // blocks, 4),
        name="attend_forward",
    )(adjacency, counts, packed, *carried)


def backward(packed, grad, pair, attn_out, stats, adjacency, counts, begin=0, end=None, carried=()):
    tokens = packed.shape[0]
    blocks = tokens // BLK
    end = end or blocks
    one = pl.BlockSpec((tokens, PAIR), lambda step: (0, 0))
    three = pl.BlockSpec((tokens, 3 * PAIR), lambda step: (0, pair))
    whole = pl.BlockSpec((tokens, 3 * PAIR), lambda step: (0, 0))
    if end < blocks:
        out_specs = [one] * 3
        out_shape = [jax.ShapeDtypeStruct((tokens, PAIR), jnp.bfloat16)]
        out_shape += [jax.ShapeDtypeStruct((tokens, PAIR), jnp.float32)] * 2
    else:
        out_specs = whole
        out_shape = jax.ShapeDtypeStruct((tokens, 3 * PAIR), jnp.bfloat16)
    return pl.pallas_call(
        functools.partial(backward_kernel, blocks=blocks, begin=begin, end=end),
        grid=(1,),
        in_specs=[
            SMEM, SMEM, three, pl.BlockSpec((tokens, PAIR), lambda step: (0, pair)), one,
            pl.BlockSpec((1, blocks * 8, 2 * BLK), lambda step: (pair, 0, 0)),
        ] + [one] * len(carried),
        out_specs=out_specs,
        out_shape=out_shape,
        scratch_shapes=[
            pltpu.VMEM((blocks, PAIR, BLK), jnp.bfloat16),
            pltpu.VMEM((tokens, PAIR), jnp.float32),
            pltpu.VMEM((tokens, PAIR), jnp.float32),
        ],
        compiler_params=WIDE,
        cost_estimate=cost(tokens * (end - begin) // blocks, 5),
        name="attend_backward",
    )(adjacency, counts, packed, grad, attn_out, stats, *carried)


STEPS = 4


def pack_kernel(queries, keys, values, out_grad, weight, packed, top, bottom, own):
    step = pl.program_id(0)
    for group in range(packed.shape[0]):
        for pair in range(2):
            start = PAIR * (2 * group + pair)
            for part, source in enumerate((queries, keys, values)):
                packed[group, :, columns(pair, part)] = source[:, start : start + PAIR]
    own[...] = weight[...]

    @pl.when(step < STEPS // 2)
    def _():
        top[...] = out_grad[...]

    @pl.when(step >= STEPS // 2)
    def _():
        bottom[...] = out_grad[...]


def pack(queries, keys, values, out_grad, out_weight, groups):
    tokens, width = queries.shape
    height, middle = tokens // STEPS, STEPS // 2
    share = width // groups // STEPS

    def weight_place(step):
        skipped = lax.axis_index("seq") * (width // groups) % out_weight.shape[0]
        return (skipped // share + step, 0)

    taken = pl.BlockSpec((height, width), lambda step: (step, 0))
    return pl.pallas_call(
        pack_kernel,
        grid=(STEPS,),
        in_specs=[taken] * 4 + [pl.BlockSpec((share, width), weight_place)],
        out_specs=[
            pl.BlockSpec((groups, height, 6 * PAIR), lambda step: (0, step, 0)),
            pl.BlockSpec((height, width), lambda step: (jnp.minimum(step, middle - 1), 0)),
            pl.BlockSpec((height, width), lambda step: (jnp.maximum(step - middle, 0), 0)),
            pl.BlockSpec((share, width), lambda step: (step, 0)),
        ],
        out_shape=[
            jax.ShapeDtypeStruct((groups, tokens, 6 * PAIR), queries.dtype),
            jax.ShapeDtypeStruct((tokens // 2, width), queries.dtype),
            jax.ShapeDtypeStruct((tokens // 2, width), queries.dtype),
            jax.ShapeDtypeStruct((width // groups, width), queries.dtype),
        ],
        compiler_params=WIDE,
        name="pack",
    )(queries, keys, values, out_grad, out_weight)


def unpack_kernel(first, second, query_g, key_g, value_g):
    for group in range(first.shape[0]):
        for pair, source in enumerate((first, second)):
            start = PAIR * (2 * group + pair)
            for part, out in enumerate((query_g, key_g, value_g)):
                out[:, start : start + PAIR] = source[group, :, PAIR * part : PAIR * (part + 1)]


def unpack(first, second):
    groups, tokens, _ = first.shape
    height = tokens // 4
    taken = pl.BlockSpec((groups, height, 3 * PAIR), lambda step: (0, step, 0))
    given = pl.BlockSpec((height, groups * 2 * PAIR), lambda step: (step, 0))
    return pl.pallas_call(
        unpack_kernel,
        grid=(4,),
        in_specs=[taken] * 2,
        out_specs=[given] * 3,
        out_shape=[jax.ShapeDtypeStruct((tokens, groups * 2 * PAIR), first.dtype)] * 3,
        compiler_params=SMALL,
        name="unpack",
    )(first, second)


def spread_kernel(*refs):
    pieces, out = refs[:-1], refs[-1]
    member = lax.axis_index("seq")
    for mask, piece in enumerate(pieces):
        width = piece.shape[1]
        start = pl.multiple_of((member ^ mask) * width, width)
        out[:, pl.ds(start, width)] = piece[...].astype(out.dtype)


def spread(pieces):
    rows, width = pieces[0].shape
    height = rows // STEPS
    return pl.pallas_call(
        spread_kernel,
        grid=(STEPS,),
        in_specs=[pl.BlockSpec((height, width), lambda step: (step, 0))] * len(pieces),
        out_specs=pl.BlockSpec((height, len(pieces) * width), lambda step: (step, 0)),
        out_shape=jax.ShapeDtypeStruct((rows, len(pieces) * width), jnp.float32),
        compiler_params=WIDE,
        name="spread",
    )(*pieces)


def exchange(chunks):
    return lax.all_to_all(chunks, "seq", split_axis=0, concat_axis=0, tiled=True)


WEIGHT_ROUTES = (
    ((0, 1), (1, 2), (2, 1), (3, 2)),
    ((0, 2), (1, 3), (2, 0), (3, 1)),
    ((2, 3), (1, 0), (2, 3), (1, 0)),
)


def send_weight(rows, step):
    planes, members = lax.axis_size("fsdp"), lax.axis_size("seq")
    routes = []
    for member in range(members):
        source, target = WEIGHT_ROUTES[step][member * planes // members]
        routes.append((source * members + member, target * members + member))
    return lax.ppermute(rows, ("fsdp", "seq"), routes)


def swap(array, mask):
    routes = [(s, s ^ mask) for s in range(lax.axis_size("seq"))]
    return lax.ppermute(array, "seq", routes)


def project_kernel(places, *refs):
    pieces, rest = refs[: len(places)], refs[len(places) :]
    weights, (first, second, attn_grad, terms) = rest[:4], rest[4:8]
    whole, weight, weight_t, landed, fetched = rest[8:]
    plane, member = lax.axis_index("fsdp"), lax.axis_index("seq")
    local = whole.shape[0] // terms.shape[0]
    copies = []
    for number, (mask, row) in enumerate(places):
        start = pl.multiple_of((member ^ mask) * local + row, BLK)
        target = whole.at[pl.ds(start, pieces[number].shape[0]), :]
        copies.append(pltpu.make_async_copy(pieces[number], target, landed.at[number]))
    for source, rows in enumerate(weights):
        held = (plane == member // 2) if source == 0 else False
        for home, (_, target) in enumerate(WEIGHT_ROUTES[source - 1] if source else ()):
            held = held | ((member // 2 == home) & (plane == target))

        @pl.when(held)
        def _():
            pltpu.make_async_copy(rows, weight, fetched).start()
    for copy in copies:
        copy.start()
    pltpu.make_async_copy(weights[0], weight, fetched).wait()
    weight_t[...] = weight[...].T
    attn_t = jnp.concatenate([first[...].T, second[...].T], axis=0)
    for copy in copies:
        copy.wait()
    groups, _, width = terms.shape
    for group in range(0, groups, 2):
        wide = dot(attn_t, whole[:, width * group : width * (group + 2)]).astype(terms.dtype)
        terms[group], terms[group + 1] = wide[:, :width], wide[:, width:]

    @pl.loop(0, 4)
    def _(part):
        rows = block_rows(part, whole.shape[0] // 4)
        attn_grad[rows, :] = dot(whole[rows, :], weight_t[...]).astype(attn_grad.dtype)


def project(pieces, weights, first, second, groups):
    places = [(mask, row) for mask, row, _ in pieces]
    arrays = [piece for _, _, piece in pieces]
    height, width = weights[0].shape
    tokens = first.shape[0]
    far = pl.BlockSpec(memory_space=pl.ANY)
    return pl.pallas_call(
        functools.partial(project_kernel, places),
        in_specs=[far] * (len(arrays) + len(weights)) + [VMEM] * 2,
        out_specs=[VMEM] * 2,
        out_shape=[
            jax.ShapeDtypeStruct((tokens, height), jnp.bfloat16),
            jax.ShapeDtypeStruct((groups, height, width // groups), jnp.bfloat16),
        ],
        scratch_shapes=[
            pltpu.VMEM((tokens, width), jnp.bfloat16),
            pltpu.VMEM((height, width), jnp.bfloat16),
            pltpu.VMEM((width, height), jnp.bfloat16),
            pltpu.SemaphoreType.DMA((len(arrays),)),
            pltpu.SemaphoreType.DMA,
        ],
        compiler_params=PARAMS,
        cost_estimate=pl.CostEstimate(
            flops=4 * tokens * width * height,
            bytes_accessed=2 * tokens * width + 8 * height * width,
            transcendentals=0,
        ),
        name="project",
    )(*arrays, *weights, first, second)


def split_kernel(whole, *parts):
    height = parts[0].shape[0]
    for offset, part in enumerate(parts):
        start = pl.multiple_of((lax.axis_index("fsdp") ^ offset) * height, height)
        part[...] = whole[pl.ds(start, height), :]


def split(whole, planes):
    rows, width = whole.shape
    return pl.pallas_call(
        split_kernel,
        in_specs=[VMEM],
        out_specs=[VMEM] * planes,
        out_shape=[jax.ShapeDtypeStruct((rows // planes, width), whole.dtype)] * planes,
        compiler_params=PARAMS,
        name="split",
    )(whole)


def fits_pairs(sizes):
    planes, members = sizes["fsdp"], sizes["seq"]
    return members == 8 and planes == 4 and members * 2 * PAIR == HEADS * HD


def pair_device(queries, keys, values, out_grad, out_weight, key_blocks, block_counts):
    planes, members = lax.axis_size("fsdp"), lax.axis_size("seq")
    home = lax.axis_index("seq") // 2
    local_tokens, model_width = queries.shape[1:]
    tokens = local_tokens * members
    adjacency, counts = key_blocks[0], block_counts[0]
    shard = out_grad[0]

    chunks, top, bottom, own = pack(queries[0], keys[0], values[0], shard, out_weight, members)
    packed = exchange(chunks).reshape(tokens, 6 * PAIR)
    near, far = send_weight(own, 0), send_weight(own, 1)
    beside = swap(shard, 1)
    packed, shard, top, bottom, near, beside = lax.optimization_barrier(
        (packed, shard, top, bottom, near, beside)
    )

    along = swap(top, 2), swap(bottom, 2)
    across = swap(top, 4), swap(bottom, 4)
    blocks = tokens // BLK
    done = forward(packed, adjacency, counts, 0, blocks // 2)
    done, far = lax.optimization_barrier((done, far))
    last = send_weight(jnp.where((home == 1) | (home == 2), own, far), 2)
    done = forward(packed, adjacency, counts, blocks // 2, blocks, done)
    (first, second, stats), along, across = lax.optimization_barrier((done, along, across))

    halves = list(zip((2, 2, 4, 4, 6, 6), (0, 1) * 3, (*along, *across, swap(along[0], 4), swap(across[1], 2))))
    pieces = [(0, 0, shard), (1, 0, beside)]
    for mask, half, piece in halves:
        row = half * local_tokens // 2
        pieces += [(mask, row, piece), (mask ^ 1, row, swap(piece, 1))]
    attn_grad, by_columns = project(pieces, (own, near, far, last), first, second, members)

    terms = exchange(by_columns).reshape(model_width, -1)
    first_g = backward(packed, attn_grad, 0, first, stats, adjacency, counts)
    first_g, terms = lax.optimization_barrier((first_g, terms))
    parts = split(terms, planes)
    received = [
        lax.ppermute(parts[offset], "fsdp", [(z, z ^ offset) for z in range(planes)])
        for offset in range(1, planes)
    ]
    first_r = exchange(first_g.reshape(members, local_tokens, 3 * PAIR))
    split_at = tokens // BLK * 11 // 16
    started = backward(
        packed, attn_grad, 1, second, stats, adjacency, counts, end=split_at
    )
    *started, received = lax.optimization_barrier((*started, received))
    summed = sum(part.astype(jnp.float32) for part in [parts[0], *received]).astype(terms.dtype)
    sides = [summed, swap(summed, 2), swap(summed, 4), swap(summed, 6)]
    second_g = backward(
        packed, attn_grad, 1, second, stats, adjacency, counts, begin=split_at, carried=started
    )
    second_g, *sides = lax.optimization_barrier((second_g, *sides))
    wo_grad = spread([part for one in sides for part in (one, swap(one, 1))])
    second_r = exchange(second_g.reshape(members, local_tokens, 3 * PAIR))
    query_g, key_g, value_g = unpack(first_r, second_r)
    return (query_g[None], key_g[None], value_g[None], wo_grad)


def general_device(queries, keys, values, out_grad, out_weight, key_blocks, block_counts):
    local_tokens = queries.shape[1]
    model_width = queries.shape[2]
    seq_devices = lax.axis_size("seq")
    loss_grad = out_grad[0]
    adjacency = key_blocks[0]
    slot_live = jnp.arange(MAXK)[None, :] < block_counts[0][:, None]

    def head_groups(array):
        return array[0].reshape(local_tokens, seq_devices, HEADS // seq_devices, HD)

    attn_grad = lax.dot_general(
        loss_grad,
        lax.all_gather(out_weight, "fsdp", axis=0, tiled=True),
        (((1,), (1,)), ((), ())),
        preferred_element_type=jnp.float32,
    ).astype(jnp.bfloat16)

    def attend(heads_in):
        query_h, key_h, value_h, grad_h = (member[:, 0] for member in heads_in)
        row_max, row_sum, attn_blocks = head_forward(query_h, key_h, value_h, adjacency, slot_live)
        query_g, key_g, value_g = head_backward(
            query_h, key_h, value_h, grad_h, row_max, row_sum, attn_blocks, adjacency, slot_live
        )
        return (query_g, key_g, value_g, attn_blocks.reshape(-1, query_h.shape[1], HD))

    query_g, key_g, value_g, attn_heads = attend(
        (
            lax.all_to_all(head_groups(queries), "seq", split_axis=1, concat_axis=0, tiled=True),
            lax.all_to_all(head_groups(keys), "seq", split_axis=1, concat_axis=0, tiled=True),
            lax.all_to_all(head_groups(values), "seq", split_axis=1, concat_axis=0, tiled=True),
            lax.all_to_all(
                head_groups(attn_grad[None]), "seq", split_axis=1, concat_axis=0, tiled=True
            ),
        )
    )
    query_t, key_t, value_t, attn_t = (
        lax.all_to_all(query_g, "seq", split_axis=0, concat_axis=1, tiled=True),
        lax.all_to_all(key_g, "seq", split_axis=0, concat_axis=1, tiled=True),
        lax.all_to_all(value_g, "seq", split_axis=0, concat_axis=1, tiled=True),
        lax.all_to_all(attn_heads, "seq", split_axis=0, concat_axis=1, tiled=True),
    )
    attn_out = attn_t.reshape(local_tokens, model_width)
    share = lax.psum_scatter(
        lax.dot_general(
            attn_out, loss_grad, (((0,), (0,)), ((), ())), preferred_element_type=jnp.float32
        ),
        ("fsdp", "seq"),
        scatter_dimension=0,
        tiled=True,
    )
    wo_grad = lax.all_gather(share.astype(jnp.bfloat16), "seq", axis=0, tiled=True).astype(
        share.dtype
    )

    def to_tokens(array):
        return array.reshape(1, local_tokens, model_width)

    return (to_tokens(query_t), to_tokens(key_t), to_tokens(value_t), wo_grad)


def on_device(mesh):
    return pair_device if fits_pairs(mesh.shape) else general_device


def solution(mesh):
    return jax.shard_map(
        on_device(mesh),
        mesh=mesh,
        in_specs=(
            P("fsdp", "seq", None),
            P("fsdp", "seq", None),
            P("fsdp", "seq", None),
            P("fsdp", "seq", None),
            P("fsdp", None),
            P("fsdp", None, None),
            P("fsdp", None),
        ),
        out_specs=(
            P("fsdp", "seq", None),
            P("fsdp", "seq", None),
            P("fsdp", "seq", None),
            P("fsdp", None),
        ),
        check_vma=False,
    )
```

```python
import functools
import math

import jax
import jax.numpy as jnp
from jax import lax
from jax.experimental import pallas as pl
from jax.experimental.pallas import tpu as pltpu
from jax.sharding import PartitionSpec as P

HEADS = 32
HD = 64
BLK = 128
MAXK = 10


NEG_FILL = -1e30


def pair_scores(query_blocks, chosen):
    return jnp.einsum(
        "iqhd,ikhd->ihqk", query_blocks, chosen, preferred_element_type=jnp.float32
    ) * HD ** (-0.5)


def blocked(array):
    return array.reshape(-1, BLK, array.shape[1], HD)


def head_forward(query_h, key_h, value_h, adjacency, slot_live):
    query_blocks = blocked(query_h)
    key_heads = blocked(key_h)
    value_heads = blocked(value_h)
    blocks_total = query_blocks.shape[0]
    head_count = query_blocks.shape[2]

    def stat_step(carried, slot):
        row_max, row_sum = carried
        score = pair_scores(query_blocks, key_heads[adjacency[:, slot]])
        usable = slot_live[:, slot][:, None, None, None]
        score = jnp.where(usable, score, NEG_FILL)
        new_max = jnp.maximum(row_max, jnp.max(score, axis=-1))
        expo = jnp.where(usable, jnp.exp(score - new_max[..., None]), 0.0)
        row_sum = row_sum * jnp.exp(row_max - new_max) + jnp.sum(expo, axis=-1)
        return ((new_max, row_sum), None)

    start_max = jnp.full((blocks_total, head_count, BLK), NEG_FILL, jnp.float32)
    start_sum = jnp.zeros((blocks_total, head_count, BLK), jnp.float32)
    (row_max, row_sum), _ = lax.scan(stat_step, (start_max, start_sum), jnp.arange(MAXK))

    def output_step(accum, slot):
        picked = adjacency[:, slot]
        score = pair_scores(query_blocks, key_heads[picked])
        usable = slot_live[:, slot][:, None, None, None]
        prob_half = jnp.where(
            usable, jnp.exp(score - row_max[..., None]) / row_sum[..., None], 0.0
        ).astype(jnp.bfloat16)
        accum = accum + jnp.einsum(
            "ihqk,ikhd->iqhd", prob_half, value_heads[picked], preferred_element_type=jnp.float32
        )
        return (accum, None)

    start_out = jnp.zeros(query_blocks.shape, jnp.float32)
    accum, _ = lax.scan(output_step, start_out, jnp.arange(MAXK))
    return (row_max, row_sum, accum.astype(jnp.bfloat16))


def head_backward(
    query_h, key_h, value_h, grad_h, row_max, row_sum, attn_blocks, adjacency, slot_live
):
    query_blocks = blocked(query_h)
    key_heads = blocked(key_h)
    value_heads = blocked(value_h)
    grad_blocks = blocked(grad_h)
    scale_factor = HD ** (-0.5)
    row_dot = jnp.sum(
        grad_blocks.astype(jnp.float32) * attn_blocks.astype(jnp.float32), axis=-1
    ).transpose(0, 2, 1)

    def grad_step(carried, slot):
        query_accum, key_accum, value_accum = carried
        picked = adjacency[:, slot]
        chosen_keys = key_heads[picked]
        chosen_values = value_heads[picked]
        score = pair_scores(query_blocks, chosen_keys)
        usable = slot_live[:, slot][:, None, None, None]
        prob_full = jnp.where(usable, jnp.exp(score - row_max[..., None]) / row_sum[..., None], 0.0)
        prob_half = prob_full.astype(jnp.bfloat16)
        prob_grad = jnp.einsum(
            "iqhd,ikhd->ihqk", grad_blocks, chosen_values, preferred_element_type=jnp.float32
        )
        score_grad = (prob_full * (prob_grad - row_dot[..., None])).astype(jnp.bfloat16)
        query_accum = (
            query_accum
            + jnp.einsum(
                "ihqk,ikhd->iqhd", score_grad, chosen_keys, preferred_element_type=jnp.float32
            )
            * scale_factor
        )
        key_terms = (
            jnp.einsum(
                "ihqk,iqhd->ikhd", score_grad, query_blocks, preferred_element_type=jnp.float32
            )
            * scale_factor
        )
        value_terms = jnp.einsum(
            "ihqk,iqhd->ikhd", prob_half, grad_blocks, preferred_element_type=jnp.float32
        )
        key_accum = key_accum.at[picked].add(key_terms)
        value_accum = value_accum.at[picked].add(value_terms)
        return ((query_accum, key_accum, value_accum), None)

    zeros_start = jnp.zeros(query_blocks.shape, jnp.float32)
    (query_accum, key_accum, value_accum), _ = lax.scan(
        grad_step, (zeros_start, zeros_start, zeros_start), jnp.arange(MAXK)
    )
    head_count = query_h.shape[1]
    return tuple(
        (
            accum.astype(jnp.bfloat16).reshape(-1, head_count, HD)
            for accum in (query_accum, key_accum, value_accum)
        )
    )


PAIR = 2 * HD
SCALE = HD ** (-0.5)
BASE2 = SCALE * math.log2(math.e)


def fold_rows(tile, combine):
    return combine(tile.reshape(-1, 8, tile.shape[1]), axis=0)


def block_rows(index, height=BLK):
    return pl.ds(pl.multiple_of(index * height, height), height)


def by_head(block):
    first = lax.broadcasted_iota(jnp.int32, block.shape, 1) < HD
    zero = jnp.zeros_like(block)
    return jnp.concatenate([jnp.where(first, block, zero), jnp.where(first, zero, block)], axis=0)


def by_head_t(block):
    turned = block.T
    first = lax.broadcasted_iota(jnp.int32, turned.shape, 0) < HD
    zero = jnp.zeros_like(turned)
    return jnp.concatenate([jnp.where(first, turned, zero), jnp.where(first, zero, turned)], axis=1)


def own_parts(wide):
    return jnp.concatenate([wide[:HD, :BLK], wide[HD:, BLK:]], axis=0)


def columns(pair, part):
    return pl.ds(PAIR * (3 * pair + part), PAIR)


def dot(left, right):
    return lax.dot_general(left, right, (((1,), (0,)), ((), ())), preferred_element_type=jnp.float32)


def stack(source, places, right):
    return dot(jnp.concatenate([source[at, :] for at in places], axis=0), right)


def each_block(counts, begin, end, step, body):
    @pl.loop(begin, end)
    def _(index):
        for slots in range(2, MAXK + 1, step):
            @pl.when((counts[index] + step - 1) // step * step == slots)
            def _():
                body(index, slots)


def forward_kernel(adjacency, counts, packed, *refs, begin, end):
    carried, (first, second, stats, value_t, queries_t, turned) = refs[:-6], refs[-6:]
    outs = (first, second)
    blocks = packed.shape[0] // BLK
    if begin:
        done = pl.ds(0, BLK * begin)
        first[done, :], second[done, :] = carried[0][done, :], carried[1][done, :]
        stats[:, : 8 * begin, :] = carried[2][:, : 8 * begin, :]

    @pl.loop(0, blocks, unroll=4)
    def _(index):
        for pair in range(2):
            value_t[pair, index] = packed[block_rows(index), columns(pair, 2)].T

    @pl.loop(begin, end, unroll=4)
    def _(index):
        for pair in range(2):
            queries_t[pair, index - begin] = by_head_t(packed[block_rows(index), columns(pair, 0)])

    def query_block(index, slots):
        picked = [adjacency[index, slot] for slot in range(slots)]
        places = [block_rows(block) for block in picked]
        raws = []
        for pair in range(2):
            raw = stack(packed.at[:, columns(pair, 1)], places, queries_t[pair, index - begin])
            unsure = jnp.where(slots - 1 < counts[index], raw[-BLK:], NEG_FILL)
            raws.append(jnp.concatenate([raw[:-BLK], unsure], axis=0))
        for pair, raw in enumerate(raws):
            row_max = jnp.max(fold_rows(raw, jnp.max), axis=0, keepdims=True)
            expo = jnp.exp2((raw - row_max) * BASE2)
            row_sum = jnp.sum(fold_rows(expo, jnp.sum), axis=0, keepdims=True)
            out_t = dot(
                jnp.concatenate([value_t[pair, block] for block in picked], axis=1),
                expo.astype(jnp.bfloat16),
            )
            turned[pair, index - begin] = out_t / row_sum
            stats[pair, block_rows(index, 8), :] = jnp.broadcast_to(
                row_max * BASE2 + jnp.log2(row_sum), (8, 2 * BLK)
            )

    each_block(counts, begin, end, 2, query_block)

    @pl.loop(begin, end, unroll=4)
    def _(index):
        for pair in range(2):
            out_t = own_parts(turned[pair, index - begin])
            outs[pair][block_rows(index), :] = out_t.T.astype(jnp.bfloat16)


def backward_kernel(
    adjacency, counts, packed, grad, attn_out, stats, *refs, blocks, begin, end
):
    query, key, value = (packed.at[:, pl.ds(PAIR * part, PAIR)] for part in range(3))
    carried, rest = refs[: 3 if begin else 0], refs[3 if begin else 0 :]
    outs, (key_t, key_sum, value_sum, queries_t, grads_t, row_dot, turned) = rest[:-7], rest[-7:]
    query_g = outs[0]

    @pl.loop(0, blocks, unroll=4)
    def _(index):
        key_t[index] = key[block_rows(index), :].T
        if begin:
            key_sum[block_rows(index), :] = carried[1][block_rows(index), :]
            value_sum[block_rows(index), :] = carried[2][block_rows(index), :]
        else:
            key_sum[block_rows(index), :] = jnp.zeros((BLK, PAIR), jnp.float32)
            value_sum[block_rows(index), :] = jnp.zeros((BLK, PAIR), jnp.float32)

    @pl.loop(begin, end, unroll=(end - begin) % 4 == 0 and 4 or end - begin)
    def _(index):
        grad_rows = grad[block_rows(index), :]
        queries_t[index - begin] = by_head_t(query[block_rows(index), :])
        grads_t[index - begin] = by_head_t(grad_rows)
        products = (
            grad_rows.astype(jnp.float32) * attn_out[block_rows(index), :].astype(jnp.float32)
        ).T
        row_dot[block_rows(index - begin, 8), :] = jnp.broadcast_to(
            jnp.concatenate(
                [
                    jnp.sum(products[:HD], axis=0, keepdims=True),
                    jnp.sum(products[HD:], axis=0, keepdims=True),
                ],
                axis=1,
            ),
            (8, 2 * BLK),
        )

    def query_block(index, slots):
        picked = [adjacency[index, slot] for slot in range(slots)]
        places = [block_rows(block) for block in picked]
        queries, grads = by_head(query[block_rows(index), :]), by_head(grad[block_rows(index), :])
        stat = stats[0, pl.ds(pl.multiple_of(index * 8, 8), 1), :]
        prob = jnp.exp2(stack(key, places, queries_t[index - begin]) * BASE2 - stat)
        change = stack(value, places, grads_t[index - begin])
        change = change - row_dot[pl.ds(pl.multiple_of((index - begin) * 8, 8), 1), :]
        term = (prob * change).astype(jnp.bfloat16)
        key_terms = dot(term, queries)
        value_terms = dot(prob.astype(jnp.bfloat16), grads)
        for number, at in enumerate(places):
            key_sum[at, :] += key_terms[BLK * number : BLK * (number + 1)]
            value_sum[at, :] += value_terms[BLK * number : BLK * (number + 1)]
        turned[index - begin] = dot(jnp.concatenate([key_t[block] for block in picked], axis=1), term)

    each_block(counts, begin, end, 1, query_block)

    @pl.loop(begin, end, unroll=(end - begin) % 4 == 0 and 4 or end - begin)
    def _(index):
        query_g[block_rows(index), :PAIR] = (
            own_parts(turned[index - begin]).T * SCALE
        ).astype(jnp.bfloat16)

    if end < blocks:
        outs[1][...], outs[2][...] = key_sum[...], value_sum[...]
    else:
        if begin:
            query_g[: BLK * begin, :PAIR] = carried[0][: BLK * begin, :]
        query_g[:, PAIR : 2 * PAIR] = (key_sum[...] * SCALE).astype(jnp.bfloat16)
        query_g[:, 2 * PAIR :] = value_sum[...].astype(jnp.bfloat16)


VMEM = pl.BlockSpec(memory_space=pltpu.VMEM)
SMEM = pl.BlockSpec(memory_space=pltpu.SMEM)
SMALL = pltpu.CompilerParams(vmem_limit_bytes=16 * 2**20)
PARAMS = pltpu.CompilerParams(vmem_limit_bytes=32 * 2**20)
WIDE = pltpu.CompilerParams(vmem_limit_bytes=60 * 2**20)


def cost(tokens, products):
    tiles = tokens // BLK * MAXK * 2
    return pl.CostEstimate(
        flops=tiles * products * 2 * BLK * BLK * HD * 4,
        bytes_accessed=12 * tokens * PAIR,
        transcendentals=tiles * BLK * BLK,
    )


def forward(packed, adjacency, counts, begin, end, carried=()):
    tokens = packed.shape[0]
    blocks = tokens // BLK
    return pl.pallas_call(
        functools.partial(forward_kernel, begin=begin, end=end),
        in_specs=[SMEM, SMEM, VMEM] + [VMEM] * len(carried),
        out_specs=[VMEM] * 3,
        out_shape=[
            jax.ShapeDtypeStruct((tokens, PAIR), jnp.bfloat16),
            jax.ShapeDtypeStruct((tokens, PAIR), jnp.bfloat16),
            jax.ShapeDtypeStruct((2, blocks * 8, 2 * BLK), jnp.float32),
        ],
        scratch_shapes=[
            pltpu.VMEM((2, blocks, PAIR, BLK), jnp.bfloat16),
            pltpu.VMEM((2, end - begin, PAIR, 2 * BLK), jnp.bfloat16),
            pltpu.VMEM((2, end - begin, PAIR, 2 * BLK), jnp.float32),
        ],
        compiler_params=PARAMS,
        cost_estimate=cost(tokens * (end - begin) // blocks, 4),
        name="attend_forward",
    )(adjacency, counts, packed, *carried)


def backward(packed, grad, pair, attn_out, stats, adjacency, counts, begin=0, end=None, carried=()):
    tokens = packed.shape[0]
    blocks = tokens // BLK
    end = end or blocks
    one = pl.BlockSpec((tokens, PAIR), lambda step: (0, 0))
    three = pl.BlockSpec((tokens, 3 * PAIR), lambda step: (0, pair))
    whole = pl.BlockSpec((tokens, 3 * PAIR), lambda step: (0, 0))
    if end < blocks:
        out_specs = [one] * 3
        out_shape = [jax.ShapeDtypeStruct((tokens, PAIR), jnp.bfloat16)]
        out_shape += [jax.ShapeDtypeStruct((tokens, PAIR), jnp.float32)] * 2
    else:
        out_specs = whole
        out_shape = jax.ShapeDtypeStruct((tokens, 3 * PAIR), jnp.bfloat16)
    return pl.pallas_call(
        functools.partial(backward_kernel, blocks=blocks, begin=begin, end=end),
        grid=(1,),
        in_specs=[
            SMEM, SMEM, three, pl.BlockSpec((tokens, PAIR), lambda step: (0, pair)), one,
            pl.BlockSpec((1, blocks * 8, 2 * BLK), lambda step: (pair, 0, 0)),
        ] + [one] * len(carried),
        out_specs=out_specs,
        out_shape=out_shape,
        scratch_shapes=[
            pltpu.VMEM((blocks, PAIR, BLK), jnp.bfloat16),
            pltpu.VMEM((tokens, PAIR), jnp.float32),
            pltpu.VMEM((tokens, PAIR), jnp.float32),
            pltpu.VMEM((end - begin, PAIR, 2 * BLK), jnp.bfloat16),
            pltpu.VMEM((end - begin, PAIR, 2 * BLK), jnp.bfloat16),
            pltpu.VMEM(((end - begin) * 8, 2 * BLK), jnp.float32),
            pltpu.VMEM((end - begin, PAIR, 2 * BLK), jnp.float32),
        ],
        compiler_params=WIDE,
        cost_estimate=cost(tokens * (end - begin) // blocks, 5),
        name="attend_backward",
    )(adjacency, counts, packed, grad, attn_out, stats, *carried)


STEPS = 4


def pack_kernel(queries, keys, values, out_grad, weight, packed, top, bottom, own):
    step = pl.program_id(0)
    for group in range(packed.shape[0]):
        for pair in range(2):
            start = PAIR * (2 * group + pair)
            for part, source in enumerate((queries, keys, values)):
                packed[group, :, columns(pair, part)] = source[:, start : start + PAIR]
    own[...] = weight[...]

    @pl.when(step < STEPS // 2)
    def _():
        top[...] = out_grad[...]

    @pl.when(step >= STEPS // 2)
    def _():
        bottom[...] = out_grad[...]


def pack(queries, keys, values, out_grad, out_weight, groups):
    tokens, width = queries.shape
    height, middle = tokens // STEPS, STEPS // 2
    share = width // groups // STEPS

    def weight_place(step):
        skipped = lax.axis_index("seq") * (width // groups) % out_weight.shape[0]
        return (skipped // share + step, 0)

    taken = pl.BlockSpec((height, width), lambda step: (step, 0))
    return pl.pallas_call(
        pack_kernel,
        grid=(STEPS,),
        in_specs=[taken] * 4 + [pl.BlockSpec((share, width), weight_place)],
        out_specs=[
            pl.BlockSpec((groups, height, 6 * PAIR), lambda step: (0, step, 0)),
            pl.BlockSpec((height, width), lambda step: (jnp.minimum(step, middle - 1), 0)),
            pl.BlockSpec((height, width), lambda step: (jnp.maximum(step - middle, 0), 0)),
            pl.BlockSpec((share, width), lambda step: (step, 0)),
        ],
        out_shape=[
            jax.ShapeDtypeStruct((groups, tokens, 6 * PAIR), queries.dtype),
            jax.ShapeDtypeStruct((tokens // 2, width), queries.dtype),
            jax.ShapeDtypeStruct((tokens // 2, width), queries.dtype),
            jax.ShapeDtypeStruct((width // groups, width), queries.dtype),
        ],
        compiler_params=WIDE,
        name="pack",
    )(queries, keys, values, out_grad, out_weight)


def unpack_kernel(first, second, query_g, key_g, value_g):
    for group in range(first.shape[0]):
        for pair, source in enumerate((first, second)):
            start = PAIR * (2 * group + pair)
            for part, out in enumerate((query_g, key_g, value_g)):
                out[:, start : start + PAIR] = source[group, :, PAIR * part : PAIR * (part + 1)]


def unpack(first, second):
    groups, tokens, _ = first.shape
    height = tokens // 4
    taken = pl.BlockSpec((groups, height, 3 * PAIR), lambda step: (0, step, 0))
    given = pl.BlockSpec((height, groups * 2 * PAIR), lambda step: (step, 0))
    return pl.pallas_call(
        unpack_kernel,
        grid=(4,),
        in_specs=[taken] * 2,
        out_specs=[given] * 3,
        out_shape=[jax.ShapeDtypeStruct((tokens, groups * 2 * PAIR), first.dtype)] * 3,
        compiler_params=SMALL,
        name="unpack",
    )(first, second)


def spread_kernel(*refs):
    pieces, out = refs[:-1], refs[-1]
    member = lax.axis_index("seq")
    for mask, piece in enumerate(pieces):
        width = piece.shape[1]
        start = pl.multiple_of((member ^ mask) * width, width)
        out[:, pl.ds(start, width)] = piece[...].astype(out.dtype)


def spread(pieces):
    rows, width = pieces[0].shape
    height = rows // STEPS
    return pl.pallas_call(
        spread_kernel,
        grid=(STEPS,),
        in_specs=[pl.BlockSpec((height, width), lambda step: (step, 0))] * len(pieces),
        out_specs=pl.BlockSpec((height, len(pieces) * width), lambda step: (step, 0)),
        out_shape=jax.ShapeDtypeStruct((rows, len(pieces) * width), jnp.float32),
        compiler_params=WIDE,
        name="spread",
    )(*pieces)


def exchange(chunks):
    return lax.all_to_all(chunks, "seq", split_axis=0, concat_axis=0, tiled=True)


WEIGHT_ROUTES = (
    ((0, 1), (1, 2), (2, 1), (3, 2)),
    ((0, 2), (1, 3), (2, 0), (3, 1)),
    ((2, 3), (1, 0), (2, 3), (1, 0)),
)


def send_weight(rows, step):
    planes, members = lax.axis_size("fsdp"), lax.axis_size("seq")
    routes = []
    for member in range(members):
        source, target = WEIGHT_ROUTES[step][member * planes // members]
        routes.append((source * members + member, target * members + member))
    return lax.ppermute(rows, ("fsdp", "seq"), routes)


def swap(array, mask):
    routes = [(s, s ^ mask) for s in range(lax.axis_size("seq"))]
    return lax.ppermute(array, "seq", routes)


def project_kernel(places, *refs):
    pieces, rest = refs[: len(places)], refs[len(places) :]
    weights, (first, second, given, sent) = rest[:4], rest[4:8]
    whole, weight, weight_t, attn_grad, terms, landed, fetched, left, gone = rest[8:]
    plane, member = lax.axis_index("fsdp"), lax.axis_index("seq")
    local = whole.shape[0] // terms.shape[0]
    copies = []
    for number, (mask, row) in enumerate(places):
        start = pl.multiple_of((member ^ mask) * local + row, BLK)
        target = whole.at[pl.ds(start, pieces[number].shape[0]), :]
        copies.append(pltpu.make_async_copy(pieces[number], target, landed.at[number]))
    for source, rows in enumerate(weights):
        held = (plane == member // 2) if source == 0 else False
        for home, (_, target) in enumerate(WEIGHT_ROUTES[source - 1] if source else ()):
            held = held | ((member // 2 == home) & (plane == target))

        @pl.when(held)
        def _():
            pltpu.make_async_copy(rows, weight, fetched).start()
    for copy in copies:
        copy.start()
    pltpu.make_async_copy(weights[0], weight, fetched).wait()
    weight_t[...] = weight[...].T
    attn_t = jnp.concatenate([first[...].T, second[...].T], axis=0)
    for copy in copies:
        copy.wait()
    groups, _, width = terms.shape
    for group in range(0, groups, 2):
        wide = dot(attn_t, whole[:, width * group : width * (group + 2)]).astype(terms.dtype)
        terms[group], terms[group + 1] = wide[:, :width], wide[:, width:]

    leaving = pltpu.make_async_copy(terms, sent, left)
    leaving.start()

    @pl.loop(0, 4)
    def _(part):
        rows = block_rows(part, whole.shape[0] // 4)
        attn_grad[rows, :] = dot(whole[rows, :], weight_t[...]).astype(attn_grad.dtype)
        pltpu.make_async_copy(attn_grad.at[rows, :], given.at[rows, :], gone.at[part]).start()

    leaving.wait()
    for part in range(4):
        rows = block_rows(part, whole.shape[0] // 4)
        pltpu.make_async_copy(attn_grad.at[rows, :], given.at[rows, :], gone.at[part]).wait()


def project(pieces, weights, first, second, groups):
    places = [(mask, row) for mask, row, _ in pieces]
    arrays = [piece for _, _, piece in pieces]
    height, width = weights[0].shape
    tokens = first.shape[0]
    far = pl.BlockSpec(memory_space=pl.ANY)
    return pl.pallas_call(
        functools.partial(project_kernel, places),
        in_specs=[far] * (len(arrays) + len(weights)) + [VMEM] * 2,
        out_specs=[pl.BlockSpec(memory_space=pltpu.HBM)] * 2,
        out_shape=[
            jax.ShapeDtypeStruct((tokens, height), jnp.bfloat16),
            jax.ShapeDtypeStruct((groups, height, width // groups), jnp.bfloat16),
        ],
        scratch_shapes=[
            pltpu.VMEM((tokens, width), jnp.bfloat16),
            pltpu.VMEM((height, width), jnp.bfloat16),
            pltpu.VMEM((width, height), jnp.bfloat16),
            pltpu.VMEM((tokens, height), jnp.bfloat16),
            pltpu.VMEM((groups, height, width // groups), jnp.bfloat16),
            pltpu.SemaphoreType.DMA((len(arrays),)),
            pltpu.SemaphoreType.DMA,
            pltpu.SemaphoreType.DMA,
            pltpu.SemaphoreType.DMA((4,)),
        ],
        compiler_params=PARAMS,
        cost_estimate=pl.CostEstimate(
            flops=4 * tokens * width * height,
            bytes_accessed=2 * tokens * width + 8 * height * width,
            transcendentals=0,
        ),
        name="project",
    )(*arrays, *weights, first, second)


def split_kernel(whole, *parts):
    height = parts[0].shape[0]
    for offset, part in enumerate(parts):
        start = pl.multiple_of((lax.axis_index("fsdp") ^ offset) * height, height)
        part[...] = whole[pl.ds(start, height), :]


def split(whole, planes):
    rows, width = whole.shape
    return pl.pallas_call(
        split_kernel,
        in_specs=[VMEM],
        out_specs=[VMEM] * planes,
        out_shape=[jax.ShapeDtypeStruct((rows // planes, width), whole.dtype)] * planes,
        compiler_params=PARAMS,
        name="split",
    )(whole)


def fits_pairs(sizes):
    planes, members = sizes["fsdp"], sizes["seq"]
    return members == 8 and planes == 4 and members * 2 * PAIR == HEADS * HD


def pair_device(queries, keys, values, out_grad, out_weight, key_blocks, block_counts):
    planes, members = lax.axis_size("fsdp"), lax.axis_size("seq")
    home = lax.axis_index("seq") // 2
    local_tokens, model_width = queries.shape[1:]
    tokens = local_tokens * members
    adjacency, counts = key_blocks[0], block_counts[0]
    shard = out_grad[0]

    chunks, top, bottom, own = pack(queries[0], keys[0], values[0], shard, out_weight, members)
    packed = exchange(chunks).reshape(tokens, 6 * PAIR)
    near, far = send_weight(own, 0), send_weight(own, 1)
    beside = swap(shard, 1)
    packed, shard, top, bottom, near, beside = lax.optimization_barrier(
        (packed, shard, top, bottom, near, beside)
    )

    along = swap(top, 2), swap(bottom, 2)
    across = swap(top, 4), swap(bottom, 4)
    blocks = tokens // BLK
    done = forward(packed, adjacency, counts, 0, blocks // 2)
    done, far = lax.optimization_barrier((done, far))
    last = send_weight(jnp.where((home == 1) | (home == 2), own, far), 2)
    done = forward(packed, adjacency, counts, blocks // 2, blocks, done)
    (first, second, stats), along, across = lax.optimization_barrier((done, along, across))

    halves = list(zip((2, 2, 4, 4, 6, 6), (0, 1) * 3, (*along, *across, swap(along[0], 4), swap(across[1], 2))))
    pieces = [(0, 0, shard), (1, 0, beside)]
    for mask, half, piece in halves:
        row = half * local_tokens // 2
        pieces += [(mask, row, piece), (mask ^ 1, row, swap(piece, 1))]
    attn_grad, by_columns = project(pieces, (own, near, far, last), first, second, members)

    terms = exchange(by_columns).reshape(model_width, -1)
    first_g = backward(packed, attn_grad, 0, first, stats, adjacency, counts)
    first_g, terms = lax.optimization_barrier((first_g, terms))
    parts = split(terms, planes)
    received = [
        lax.ppermute(parts[offset], "fsdp", [(z, z ^ offset) for z in range(planes)])
        for offset in range(1, planes)
    ]
    first_r = exchange(first_g.reshape(members, local_tokens, 3 * PAIR))
    split_at = tokens // BLK * 12 // 16
    started = backward(
        packed, attn_grad, 1, second, stats, adjacency, counts, end=split_at
    )
    *started, received = lax.optimization_barrier((*started, received))
    summed = sum(part.astype(jnp.float32) for part in [parts[0], *received]).astype(terms.dtype)
    sides = [summed, swap(summed, 2), swap(summed, 4), swap(summed, 6)]
    second_g = backward(
        packed, attn_grad, 1, second, stats, adjacency, counts, begin=split_at, carried=started
    )
    second_g, *sides = lax.optimization_barrier((second_g, *sides))
    wo_grad = spread([part for one in sides for part in (one, swap(one, 1))])
    second_r = exchange(second_g.reshape(members, local_tokens, 3 * PAIR))
    query_g, key_g, value_g = unpack(first_r, second_r)
    return (query_g[None], key_g[None], value_g[None], wo_grad)


def general_device(queries, keys, values, out_grad, out_weight, key_blocks, block_counts):
    local_tokens = queries.shape[1]
    model_width = queries.shape[2]
    seq_devices = lax.axis_size("seq")
    loss_grad = out_grad[0]
    adjacency = key_blocks[0]
    slot_live = jnp.arange(MAXK)[None, :] < block_counts[0][:, None]

    def head_groups(array):
        return array[0].reshape(local_tokens, seq_devices, HEADS // seq_devices, HD)

    attn_grad = lax.dot_general(
        loss_grad,
        lax.all_gather(out_weight, "fsdp", axis=0, tiled=True),
        (((1,), (1,)), ((), ())),
        preferred_element_type=jnp.float32,
    ).astype(jnp.bfloat16)

    def attend(heads_in):
        query_h, key_h, value_h, grad_h = (member[:, 0] for member in heads_in)
        row_max, row_sum, attn_blocks = head_forward(query_h, key_h, value_h, adjacency, slot_live)
        query_g, key_g, value_g = head_backward(
            query_h, key_h, value_h, grad_h, row_max, row_sum, attn_blocks, adjacency, slot_live
        )
        return (query_g, key_g, value_g, attn_blocks.reshape(-1, query_h.shape[1], HD))

    query_g, key_g, value_g, attn_heads = attend(
        (
            lax.all_to_all(head_groups(queries), "seq", split_axis=1, concat_axis=0, tiled=True),
            lax.all_to_all(head_groups(keys), "seq", split_axis=1, concat_axis=0, tiled=True),
            lax.all_to_all(head_groups(values), "seq", split_axis=1, concat_axis=0, tiled=True),
            lax.all_to_all(
                head_groups(attn_grad[None]), "seq", split_axis=1, concat_axis=0, tiled=True
            ),
        )
    )
    query_t, key_t, value_t, attn_t = (
        lax.all_to_all(query_g, "seq", split_axis=0, concat_axis=1, tiled=True),
        lax.all_to_all(key_g, "seq", split_axis=0, concat_axis=1, tiled=True),
        lax.all_to_all(value_g, "seq", split_axis=0, concat_axis=1, tiled=True),
        lax.all_to_all(attn_heads, "seq", split_axis=0, concat_axis=1, tiled=True),
    )
    attn_out = attn_t.reshape(local_tokens, model_width)
    share = lax.psum_scatter(
        lax.dot_general(
            attn_out, loss_grad, (((0,), (0,)), ((), ())), preferred_element_type=jnp.float32
        ),
        ("fsdp", "seq"),
        scatter_dimension=0,
        tiled=True,
    )
    wo_grad = lax.all_gather(share.astype(jnp.bfloat16), "seq", axis=0, tiled=True).astype(
        share.dtype
    )

    def to_tokens(array):
        return array.reshape(1, local_tokens, model_width)

    return (to_tokens(query_t), to_tokens(key_t), to_tokens(value_t), wo_grad)


def on_device(mesh):
    return pair_device if fits_pairs(mesh.shape) else general_device


def solution(mesh):
    return jax.shard_map(
        on_device(mesh),
        mesh=mesh,
        in_specs=(
            P("fsdp", "seq", None),
            P("fsdp", "seq", None),
            P("fsdp", "seq", None),
            P("fsdp", "seq", None),
            P("fsdp", None),
            P("fsdp", None, None),
            P("fsdp", None),
        ),
        out_specs=(
            P("fsdp", "seq", None),
            P("fsdp", "seq", None),
            P("fsdp", "seq", None),
            P("fsdp", None),
        ),
        check_vma=False,
    )
```

```python
import functools
import math

import jax
import jax.numpy as jnp
from jax import lax
from jax.experimental import pallas as pl
from jax.experimental.pallas import tpu as pltpu
from jax.sharding import PartitionSpec as P

HEADS = 32
HD = 64
BLK = 128
MAXK = 10


NEG_FILL = -1e30


def pair_scores(query_blocks, chosen):
    return jnp.einsum(
        "iqhd,ikhd->ihqk", query_blocks, chosen, preferred_element_type=jnp.float32
    ) * HD ** (-0.5)


def blocked(array):
    return array.reshape(-1, BLK, array.shape[1], HD)


def head_forward(query_h, key_h, value_h, adjacency, slot_live):
    query_blocks = blocked(query_h)
    key_heads = blocked(key_h)
    value_heads = blocked(value_h)
    blocks_total = query_blocks.shape[0]
    head_count = query_blocks.shape[2]

    def stat_step(carried, slot):
        row_max, row_sum = carried
        score = pair_scores(query_blocks, key_heads[adjacency[:, slot]])
        usable = slot_live[:, slot][:, None, None, None]
        score = jnp.where(usable, score, NEG_FILL)
        new_max = jnp.maximum(row_max, jnp.max(score, axis=-1))
        expo = jnp.where(usable, jnp.exp(score - new_max[..., None]), 0.0)
        row_sum = row_sum * jnp.exp(row_max - new_max) + jnp.sum(expo, axis=-1)
        return ((new_max, row_sum), None)

    start_max = jnp.full((blocks_total, head_count, BLK), NEG_FILL, jnp.float32)
    start_sum = jnp.zeros((blocks_total, head_count, BLK), jnp.float32)
    (row_max, row_sum), _ = lax.scan(stat_step, (start_max, start_sum), jnp.arange(MAXK))

    def output_step(accum, slot):
        picked = adjacency[:, slot]
        score = pair_scores(query_blocks, key_heads[picked])
        usable = slot_live[:, slot][:, None, None, None]
        prob_half = jnp.where(
            usable, jnp.exp(score - row_max[..., None]) / row_sum[..., None], 0.0
        ).astype(jnp.bfloat16)
        accum = accum + jnp.einsum(
            "ihqk,ikhd->iqhd", prob_half, value_heads[picked], preferred_element_type=jnp.float32
        )
        return (accum, None)

    start_out = jnp.zeros(query_blocks.shape, jnp.float32)
    accum, _ = lax.scan(output_step, start_out, jnp.arange(MAXK))
    return (row_max, row_sum, accum.astype(jnp.bfloat16))


def head_backward(
    query_h, key_h, value_h, grad_h, row_max, row_sum, attn_blocks, adjacency, slot_live
):
    query_blocks = blocked(query_h)
    key_heads = blocked(key_h)
    value_heads = blocked(value_h)
    grad_blocks = blocked(grad_h)
    scale_factor = HD ** (-0.5)
    row_dot = jnp.sum(
        grad_blocks.astype(jnp.float32) * attn_blocks.astype(jnp.float32), axis=-1
    ).transpose(0, 2, 1)

    def grad_step(carried, slot):
        query_accum, key_accum, value_accum = carried
        picked = adjacency[:, slot]
        chosen_keys = key_heads[picked]
        chosen_values = value_heads[picked]
        score = pair_scores(query_blocks, chosen_keys)
        usable = slot_live[:, slot][:, None, None, None]
        prob_full = jnp.where(usable, jnp.exp(score - row_max[..., None]) / row_sum[..., None], 0.0)
        prob_half = prob_full.astype(jnp.bfloat16)
        prob_grad = jnp.einsum(
            "iqhd,ikhd->ihqk", grad_blocks, chosen_values, preferred_element_type=jnp.float32
        )
        score_grad = (prob_full * (prob_grad - row_dot[..., None])).astype(jnp.bfloat16)
        query_accum = (
            query_accum
            + jnp.einsum(
                "ihqk,ikhd->iqhd", score_grad, chosen_keys, preferred_element_type=jnp.float32
            )
            * scale_factor
        )
        key_terms = (
            jnp.einsum(
                "ihqk,iqhd->ikhd", score_grad, query_blocks, preferred_element_type=jnp.float32
            )
            * scale_factor
        )
        value_terms = jnp.einsum(
            "ihqk,iqhd->ikhd", prob_half, grad_blocks, preferred_element_type=jnp.float32
        )
        key_accum = key_accum.at[picked].add(key_terms)
        value_accum = value_accum.at[picked].add(value_terms)
        return ((query_accum, key_accum, value_accum), None)

    zeros_start = jnp.zeros(query_blocks.shape, jnp.float32)
    (query_accum, key_accum, value_accum), _ = lax.scan(
        grad_step, (zeros_start, zeros_start, zeros_start), jnp.arange(MAXK)
    )
    head_count = query_h.shape[1]
    return tuple(
        (
            accum.astype(jnp.bfloat16).reshape(-1, head_count, HD)
            for accum in (query_accum, key_accum, value_accum)
        )
    )


PAIR = 2 * HD
SCALE = HD ** (-0.5)
BASE2 = SCALE * math.log2(math.e)


def fold_rows(tile, combine):
    return combine(tile.reshape(-1, 8, tile.shape[1]), axis=0)


def block_rows(index, height=BLK):
    return pl.ds(pl.multiple_of(index * height, height), height)


def by_head(block):
    first = lax.broadcasted_iota(jnp.int32, block.shape, 1) < HD
    zero = jnp.zeros_like(block)
    return jnp.concatenate([jnp.where(first, block, zero), jnp.where(first, zero, block)], axis=0)


def by_head_t(block):
    turned = block.T
    first = lax.broadcasted_iota(jnp.int32, turned.shape, 0) < HD
    zero = jnp.zeros_like(turned)
    return jnp.concatenate([jnp.where(first, turned, zero), jnp.where(first, zero, turned)], axis=1)


def own_parts(wide):
    return jnp.concatenate([wide[:HD, :BLK], wide[HD:, BLK:]], axis=0)


def columns(pair, part):
    return pl.ds(PAIR * (3 * pair + part), PAIR)


def dot(left, right):
    return lax.dot_general(left, right, (((1,), (0,)), ((), ())), preferred_element_type=jnp.float32)


def stack(source, places, right):
    return dot(jnp.concatenate([source[at, :] for at in places], axis=0), right)


def each_block(counts, begin, end, step, body):
    @pl.loop(begin, end)
    def _(index):
        for slots in range(2, MAXK + 1, step):
            @pl.when((counts[index] + step - 1) // step * step == slots)
            def _():
                body(index, slots)


def forward_kernel(adjacency, counts, packed, *refs, begin, end):
    carried, (first, second, stats, value_t, queries_t, turned) = refs[:-6], refs[-6:]
    outs = (first, second)
    blocks = packed.shape[0] // BLK
    if begin:
        done = pl.ds(0, BLK * begin)
        first[done, :], second[done, :] = carried[0][done, :], carried[1][done, :]
        stats[:, : 8 * begin, :] = carried[2][:, : 8 * begin, :]

    @pl.loop(0, blocks, unroll=4)
    def _(index):
        for pair in range(2):
            value_t[pair, index] = packed[block_rows(index), columns(pair, 2)].T

    @pl.loop(begin, end, unroll=4)
    def _(index):
        for pair in range(2):
            queries_t[pair, index - begin] = by_head_t(packed[block_rows(index), columns(pair, 0)])

    def query_block(index, slots):
        picked = [adjacency[index, slot] for slot in range(slots)]
        places = [block_rows(block) for block in picked]
        raws = []
        for pair in range(2):
            raw = stack(packed.at[:, columns(pair, 1)], places, queries_t[pair, index - begin])
            unsure = jnp.where(slots - 1 < counts[index], raw[-BLK:], NEG_FILL)
            raws.append(jnp.concatenate([raw[:-BLK], unsure], axis=0))
        for pair, raw in enumerate(raws):
            row_max = jnp.max(fold_rows(raw, jnp.max), axis=0, keepdims=True)
            expo = jnp.exp2((raw - row_max) * BASE2)
            row_sum = jnp.sum(fold_rows(expo, jnp.sum), axis=0, keepdims=True)
            out_t = dot(
                jnp.concatenate([value_t[pair, block] for block in picked], axis=1),
                expo.astype(jnp.bfloat16),
            )
            turned[pair, index - begin] = out_t / row_sum
            stats[pair, block_rows(index, 8), :] = jnp.broadcast_to(
                row_max * BASE2 + jnp.log2(row_sum), (8, 2 * BLK)
            )

    each_block(counts, begin, end, 2, query_block)

    @pl.loop(begin, end, unroll=4)
    def _(index):
        for pair in range(2):
            out_t = own_parts(turned[pair, index - begin])
            outs[pair][block_rows(index), :] = out_t.T.astype(jnp.bfloat16)


def backward_kernel(
    adjacency, counts, packed, grad, attn_out, stats, *refs, blocks, begin, end
):
    query, key, value = (packed.at[:, pl.ds(PAIR * part, PAIR)] for part in range(3))
    carried, rest = refs[: 3 if begin else 0], refs[3 if begin else 0 :]
    outs, (key_t, key_sum, value_sum, queries_t, grads_t, row_dot, turned) = rest[:-7], rest[-7:]
    query_g = outs[0]

    @pl.loop(0, blocks, unroll=4)
    def _(index):
        key_t[index] = key[block_rows(index), :].T
        if begin:
            key_sum[block_rows(index), :] = carried[1][block_rows(index), :]
            value_sum[block_rows(index), :] = carried[2][block_rows(index), :]
        else:
            key_sum[block_rows(index), :] = jnp.zeros((BLK, PAIR), jnp.float32)
            value_sum[block_rows(index), :] = jnp.zeros((BLK, PAIR), jnp.float32)

    @pl.loop(begin, end, unroll=(end - begin) % 4 == 0 and 4 or end - begin)
    def _(index):
        grad_rows = grad[block_rows(index), :]
        queries_t[index - begin] = by_head_t(query[block_rows(index), :])
        grads_t[index - begin] = by_head_t(grad_rows)
        products = (
            grad_rows.astype(jnp.float32) * attn_out[block_rows(index), :].astype(jnp.float32)
        ).T
        row_dot[block_rows(index - begin, 8), :] = jnp.broadcast_to(
            jnp.concatenate(
                [
                    jnp.sum(products[:HD], axis=0, keepdims=True),
                    jnp.sum(products[HD:], axis=0, keepdims=True),
                ],
                axis=1,
            ),
            (8, 2 * BLK),
        )

    def query_block(index, slots):
        picked = [adjacency[index, slot] for slot in range(slots)]
        places = [block_rows(block) for block in picked]
        queries, grads = by_head(query[block_rows(index), :]), by_head(grad[block_rows(index), :])
        stat = stats[0, pl.ds(pl.multiple_of(index * 8, 8), 1), :]
        prob = jnp.exp2(stack(key, places, queries_t[index - begin]) * BASE2 - stat)
        change = stack(value, places, grads_t[index - begin])
        change = change - row_dot[pl.ds(pl.multiple_of((index - begin) * 8, 8), 1), :]
        term = (prob * change).astype(jnp.bfloat16)
        key_terms = dot(term, queries)
        value_terms = dot(prob.astype(jnp.bfloat16), grads)
        for number, at in enumerate(places):
            key_sum[at, :] += key_terms[BLK * number : BLK * (number + 1)]
            value_sum[at, :] += value_terms[BLK * number : BLK * (number + 1)]
        turned[index - begin] = dot(jnp.concatenate([key_t[block] for block in picked], axis=1), term)

    each_block(counts, begin, end, 1, query_block)

    @pl.loop(begin, end, unroll=(end - begin) % 4 == 0 and 4 or end - begin)
    def _(index):
        query_g[block_rows(index), :PAIR] = (
            own_parts(turned[index - begin]).T * SCALE
        ).astype(jnp.bfloat16)

    if end < blocks:
        outs[1][...], outs[2][...] = key_sum[...], value_sum[...]
    else:
        if begin:
            query_g[: BLK * begin, :PAIR] = carried[0][: BLK * begin, :]
        query_g[:, PAIR : 2 * PAIR] = (key_sum[...] * SCALE).astype(jnp.bfloat16)
        query_g[:, 2 * PAIR :] = value_sum[...].astype(jnp.bfloat16)


VMEM = pl.BlockSpec(memory_space=pltpu.VMEM)
SMEM = pl.BlockSpec(memory_space=pltpu.SMEM)
SMALL = pltpu.CompilerParams(vmem_limit_bytes=16 * 2**20)
PARAMS = pltpu.CompilerParams(vmem_limit_bytes=32 * 2**20)
WIDE = pltpu.CompilerParams(vmem_limit_bytes=60 * 2**20)


def cost(tokens, products):
    tiles = tokens // BLK * MAXK * 2
    return pl.CostEstimate(
        flops=tiles * products * 2 * BLK * BLK * HD * 4,
        bytes_accessed=12 * tokens * PAIR,
        transcendentals=tiles * BLK * BLK,
    )


def forward(packed, adjacency, counts, begin, end, carried=()):
    tokens = packed.shape[0]
    blocks = tokens // BLK
    return pl.pallas_call(
        functools.partial(forward_kernel, begin=begin, end=end),
        in_specs=[SMEM, SMEM, VMEM] + [VMEM] * len(carried),
        out_specs=[VMEM] * 3,
        out_shape=[
            jax.ShapeDtypeStruct((tokens, PAIR), jnp.bfloat16),
            jax.ShapeDtypeStruct((tokens, PAIR), jnp.bfloat16),
            jax.ShapeDtypeStruct((2, blocks * 8, 2 * BLK), jnp.float32),
        ],
        scratch_shapes=[
            pltpu.VMEM((2, blocks, PAIR, BLK), jnp.bfloat16),
            pltpu.VMEM((2, end - begin, PAIR, 2 * BLK), jnp.bfloat16),
            pltpu.VMEM((2, end - begin, PAIR, 2 * BLK), jnp.float32),
        ],
        compiler_params=PARAMS,
        cost_estimate=cost(tokens * (end - begin) // blocks, 4),
        name="attend_forward",
    )(adjacency, counts, packed, *carried)


def backward(packed, grad, pair, attn_out, stats, adjacency, counts, begin=0, end=None, carried=()):
    tokens = packed.shape[0]
    blocks = tokens // BLK
    end = end or blocks
    one = pl.BlockSpec((tokens, PAIR), lambda step: (0, 0))
    three = pl.BlockSpec((tokens, 3 * PAIR), lambda step: (0, pair))
    whole = pl.BlockSpec((tokens, 3 * PAIR), lambda step: (0, 0))
    if end < blocks:
        out_specs = [one] * 3
        out_shape = [jax.ShapeDtypeStruct((tokens, PAIR), jnp.bfloat16)]
        out_shape += [jax.ShapeDtypeStruct((tokens, PAIR), jnp.float32)] * 2
    else:
        out_specs = whole
        out_shape = jax.ShapeDtypeStruct((tokens, 3 * PAIR), jnp.bfloat16)
    return pl.pallas_call(
        functools.partial(backward_kernel, blocks=blocks, begin=begin, end=end),
        grid=(1,),
        in_specs=[
            SMEM, SMEM, three, pl.BlockSpec((tokens, PAIR), lambda step: (0, pair)), one,
            pl.BlockSpec((1, blocks * 8, 2 * BLK), lambda step: (pair, 0, 0)),
        ] + [one] * len(carried),
        out_specs=out_specs,
        out_shape=out_shape,
        scratch_shapes=[
            pltpu.VMEM((blocks, PAIR, BLK), jnp.bfloat16),
            pltpu.VMEM((tokens, PAIR), jnp.float32),
            pltpu.VMEM((tokens, PAIR), jnp.float32),
            pltpu.VMEM((end - begin, PAIR, 2 * BLK), jnp.bfloat16),
            pltpu.VMEM((end - begin, PAIR, 2 * BLK), jnp.bfloat16),
            pltpu.VMEM(((end - begin) * 8, 2 * BLK), jnp.float32),
            pltpu.VMEM((end - begin, PAIR, 2 * BLK), jnp.float32),
        ],
        compiler_params=WIDE,
        cost_estimate=cost(tokens * (end - begin) // blocks, 5),
        name="attend_backward",
    )(adjacency, counts, packed, grad, attn_out, stats, *carried)


STEPS = 2


def pack_kernel(queries, keys, values, out_grad, weight, packed, top, bottom, own):
    step = pl.program_id(0)
    for group in range(packed.shape[0]):
        for pair in range(2):
            start = PAIR * (2 * group + pair)
            for part, source in enumerate((queries, keys, values)):
                packed[group, :, columns(pair, part)] = source[:, start : start + PAIR]
    own[...] = weight[...]

    @pl.when(step < STEPS // 2)
    def _():
        top[...] = out_grad[...]

    @pl.when(step >= STEPS // 2)
    def _():
        bottom[...] = out_grad[...]


def pack(queries, keys, values, out_grad, out_weight, groups):
    tokens, width = queries.shape
    height, middle = tokens // STEPS, STEPS // 2
    share = width // groups // STEPS

    def weight_place(step):
        skipped = lax.axis_index("seq") * (width // groups) % out_weight.shape[0]
        return (skipped // share + step, 0)

    taken = pl.BlockSpec((height, width), lambda step: (step, 0))
    return pl.pallas_call(
        pack_kernel,
        grid=(STEPS,),
        in_specs=[taken] * 4 + [pl.BlockSpec((share, width), weight_place)],
        out_specs=[
            pl.BlockSpec((groups, height, 6 * PAIR), lambda step: (0, step, 0)),
            pl.BlockSpec((height, width), lambda step: (jnp.minimum(step, middle - 1), 0)),
            pl.BlockSpec((height, width), lambda step: (jnp.maximum(step - middle, 0), 0)),
            pl.BlockSpec((share, width), lambda step: (step, 0)),
        ],
        out_shape=[
            jax.ShapeDtypeStruct((groups, tokens, 6 * PAIR), queries.dtype),
            jax.ShapeDtypeStruct((tokens // 2, width), queries.dtype),
            jax.ShapeDtypeStruct((tokens // 2, width), queries.dtype),
            jax.ShapeDtypeStruct((width // groups, width), queries.dtype),
        ],
        compiler_params=WIDE,
        name="pack",
    )(queries, keys, values, out_grad, out_weight)


def unpack_kernel(first, second, query_g, key_g, value_g):
    for group in range(first.shape[0]):
        for pair, source in enumerate((first, second)):
            start = PAIR * (2 * group + pair)
            for part, out in enumerate((query_g, key_g, value_g)):
                out[:, start : start + PAIR] = source[group, :, PAIR * part : PAIR * (part + 1)]


def unpack(first, second):
    groups, tokens, _ = first.shape
    height = tokens // STEPS
    taken = pl.BlockSpec((groups, height, 3 * PAIR), lambda step: (0, step, 0))
    given = pl.BlockSpec((height, groups * 2 * PAIR), lambda step: (step, 0))
    return pl.pallas_call(
        unpack_kernel,
        grid=(STEPS,),
        in_specs=[taken] * 2,
        out_specs=[given] * 3,
        out_shape=[jax.ShapeDtypeStruct((tokens, groups * 2 * PAIR), first.dtype)] * 3,
        compiler_params=SMALL,
        name="unpack",
    )(first, second)


def spread_kernel(*refs):
    pieces, out = refs[:-1], refs[-1]
    member = lax.axis_index("seq")
    for mask, piece in enumerate(pieces):
        width = piece.shape[1]
        start = pl.multiple_of((member ^ mask) * width, width)
        out[:, pl.ds(start, width)] = piece[...].astype(out.dtype)


def spread(pieces):
    rows, width = pieces[0].shape
    height = rows // STEPS
    return pl.pallas_call(
        spread_kernel,
        grid=(STEPS,),
        in_specs=[pl.BlockSpec((height, width), lambda step: (step, 0))] * len(pieces),
        out_specs=pl.BlockSpec((height, len(pieces) * width), lambda step: (step, 0)),
        out_shape=jax.ShapeDtypeStruct((rows, len(pieces) * width), jnp.float32),
        compiler_params=WIDE,
        name="spread",
    )(*pieces)


def exchange(chunks):
    return lax.all_to_all(chunks, "seq", split_axis=0, concat_axis=0, tiled=True)


WEIGHT_ROUTES = (
    ((0, 1), (1, 2), (2, 1), (3, 2)),
    ((0, 2), (1, 3), (2, 0), (3, 1)),
    ((2, 3), (1, 0), (2, 3), (1, 0)),
)


def send_weight(rows, step):
    planes, members = lax.axis_size("fsdp"), lax.axis_size("seq")
    routes = []
    for member in range(members):
        source, target = WEIGHT_ROUTES[step][member * planes // members]
        routes.append((source * members + member, target * members + member))
    return lax.ppermute(rows, ("fsdp", "seq"), routes)


def swap(array, mask):
    routes = [(s, s ^ mask) for s in range(lax.axis_size("seq"))]
    return lax.ppermute(array, "seq", routes)


def project_kernel(places, *refs):
    pieces, rest = refs[: len(places)], refs[len(places) :]
    weights, (first, second, given, sent) = rest[:4], rest[4:8]
    whole, weight, weight_t, attn_grad, terms, landed, fetched, left, gone = rest[8:]
    plane, member = lax.axis_index("fsdp"), lax.axis_index("seq")
    local = whole.shape[0] // terms.shape[0]
    copies = []
    for number, (mask, row) in enumerate(places):
        start = pl.multiple_of((member ^ mask) * local + row, BLK)
        target = whole.at[pl.ds(start, pieces[number].shape[0]), :]
        copies.append(pltpu.make_async_copy(pieces[number], target, landed.at[number]))
    for source, rows in enumerate(weights):
        held = (plane == member // 2) if source == 0 else False
        for home, (_, target) in enumerate(WEIGHT_ROUTES[source - 1] if source else ()):
            held = held | ((member // 2 == home) & (plane == target))

        @pl.when(held)
        def _():
            pltpu.make_async_copy(rows, weight, fetched).start()
    for copy in copies:
        copy.start()
    pltpu.make_async_copy(weights[0], weight, fetched).wait()
    weight_t[...] = weight[...].T
    attn_t = jnp.concatenate([first[...].T, second[...].T], axis=0)
    for copy in copies:
        copy.wait()
    groups, _, width = terms.shape
    for group in range(0, groups, 2):
        wide = dot(attn_t, whole[:, width * group : width * (group + 2)]).astype(terms.dtype)
        terms[group], terms[group + 1] = wide[:, :width], wide[:, width:]

    leaving = pltpu.make_async_copy(terms, sent, left)
    leaving.start()

    @pl.loop(0, 4)
    def _(part):
        rows = block_rows(part, whole.shape[0] // 4)
        attn_grad[rows, :] = dot(whole[rows, :], weight_t[...]).astype(attn_grad.dtype)
        pltpu.make_async_copy(attn_grad.at[rows, :], given.at[rows, :], gone.at[part]).start()

    leaving.wait()
    for part in range(4):
        rows = block_rows(part, whole.shape[0] // 4)
        pltpu.make_async_copy(attn_grad.at[rows, :], given.at[rows, :], gone.at[part]).wait()


def project(pieces, weights, first, second, groups):
    places = [(mask, row) for mask, row, _ in pieces]
    arrays = [piece for _, _, piece in pieces]
    height, width = weights[0].shape
    tokens = first.shape[0]
    far = pl.BlockSpec(memory_space=pl.ANY)
    return pl.pallas_call(
        functools.partial(project_kernel, places),
        in_specs=[far] * (len(arrays) + len(weights)) + [VMEM] * 2,
        out_specs=[pl.BlockSpec(memory_space=pltpu.HBM)] * 2,
        out_shape=[
            jax.ShapeDtypeStruct((tokens, height), jnp.bfloat16),
            jax.ShapeDtypeStruct((groups, height, width // groups), jnp.bfloat16),
        ],
        scratch_shapes=[
            pltpu.VMEM((tokens, width), jnp.bfloat16),
            pltpu.VMEM((height, width), jnp.bfloat16),
            pltpu.VMEM((width, height), jnp.bfloat16),
            pltpu.VMEM((tokens, height), jnp.bfloat16),
            pltpu.VMEM((groups, height, width // groups), jnp.bfloat16),
            pltpu.SemaphoreType.DMA((len(arrays),)),
            pltpu.SemaphoreType.DMA,
            pltpu.SemaphoreType.DMA,
            pltpu.SemaphoreType.DMA((4,)),
        ],
        compiler_params=PARAMS,
        cost_estimate=pl.CostEstimate(
            flops=4 * tokens * width * height,
            bytes_accessed=2 * tokens * width + 8 * height * width,
            transcendentals=0,
        ),
        name="project",
    )(*arrays, *weights, first, second)


def split_kernel(whole, *parts):
    height = parts[0].shape[0]
    for offset, part in enumerate(parts):
        start = pl.multiple_of((lax.axis_index("fsdp") ^ offset) * height, height)
        part[...] = whole[pl.ds(start, height), :]


def split(whole, planes):
    rows, width = whole.shape
    return pl.pallas_call(
        split_kernel,
        in_specs=[VMEM],
        out_specs=[VMEM] * planes,
        out_shape=[jax.ShapeDtypeStruct((rows // planes, width), whole.dtype)] * planes,
        compiler_params=PARAMS,
        name="split",
    )(whole)


def fits_pairs(sizes):
    planes, members = sizes["fsdp"], sizes["seq"]
    return members == 8 and planes == 4 and members * 2 * PAIR == HEADS * HD


def pair_device(queries, keys, values, out_grad, out_weight, key_blocks, block_counts):
    planes, members = lax.axis_size("fsdp"), lax.axis_size("seq")
    home = lax.axis_index("seq") // 2
    local_tokens, model_width = queries.shape[1:]
    tokens = local_tokens * members
    adjacency, counts = key_blocks[0], block_counts[0]
    shard = out_grad[0]

    chunks, top, bottom, own = pack(queries[0], keys[0], values[0], shard, out_weight, members)
    packed = exchange(chunks).reshape(tokens, 6 * PAIR)
    near, far = send_weight(own, 0), send_weight(own, 1)
    beside = swap(shard, 1)
    packed, shard, top, bottom, near, beside = lax.optimization_barrier(
        (packed, shard, top, bottom, near, beside)
    )

    along = swap(top, 2), swap(bottom, 2)
    across = swap(top, 4), swap(bottom, 4)
    blocks = tokens // BLK
    done = forward(packed, adjacency, counts, 0, blocks // 2)
    done, far = lax.optimization_barrier((done, far))
    last = send_weight(jnp.where((home == 1) | (home == 2), own, far), 2)
    done = forward(packed, adjacency, counts, blocks // 2, blocks, done)
    (first, second, stats), along, across = lax.optimization_barrier((done, along, across))

    halves = list(zip((2, 2, 4, 4, 6, 6), (0, 1) * 3, (*along, *across, swap(along[0], 4), swap(across[1], 2))))
    pieces = [(0, 0, shard), (1, 0, beside)]
    for mask, half, piece in halves:
        row = half * local_tokens // 2
        pieces += [(mask, row, piece), (mask ^ 1, row, swap(piece, 1))]
    attn_grad, by_columns = project(pieces, (own, near, far, last), first, second, members)

    terms = exchange(by_columns).reshape(model_width, -1)
    first_g = backward(packed, attn_grad, 0, first, stats, adjacency, counts)
    first_g, terms = lax.optimization_barrier((first_g, terms))
    parts = split(terms, planes)
    received = [
        lax.ppermute(parts[offset], "fsdp", [(z, z ^ offset) for z in range(planes)])
        for offset in range(1, planes)
    ]
    first_r = exchange(first_g.reshape(members, local_tokens, 3 * PAIR))
    split_at = tokens // BLK * 12 // 16
    started = backward(
        packed, attn_grad, 1, second, stats, adjacency, counts, end=split_at
    )
    *started, received = lax.optimization_barrier((*started, received))
    summed = sum(part.astype(jnp.float32) for part in [parts[0], *received]).astype(terms.dtype)
    sides = [summed, swap(summed, 2), swap(summed, 4), swap(summed, 6)]
    second_g = backward(
        packed, attn_grad, 1, second, stats, adjacency, counts, begin=split_at, carried=started
    )
    second_g, *sides = lax.optimization_barrier((second_g, *sides))
    wo_grad = spread([part for one in sides for part in (one, swap(one, 1))])
    second_r = exchange(second_g.reshape(members, local_tokens, 3 * PAIR))
    query_g, key_g, value_g = unpack(first_r, second_r)
    return (query_g[None], key_g[None], value_g[None], wo_grad)


def general_device(queries, keys, values, out_grad, out_weight, key_blocks, block_counts):
    local_tokens = queries.shape[1]
    model_width = queries.shape[2]
    seq_devices = lax.axis_size("seq")
    loss_grad = out_grad[0]
    adjacency = key_blocks[0]
    slot_live = jnp.arange(MAXK)[None, :] < block_counts[0][:, None]

    def head_groups(array):
        return array[0].reshape(local_tokens, seq_devices, HEADS // seq_devices, HD)

    attn_grad = lax.dot_general(
        loss_grad,
        lax.all_gather(out_weight, "fsdp", axis=0, tiled=True),
        (((1,), (1,)), ((), ())),
        preferred_element_type=jnp.float32,
    ).astype(jnp.bfloat16)

    def attend(heads_in):
        query_h, key_h, value_h, grad_h = (member[:, 0] for member in heads_in)
        row_max, row_sum, attn_blocks = head_forward(query_h, key_h, value_h, adjacency, slot_live)
        query_g, key_g, value_g = head_backward(
            query_h, key_h, value_h, grad_h, row_max, row_sum, attn_blocks, adjacency, slot_live
        )
        return (query_g, key_g, value_g, attn_blocks.reshape(-1, query_h.shape[1], HD))

    query_g, key_g, value_g, attn_heads = attend(
        (
            lax.all_to_all(head_groups(queries), "seq", split_axis=1, concat_axis=0, tiled=True),
            lax.all_to_all(head_groups(keys), "seq", split_axis=1, concat_axis=0, tiled=True),
            lax.all_to_all(head_groups(values), "seq", split_axis=1, concat_axis=0, tiled=True),
            lax.all_to_all(
                head_groups(attn_grad[None]), "seq", split_axis=1, concat_axis=0, tiled=True
            ),
        )
    )
    query_t, key_t, value_t, attn_t = (
        lax.all_to_all(query_g, "seq", split_axis=0, concat_axis=1, tiled=True),
        lax.all_to_all(key_g, "seq", split_axis=0, concat_axis=1, tiled=True),
        lax.all_to_all(value_g, "seq", split_axis=0, concat_axis=1, tiled=True),
        lax.all_to_all(attn_heads, "seq", split_axis=0, concat_axis=1, tiled=True),
    )
    attn_out = attn_t.reshape(local_tokens, model_width)
    share = lax.psum_scatter(
        lax.dot_general(
            attn_out, loss_grad, (((0,), (0,)), ((), ())), preferred_element_type=jnp.float32
        ),
        ("fsdp", "seq"),
        scatter_dimension=0,
        tiled=True,
    )
    wo_grad = lax.all_gather(share.astype(jnp.bfloat16), "seq", axis=0, tiled=True).astype(
        share.dtype
    )

    def to_tokens(array):
        return array.reshape(1, local_tokens, model_width)

    return (to_tokens(query_t), to_tokens(key_t), to_tokens(value_t), wo_grad)


def on_device(mesh):
    return pair_device if fits_pairs(mesh.shape) else general_device


def solution(mesh):
    return jax.shard_map(
        on_device(mesh),
        mesh=mesh,
        in_specs=(
            P("fsdp", "seq", None),
            P("fsdp", "seq", None),
            P("fsdp", "seq", None),
            P("fsdp", "seq", None),
            P("fsdp", None),
            P("fsdp", None, None),
            P("fsdp", None),
        ),
        out_specs=(
            P("fsdp", "seq", None),
            P("fsdp", "seq", None),
            P("fsdp", "seq", None),
            P("fsdp", None),
        ),
        check_vma=False,
    )
```

```python
import functools
import math

import jax
import jax.numpy as jnp
from jax import lax
from jax.experimental import pallas as pl
from jax.experimental.pallas import tpu as pltpu
from jax.sharding import PartitionSpec as P

HEADS = 32
HD = 64
BLK = 128
MAXK = 10


NEG_FILL = -1e30


def pair_scores(query_blocks, chosen):
    return jnp.einsum(
        "iqhd,ikhd->ihqk", query_blocks, chosen, preferred_element_type=jnp.float32
    ) * HD ** (-0.5)


def blocked(array):
    return array.reshape(-1, BLK, array.shape[1], HD)


def head_forward(query_h, key_h, value_h, adjacency, slot_live):
    query_blocks = blocked(query_h)
    key_heads = blocked(key_h)
    value_heads = blocked(value_h)
    blocks_total = query_blocks.shape[0]
    head_count = query_blocks.shape[2]

    def stat_step(carried, slot):
        row_max, row_sum = carried
        score = pair_scores(query_blocks, key_heads[adjacency[:, slot]])
        usable = slot_live[:, slot][:, None, None, None]
        score = jnp.where(usable, score, NEG_FILL)
        new_max = jnp.maximum(row_max, jnp.max(score, axis=-1))
        expo = jnp.where(usable, jnp.exp(score - new_max[..., None]), 0.0)
        row_sum = row_sum * jnp.exp(row_max - new_max) + jnp.sum(expo, axis=-1)
        return ((new_max, row_sum), None)

    start_max = jnp.full((blocks_total, head_count, BLK), NEG_FILL, jnp.float32)
    start_sum = jnp.zeros((blocks_total, head_count, BLK), jnp.float32)
    (row_max, row_sum), _ = lax.scan(stat_step, (start_max, start_sum), jnp.arange(MAXK))

    def output_step(accum, slot):
        picked = adjacency[:, slot]
        score = pair_scores(query_blocks, key_heads[picked])
        usable = slot_live[:, slot][:, None, None, None]
        prob_half = jnp.where(
            usable, jnp.exp(score - row_max[..., None]) / row_sum[..., None], 0.0
        ).astype(jnp.bfloat16)
        accum = accum + jnp.einsum(
            "ihqk,ikhd->iqhd", prob_half, value_heads[picked], preferred_element_type=jnp.float32
        )
        return (accum, None)

    start_out = jnp.zeros(query_blocks.shape, jnp.float32)
    accum, _ = lax.scan(output_step, start_out, jnp.arange(MAXK))
    return (row_max, row_sum, accum.astype(jnp.bfloat16))


def head_backward(
    query_h, key_h, value_h, grad_h, row_max, row_sum, attn_blocks, adjacency, slot_live
):
    query_blocks = blocked(query_h)
    key_heads = blocked(key_h)
    value_heads = blocked(value_h)
    grad_blocks = blocked(grad_h)
    scale_factor = HD ** (-0.5)
    row_dot = jnp.sum(
        grad_blocks.astype(jnp.float32) * attn_blocks.astype(jnp.float32), axis=-1
    ).transpose(0, 2, 1)

    def grad_step(carried, slot):
        query_accum, key_accum, value_accum = carried
        picked = adjacency[:, slot]
        chosen_keys = key_heads[picked]
        chosen_values = value_heads[picked]
        score = pair_scores(query_blocks, chosen_keys)
        usable = slot_live[:, slot][:, None, None, None]
        prob_full = jnp.where(usable, jnp.exp(score - row_max[..., None]) / row_sum[..., None], 0.0)
        prob_half = prob_full.astype(jnp.bfloat16)
        prob_grad = jnp.einsum(
            "iqhd,ikhd->ihqk", grad_blocks, chosen_values, preferred_element_type=jnp.float32
        )
        score_grad = (prob_full * (prob_grad - row_dot[..., None])).astype(jnp.bfloat16)
        query_accum = (
            query_accum
            + jnp.einsum(
                "ihqk,ikhd->iqhd", score_grad, chosen_keys, preferred_element_type=jnp.float32
            )
            * scale_factor
        )
        key_terms = (
            jnp.einsum(
                "ihqk,iqhd->ikhd", score_grad, query_blocks, preferred_element_type=jnp.float32
            )
            * scale_factor
        )
        value_terms = jnp.einsum(
            "ihqk,iqhd->ikhd", prob_half, grad_blocks, preferred_element_type=jnp.float32
        )
        key_accum = key_accum.at[picked].add(key_terms)
        value_accum = value_accum.at[picked].add(value_terms)
        return ((query_accum, key_accum, value_accum), None)

    zeros_start = jnp.zeros(query_blocks.shape, jnp.float32)
    (query_accum, key_accum, value_accum), _ = lax.scan(
        grad_step, (zeros_start, zeros_start, zeros_start), jnp.arange(MAXK)
    )
    head_count = query_h.shape[1]
    return tuple(
        (
            accum.astype(jnp.bfloat16).reshape(-1, head_count, HD)
            for accum in (query_accum, key_accum, value_accum)
        )
    )


PAIR = 2 * HD
SCALE = HD ** (-0.5)
BASE2 = SCALE * math.log2(math.e)


def fold_rows(tile, combine):
    return combine(tile.reshape(-1, 8, tile.shape[1]), axis=0)


def block_rows(index, height=BLK):
    return pl.ds(pl.multiple_of(index * height, height), height)


def by_head(block):
    first = lax.broadcasted_iota(jnp.int32, block.shape, 1) < HD
    zero = jnp.zeros_like(block)
    return jnp.concatenate([jnp.where(first, block, zero), jnp.where(first, zero, block)], axis=0)


def by_head_t(block):
    turned = block.T
    first = lax.broadcasted_iota(jnp.int32, turned.shape, 0) < HD
    zero = jnp.zeros_like(turned)
    return jnp.concatenate([jnp.where(first, turned, zero), jnp.where(first, zero, turned)], axis=1)


def own_parts(wide):
    return jnp.concatenate([wide[:HD, :BLK], wide[HD:, BLK:]], axis=0)


def columns(pair, part):
    return pl.ds(PAIR * (3 * pair + part), PAIR)


def dot(left, right):
    return lax.dot_general(left, right, (((1,), (0,)), ((), ())), preferred_element_type=jnp.float32)


def stack(source, places, right):
    return dot(jnp.concatenate([source[at, :] for at in places], axis=0), right)


def each_block(counts, begin, end, step, body):
    @pl.loop(begin, end)
    def _(index):
        for slots in range(2, MAXK + 1, step):
            @pl.when((counts[index] + step - 1) // step * step == slots)
            def _():
                body(index, slots)


def forward_kernel(adjacency, counts, packed, *refs, begin, end):
    carried, (first, second, stats, value_t, queries_t, turned) = refs[:-6], refs[-6:]
    outs = (first, second)
    blocks = packed.shape[0] // BLK
    if begin:
        done = pl.ds(0, BLK * begin)
        first[done, :], second[done, :] = carried[0][done, :], carried[1][done, :]
        stats[:, : 8 * begin, :] = carried[2][:, : 8 * begin, :]

    @pl.loop(0, blocks, unroll=4)
    def _(index):
        for pair in range(2):
            value_t[pair, index] = packed[block_rows(index), columns(pair, 2)].T

    @pl.loop(begin, end, unroll=4)
    def _(index):
        for pair in range(2):
            queries_t[pair, index - begin] = by_head_t(packed[block_rows(index), columns(pair, 0)])

    def query_block(index, slots):
        picked = [adjacency[index, slot] for slot in range(slots)]
        places = [block_rows(block) for block in picked]
        raws = []
        for pair in range(2):
            raw = stack(packed.at[:, columns(pair, 1)], places, queries_t[pair, index - begin])
            unsure = jnp.where(slots - 1 < counts[index], raw[-BLK:], NEG_FILL)
            raws.append(jnp.concatenate([raw[:-BLK], unsure], axis=0))
        for pair, raw in enumerate(raws):
            row_max = jnp.max(fold_rows(raw, jnp.max), axis=0, keepdims=True)
            expo = jnp.exp2((raw - row_max) * BASE2)
            row_sum = jnp.sum(fold_rows(expo, jnp.sum), axis=0, keepdims=True)
            out_t = dot(
                jnp.concatenate([value_t[pair, block] for block in picked], axis=1),
                expo.astype(jnp.bfloat16),
            )
            turned[pair, index - begin] = out_t / row_sum
            stats[pair, block_rows(index, 8), :] = jnp.broadcast_to(
                row_max * BASE2 + jnp.log2(row_sum), (8, 2 * BLK)
            )

    each_block(counts, begin, end, 2, query_block)

    @pl.loop(begin, end, unroll=4)
    def _(index):
        for pair in range(2):
            out_t = own_parts(turned[pair, index - begin])
            outs[pair][block_rows(index), :] = out_t.T.astype(jnp.bfloat16)


def backward_kernel(
    adjacency, counts, packed, grad, attn_out, stats, *refs, blocks, begin, end
):
    query, key, value = (packed.at[:, pl.ds(PAIR * part, PAIR)] for part in range(3))
    carried, rest = refs[: 3 if begin else 0], refs[3 if begin else 0 :]
    outs, (key_t, key_sum, value_sum, queries_t, grads_t, row_dot, turned) = rest[:-7], rest[-7:]
    query_g = outs[0]

    @pl.loop(0, blocks, unroll=4)
    def _(index):
        key_t[index] = key[block_rows(index), :].T
        if begin:
            key_sum[block_rows(index), :] = carried[1][block_rows(index), :]
            value_sum[block_rows(index), :] = carried[2][block_rows(index), :]
        else:
            key_sum[block_rows(index), :] = jnp.zeros((BLK, PAIR), jnp.float32)
            value_sum[block_rows(index), :] = jnp.zeros((BLK, PAIR), jnp.float32)

    @pl.loop(begin, end, unroll=(end - begin) % 4 == 0 and 4 or end - begin)
    def _(index):
        grad_rows = grad[block_rows(index), :]
        queries_t[index - begin] = by_head_t(query[block_rows(index), :])
        grads_t[index - begin] = by_head_t(grad_rows)
        products = (
            grad_rows.astype(jnp.float32) * attn_out[block_rows(index), :].astype(jnp.float32)
        ).T
        row_dot[block_rows(index - begin, 8), :] = jnp.broadcast_to(
            jnp.concatenate(
                [
                    jnp.sum(products[:HD], axis=0, keepdims=True),
                    jnp.sum(products[HD:], axis=0, keepdims=True),
                ],
                axis=1,
            ),
            (8, 2 * BLK),
        )

    def query_block(index, slots):
        picked = [adjacency[index, slot] for slot in range(slots)]
        places = [block_rows(block) for block in picked]
        queries, grads = by_head(query[block_rows(index), :]), by_head(grad[block_rows(index), :])
        stat = stats[0, pl.ds(pl.multiple_of(index * 8, 8), 1), :]
        prob = jnp.exp2(stack(key, places, queries_t[index - begin]) * BASE2 - stat)
        change = stack(value, places, grads_t[index - begin])
        change = change - row_dot[pl.ds(pl.multiple_of((index - begin) * 8, 8), 1), :]
        term = (prob * change).astype(jnp.bfloat16)
        key_terms = dot(term, queries)
        value_terms = dot(prob.astype(jnp.bfloat16), grads)
        for number, at in enumerate(places):
            key_sum[at, :] += key_terms[BLK * number : BLK * (number + 1)]
            value_sum[at, :] += value_terms[BLK * number : BLK * (number + 1)]
        turned[index - begin] = dot(jnp.concatenate([key_t[block] for block in picked], axis=1), term)

    each_block(counts, begin, end, 1, query_block)

    @pl.loop(begin, end, unroll=(end - begin) % 4 == 0 and 4 or end - begin)
    def _(index):
        query_g[block_rows(index), :PAIR] = (
            own_parts(turned[index - begin]).T * SCALE
        ).astype(jnp.bfloat16)

    if end < blocks:
        outs[1][...], outs[2][...] = key_sum[...], value_sum[...]
    else:
        if begin:
            query_g[: BLK * begin, :PAIR] = carried[0][: BLK * begin, :]
        query_g[:, PAIR : 2 * PAIR] = (key_sum[...] * SCALE).astype(jnp.bfloat16)
        query_g[:, 2 * PAIR :] = value_sum[...].astype(jnp.bfloat16)


VMEM = pl.BlockSpec(memory_space=pltpu.VMEM)
SMEM = pl.BlockSpec(memory_space=pltpu.SMEM)
SMALL = pltpu.CompilerParams(vmem_limit_bytes=16 * 2**20)
PARAMS = pltpu.CompilerParams(vmem_limit_bytes=32 * 2**20)
WIDE = pltpu.CompilerParams(vmem_limit_bytes=60 * 2**20)
BACKWARD = pltpu.CompilerParams(vmem_limit_bytes=60716 * 2**10)


def cost(tokens, products):
    tiles = tokens // BLK * MAXK * 2
    return pl.CostEstimate(
        flops=tiles * products * 2 * BLK * BLK * HD * 4,
        bytes_accessed=12 * tokens * PAIR,
        transcendentals=tiles * BLK * BLK,
    )


def forward(packed, adjacency, counts, begin, end, carried=()):
    tokens = packed.shape[0]
    blocks = tokens // BLK
    return pl.pallas_call(
        functools.partial(forward_kernel, begin=begin, end=end),
        in_specs=[SMEM, SMEM, VMEM] + [VMEM] * len(carried),
        out_specs=[VMEM] * 3,
        out_shape=[
            jax.ShapeDtypeStruct((tokens, PAIR), jnp.bfloat16),
            jax.ShapeDtypeStruct((tokens, PAIR), jnp.bfloat16),
            jax.ShapeDtypeStruct((2, blocks * 8, 2 * BLK), jnp.float32),
        ],
        scratch_shapes=[
            pltpu.VMEM((2, blocks, PAIR, BLK), jnp.bfloat16),
            pltpu.VMEM((2, end - begin, PAIR, 2 * BLK), jnp.bfloat16),
            pltpu.VMEM((2, end - begin, PAIR, 2 * BLK), jnp.float32),
        ],
        compiler_params=PARAMS,
        cost_estimate=cost(tokens * (end - begin) // blocks, 4),
        name="attend_forward",
    )(adjacency, counts, packed, *carried)


def backward(packed, grad, pair, attn_out, stats, adjacency, counts, begin=0, end=None, carried=()):
    tokens = packed.shape[0]
    blocks = tokens // BLK
    end = end or blocks
    one = pl.BlockSpec((tokens, PAIR), lambda step: (0, 0))
    three = pl.BlockSpec((tokens, 3 * PAIR), lambda step: (0, pair))
    whole = pl.BlockSpec((tokens, 3 * PAIR), lambda step: (0, 0))
    if end < blocks:
        out_specs = [one] * 3
        out_shape = [jax.ShapeDtypeStruct((tokens, PAIR), jnp.bfloat16)]
        out_shape += [jax.ShapeDtypeStruct((tokens, PAIR), jnp.float32)] * 2
    else:
        out_specs = whole
        out_shape = jax.ShapeDtypeStruct((tokens, 3 * PAIR), jnp.bfloat16)
    return pl.pallas_call(
        functools.partial(backward_kernel, blocks=blocks, begin=begin, end=end),
        grid=(1,),
        in_specs=[
            SMEM, SMEM, three, pl.BlockSpec((tokens, PAIR), lambda step: (0, pair)), one,
            pl.BlockSpec((1, blocks * 8, 2 * BLK), lambda step: (pair, 0, 0)),
        ] + [one] * len(carried),
        out_specs=out_specs,
        out_shape=out_shape,
        scratch_shapes=[
            pltpu.VMEM((blocks, PAIR, BLK), jnp.bfloat16),
            pltpu.VMEM((tokens, PAIR), jnp.float32),
            pltpu.VMEM((tokens, PAIR), jnp.float32),
            pltpu.VMEM((end - begin, PAIR, 2 * BLK), jnp.bfloat16),
            pltpu.VMEM((end - begin, PAIR, 2 * BLK), jnp.bfloat16),
            pltpu.VMEM(((end - begin) * 8, 2 * BLK), jnp.float32),
            pltpu.VMEM((end - begin, PAIR, 2 * BLK), jnp.float32),
        ],
        compiler_params=BACKWARD,
        cost_estimate=cost(tokens * (end - begin) // blocks, 5),
        name="attend_backward",
    )(adjacency, counts, packed, grad, attn_out, stats, *carried)


STEPS = 2


def pack_kernel(queries, keys, values, out_grad, weight, packed, top, bottom, own):
    step = pl.program_id(0)
    for group in range(packed.shape[0]):
        for pair in range(2):
            start = PAIR * (2 * group + pair)
            for part, source in enumerate((queries, keys, values)):
                packed[group, :, columns(pair, part)] = source[:, start : start + PAIR]
    own[...] = weight[...]

    @pl.when(step < STEPS // 2)
    def _():
        top[...] = out_grad[...]

    @pl.when(step >= STEPS // 2)
    def _():
        bottom[...] = out_grad[...]


def pack(queries, keys, values, out_grad, out_weight, groups):
    tokens, width = queries.shape
    height, middle = tokens // STEPS, STEPS // 2
    share = width // groups // STEPS

    def weight_place(step):
        skipped = lax.axis_index("seq") * (width // groups) % out_weight.shape[0]
        return (skipped // share + step, 0)

    taken = pl.BlockSpec((height, width), lambda step: (step, 0))
    return pl.pallas_call(
        pack_kernel,
        grid=(STEPS,),
        in_specs=[taken] * 4 + [pl.BlockSpec((share, width), weight_place)],
        out_specs=[
            pl.BlockSpec((groups, height, 6 * PAIR), lambda step: (0, step, 0)),
            pl.BlockSpec((height, width), lambda step: (jnp.minimum(step, middle - 1), 0)),
            pl.BlockSpec((height, width), lambda step: (jnp.maximum(step - middle, 0), 0)),
            pl.BlockSpec((share, width), lambda step: (step, 0)),
        ],
        out_shape=[
            jax.ShapeDtypeStruct((groups, tokens, 6 * PAIR), queries.dtype),
            jax.ShapeDtypeStruct((tokens // 2, width), queries.dtype),
            jax.ShapeDtypeStruct((tokens // 2, width), queries.dtype),
            jax.ShapeDtypeStruct((width // groups, width), queries.dtype),
        ],
        compiler_params=WIDE,
        name="pack",
    )(queries, keys, values, out_grad, out_weight)


def unpack_kernel(first, second, query_g, key_g, value_g):
    for group in range(first.shape[0]):
        for pair, source in enumerate((first, second)):
            start = PAIR * (2 * group + pair)
            for part, out in enumerate((query_g, key_g, value_g)):
                out[:, start : start + PAIR] = source[group, :, PAIR * part : PAIR * (part + 1)]


def unpack(first, second):
    groups, tokens, _ = first.shape
    height = tokens // STEPS
    taken = pl.BlockSpec((groups, height, 3 * PAIR), lambda step: (0, step, 0))
    given = pl.BlockSpec((height, groups * 2 * PAIR), lambda step: (step, 0))
    return pl.pallas_call(
        unpack_kernel,
        grid=(STEPS,),
        in_specs=[taken] * 2,
        out_specs=[given] * 3,
        out_shape=[jax.ShapeDtypeStruct((tokens, groups * 2 * PAIR), first.dtype)] * 3,
        compiler_params=SMALL,
        name="unpack",
    )(first, second)


def spread_kernel(*refs):
    pieces, out = refs[:-1], refs[-1]
    member = lax.axis_index("seq")
    for mask, piece in enumerate(pieces):
        width = piece.shape[1]
        start = pl.multiple_of((member ^ mask) * width, width)
        out[:, pl.ds(start, width)] = piece[...].astype(out.dtype)


def spread(pieces):
    rows, width = pieces[0].shape
    height = rows // STEPS
    return pl.pallas_call(
        spread_kernel,
        grid=(STEPS,),
        in_specs=[pl.BlockSpec((height, width), lambda step: (step, 0))] * len(pieces),
        out_specs=pl.BlockSpec((height, len(pieces) * width), lambda step: (step, 0)),
        out_shape=jax.ShapeDtypeStruct((rows, len(pieces) * width), jnp.float32),
        compiler_params=WIDE,
        name="spread",
    )(*pieces)


def exchange(chunks):
    return lax.all_to_all(chunks, "seq", split_axis=0, concat_axis=0, tiled=True)


WEIGHT_ROUTES = (
    ((0, 1), (1, 2), (2, 1), (3, 2)),
    ((0, 2), (1, 3), (2, 0), (3, 1)),
    ((2, 3), (1, 0), (2, 3), (1, 0)),
)


def send_weight(rows, step):
    planes, members = lax.axis_size("fsdp"), lax.axis_size("seq")
    routes = []
    for member in range(members):
        source, target = WEIGHT_ROUTES[step][member * planes // members]
        routes.append((source * members + member, target * members + member))
    return lax.ppermute(rows, ("fsdp", "seq"), routes)


def swap(array, mask):
    routes = [(s, s ^ mask) for s in range(lax.axis_size("seq"))]
    return lax.ppermute(array, "seq", routes)


def project_kernel(places, *refs):
    pieces, rest = refs[: len(places)], refs[len(places) :]
    weights, (first, second, given, sent) = rest[:4], rest[4:8]
    whole, weight, weight_t, attn_grad, terms, landed, fetched, left, gone = rest[8:]
    plane, member = lax.axis_index("fsdp"), lax.axis_index("seq")
    local = whole.shape[0] // terms.shape[0]
    copies = []
    for number, (mask, row) in enumerate(places):
        start = pl.multiple_of((member ^ mask) * local + row, BLK)
        target = whole.at[pl.ds(start, pieces[number].shape[0]), :]
        copies.append(pltpu.make_async_copy(pieces[number], target, landed.at[number]))
    for source, rows in enumerate(weights):
        held = (plane == member // 2) if source == 0 else False
        for home, (_, target) in enumerate(WEIGHT_ROUTES[source - 1] if source else ()):
            held = held | ((member // 2 == home) & (plane == target))

        @pl.when(held)
        def _():
            pltpu.make_async_copy(rows, weight, fetched).start()
    for copy in copies:
        copy.start()
    pltpu.make_async_copy(weights[0], weight, fetched).wait()
    weight_t[...] = weight[...].T
    attn_t = jnp.concatenate([first[...].T, second[...].T], axis=0)
    for copy in copies:
        copy.wait()
    groups, _, width = terms.shape
    for group in range(0, groups, 2):
        wide = dot(attn_t, whole[:, width * group : width * (group + 2)]).astype(terms.dtype)
        terms[group], terms[group + 1] = wide[:, :width], wide[:, width:]

    leaving = pltpu.make_async_copy(terms, sent, left)
    leaving.start()

    @pl.loop(0, 4)
    def _(part):
        rows = block_rows(part, whole.shape[0] // 4)
        attn_grad[rows, :] = dot(whole[rows, :], weight_t[...]).astype(attn_grad.dtype)
        pltpu.make_async_copy(attn_grad.at[rows, :], given.at[rows, :], gone.at[part]).start()

    leaving.wait()
    for part in range(4):
        rows = block_rows(part, whole.shape[0] // 4)
        pltpu.make_async_copy(attn_grad.at[rows, :], given.at[rows, :], gone.at[part]).wait()


def project(pieces, weights, first, second, groups):
    places = [(mask, row) for mask, row, _ in pieces]
    arrays = [piece for _, _, piece in pieces]
    height, width = weights[0].shape
    tokens = first.shape[0]
    far = pl.BlockSpec(memory_space=pl.ANY)
    return pl.pallas_call(
        functools.partial(project_kernel, places),
        in_specs=[far] * (len(arrays) + len(weights)) + [VMEM] * 2,
        out_specs=[pl.BlockSpec(memory_space=pltpu.HBM)] * 2,
        out_shape=[
            jax.ShapeDtypeStruct((tokens, height), jnp.bfloat16),
            jax.ShapeDtypeStruct((groups, height, width // groups), jnp.bfloat16),
        ],
        scratch_shapes=[
            pltpu.VMEM((tokens, width), jnp.bfloat16),
            pltpu.VMEM((height, width), jnp.bfloat16),
            pltpu.VMEM((width, height), jnp.bfloat16),
            pltpu.VMEM((tokens, height), jnp.bfloat16),
            pltpu.VMEM((groups, height, width // groups), jnp.bfloat16),
            pltpu.SemaphoreType.DMA((len(arrays),)),
            pltpu.SemaphoreType.DMA,
            pltpu.SemaphoreType.DMA,
            pltpu.SemaphoreType.DMA((4,)),
        ],
        compiler_params=PARAMS,
        cost_estimate=pl.CostEstimate(
            flops=4 * tokens * width * height,
            bytes_accessed=2 * tokens * width + 8 * height * width,
            transcendentals=0,
        ),
        name="project",
    )(*arrays, *weights, first, second)


def split_kernel(whole, *parts):
    height = parts[0].shape[0]
    for offset, part in enumerate(parts):
        start = pl.multiple_of((lax.axis_index("fsdp") ^ offset) * height, height)
        part[...] = whole[pl.ds(start, height), :]


def split(whole, planes):
    rows, width = whole.shape
    return pl.pallas_call(
        split_kernel,
        in_specs=[VMEM],
        out_specs=[VMEM] * planes,
        out_shape=[jax.ShapeDtypeStruct((rows // planes, width), whole.dtype)] * planes,
        compiler_params=PARAMS,
        name="split",
    )(whole)


def fits_pairs(sizes):
    planes, members = sizes["fsdp"], sizes["seq"]
    return members == 8 and planes == 4 and members * 2 * PAIR == HEADS * HD


def pair_device(queries, keys, values, out_grad, out_weight, key_blocks, block_counts):
    planes, members = lax.axis_size("fsdp"), lax.axis_size("seq")
    home = lax.axis_index("seq") // 2
    local_tokens, model_width = queries.shape[1:]
    tokens = local_tokens * members
    adjacency, counts = key_blocks[0], block_counts[0]
    shard = out_grad[0]

    chunks, top, bottom, own = pack(queries[0], keys[0], values[0], shard, out_weight, members)
    packed = exchange(chunks).reshape(tokens, 6 * PAIR)
    near, far = send_weight(own, 0), send_weight(own, 1)
    beside = swap(shard, 1)
    packed, shard, top, bottom, near, beside = lax.optimization_barrier(
        (packed, shard, top, bottom, near, beside)
    )

    along = swap(top, 2), swap(bottom, 2)
    across = swap(top, 4), swap(bottom, 4)
    blocks = tokens // BLK
    done = forward(packed, adjacency, counts, 0, blocks // 2)
    done, far = lax.optimization_barrier((done, far))
    last = send_weight(jnp.where((home == 1) | (home == 2), own, far), 2)
    done = forward(packed, adjacency, counts, blocks // 2, blocks, done)
    (first, second, stats), along, across = lax.optimization_barrier((done, along, across))

    halves = list(zip((2, 2, 4, 4, 6, 6), (0, 1) * 3, (*along, *across, swap(along[0], 4), swap(across[1], 2))))
    pieces = [(0, 0, shard), (1, 0, beside)]
    for mask, half, piece in halves:
        row = half * local_tokens // 2
        pieces += [(mask, row, piece), (mask ^ 1, row, swap(piece, 1))]
    attn_grad, by_columns = project(pieces, (own, near, far, last), first, second, members)

    terms = exchange(by_columns).reshape(model_width, -1)
    first_g = backward(packed, attn_grad, 0, first, stats, adjacency, counts)
    first_g, terms = lax.optimization_barrier((first_g, terms))
    parts = split(terms, planes)
    received = [
        lax.ppermute(parts[offset], "fsdp", [(z, z ^ offset) for z in range(planes)])
        for offset in range(1, planes)
    ]
    first_r = exchange(first_g.reshape(members, local_tokens, 3 * PAIR))
    split_at = tokens // BLK * 12 // 16
    started = backward(
        packed, attn_grad, 1, second, stats, adjacency, counts, end=split_at
    )
    *started, received = lax.optimization_barrier((*started, received))
    summed = sum(part.astype(jnp.float32) for part in [parts[0], *received]).astype(terms.dtype)
    sides = [summed, swap(summed, 2), swap(summed, 4), swap(summed, 6)]
    second_g = backward(
        packed, attn_grad, 1, second, stats, adjacency, counts, begin=split_at, carried=started
    )
    second_g, *sides = lax.optimization_barrier((second_g, *sides))
    wo_grad = spread([part for one in sides for part in (one, swap(one, 1))])
    second_r = exchange(second_g.reshape(members, local_tokens, 3 * PAIR))
    query_g, key_g, value_g = unpack(first_r, second_r)
    return (query_g[None], key_g[None], value_g[None], wo_grad)


def general_device(queries, keys, values, out_grad, out_weight, key_blocks, block_counts):
    local_tokens = queries.shape[1]
    model_width = queries.shape[2]
    seq_devices = lax.axis_size("seq")
    loss_grad = out_grad[0]
    adjacency = key_blocks[0]
    slot_live = jnp.arange(MAXK)[None, :] < block_counts[0][:, None]

    def head_groups(array):
        return array[0].reshape(local_tokens, seq_devices, HEADS // seq_devices, HD)

    attn_grad = lax.dot_general(
        loss_grad,
        lax.all_gather(out_weight, "fsdp", axis=0, tiled=True),
        (((1,), (1,)), ((), ())),
        preferred_element_type=jnp.float32,
    ).astype(jnp.bfloat16)

    def attend(heads_in):
        query_h, key_h, value_h, grad_h = (member[:, 0] for member in heads_in)
        row_max, row_sum, attn_blocks = head_forward(query_h, key_h, value_h, adjacency, slot_live)
        query_g, key_g, value_g = head_backward(
            query_h, key_h, value_h, grad_h, row_max, row_sum, attn_blocks, adjacency, slot_live
        )
        return (query_g, key_g, value_g, attn_blocks.reshape(-1, query_h.shape[1], HD))

    query_g, key_g, value_g, attn_heads = attend(
        (
            lax.all_to_all(head_groups(queries), "seq", split_axis=1, concat_axis=0, tiled=True),
            lax.all_to_all(head_groups(keys), "seq", split_axis=1, concat_axis=0, tiled=True),
            lax.all_to_all(head_groups(values), "seq", split_axis=1, concat_axis=0, tiled=True),
            lax.all_to_all(
                head_groups(attn_grad[None]), "seq", split_axis=1, concat_axis=0, tiled=True
            ),
        )
    )
    query_t, key_t, value_t, attn_t = (
        lax.all_to_all(query_g, "seq", split_axis=0, concat_axis=1, tiled=True),
        lax.all_to_all(key_g, "seq", split_axis=0, concat_axis=1, tiled=True),
        lax.all_to_all(value_g, "seq", split_axis=0, concat_axis=1, tiled=True),
        lax.all_to_all(attn_heads, "seq", split_axis=0, concat_axis=1, tiled=True),
    )
    attn_out = attn_t.reshape(local_tokens, model_width)
    share = lax.psum_scatter(
        lax.dot_general(
            attn_out, loss_grad, (((0,), (0,)), ((), ())), preferred_element_type=jnp.float32
        ),
        ("fsdp", "seq"),
        scatter_dimension=0,
        tiled=True,
    )
    wo_grad = lax.all_gather(share.astype(jnp.bfloat16), "seq", axis=0, tiled=True).astype(
        share.dtype
    )

    def to_tokens(array):
        return array.reshape(1, local_tokens, model_width)

    return (to_tokens(query_t), to_tokens(key_t), to_tokens(value_t), wo_grad)


def on_device(mesh):
    return pair_device if fits_pairs(mesh.shape) else general_device


def solution(mesh):
    return jax.shard_map(
        on_device(mesh),
        mesh=mesh,
        in_specs=(
            P("fsdp", "seq", None),
            P("fsdp", "seq", None),
            P("fsdp", "seq", None),
            P("fsdp", "seq", None),
            P("fsdp", None),
            P("fsdp", None, None),
            P("fsdp", None),
        ),
        out_specs=(
            P("fsdp", "seq", None),
            P("fsdp", "seq", None),
            P("fsdp", "seq", None),
            P("fsdp", None),
        ),
        check_vma=False,
    )
```
